32 devices in a mesh: seq: 4 (over x, core), branch: 2 (over y), tensor: 4 (over z).
Axes of the slice: x: 2, y: 2, z: 4, core: 2. Of those that a mesh axis runs over, the one named last changes fastest.
Arguments:
- tokens: bfloat16 [1024, 2048], P('seq', ('branch', 'tensor')), may hold values from -6 to 6
- cotangent: bfloat16 [1024, 2048], P('seq', ('branch', 'tensor')), may hold values from -6 to 6
- documents: int32 [1024], P('seq'), may hold values from 0 to 2, as said below
- positions: int32 [1024], P('seq'), may hold values from 0 to 1023, as said below
- project_weight: bfloat16 [2048, 6144], P(None, 'tensor'), may hold values from -0.125 to 0.125
- offsets: float32 [6144], P('tensor'), may hold values from -0.75 to 0.75
- output_weight: bfloat16 [2048, 2048], P(None, 'tensor'), may hold values from -0.75 to 0.75
- up_weight: bfloat16 [2048, 8192], P(None, 'tensor'), may hold values from -0.125 to 0.125
- hidden_bias: float32 [8192], P('tensor'), may hold values from -6 to 6
- down_weight: bfloat16 [2048, 8192], P(None, 'tensor'), may hold values from -0.0625 to 0.0625
- norm_gain: float32 [2, 2048], P('branch'), may hold values from 0.1 to 1.9
- norm_bias: float32 [2, 2048], P('branch'), may hold values from -4 to 4
- residual_bias: float32 [2, 2048], P('branch'), may hold values from -4 to 4
Outputs:
- layer_out: bfloat16 [1024, 2048], P('seq', ('branch', 'tensor'))
- input_grad: float32 [1024, 2048], P('seq', ('branch', 'tensor'))
- project_grad: float32 [2048, 6144], P(('seq', 'branch'), 'tensor')
- output_grad: float32 [2048, 2048], P(('seq', 'branch'), 'tensor')
- up_grad: float32 [2048, 8192], P(('seq', 'branch'), 'tensor')
- down_grad: float32 [2048, 8192], P(('seq', 'branch'), 'tensor')
- offsets_grad: float32 [6144], replicated
- hidden_grad: float32 [8192], replicated
- gain_grad: float32 [2, 2048], replicated
- center_grad: float32 [2, 2048], replicated
- residual_grad: float32 [2, 2048], replicated
The draws below stay inside these ranges and needn't reach their ends.
Inputs may be any that keep to these rules, and one draw needn't show every extreme that they name: `documents`: document numbers never fall along the tokens; each document is one contiguous run of tokens and none is empty; document 1 begins within the first 256 tokens and ends within the last 256. Within a document positions start at 0 and rise by 1 from each token to the next.
All inputs are finite; a program needn't handle non-finite values.
Results may differ from the reference program's by a relative error of at most 0.015.
Values may be sent and summed in bfloat16 or wider, within the bound.
A program may use at most 192 MiB of HBM per device.

```python
import jax
import jax.numpy as jnp
from jax import lax

D = 2048
HEADS = 16
HEAD_DIM = 128
ROT = 32
FF = 8192
TOK_DEV = 256
TOKENS = 1024


def document_cuts(key):
    head_key, tail_key = jax.random.split(key)
    head_length = jax.random.randint(head_key, (), 1, TOK_DEV)
    tail_length = jax.random.randint(tail_key, (), 1, TOK_DEV)
    token_index = jnp.arange(TOKENS, dtype=jnp.int32)
    labels = (token_index >= head_length).astype(jnp.int32) + (token_index >= TOKENS - tail_length).astype(jnp.int32)
    starts = jnp.where(labels == 0, 0, jnp.where(labels == 1, head_length, TOKENS - tail_length)).astype(jnp.int32)
    return (labels, starts)


def draw_documents(key, part):
    labels, starts = document_cuts(key)
    return labels


def draw_positions(key, part):
    labels, starts = document_cuts(key)
    token_index = jnp.arange(TOKENS, dtype=jnp.int32)
    return (token_index - starts).astype(jnp.int32)


def block_scale(stream_key, dims, cuts, low, top_value):
    factor_of, own = 1.0, jax.random.fold_in(stream_key, 6)
    for dim, parts in cuts:
        heights = jnp.exp(jax.random.uniform(jax.random.fold_in(own, dim), (parts,), jnp.float32, low / len(cuts), top_value / len(cuts)))
        factor_of = factor_of * jnp.repeat(heights, dims[dim] // parts).reshape([-1 if axis == dim else 1 for axis in range(len(dims))])
    return factor_of


def normal_values(stream_key, extent, scale, bound, cuts=(), kind=jnp.bfloat16):
    drawn = jax.random.normal(stream_key, extent, jnp.float32) * scale
    if len(cuts) > 0:
        drawn = block_scale(stream_key, extent, cuts, -0.22, 0.18) * drawn
    return jnp.clip(drawn, min=-bound, max=bound).astype(kind)


def setup_inputs(seed: int = 0) -> dict:
    splits = jax.random.split(jax.random.key(seed), 14)
    tokens = normal_values(splits[0], (TOKENS, D), 1.0, 6.0, ((0, 4), (1, 8)))
    cotangent = normal_values(splits[1], (TOKENS, D), 1.0, 6.0, ((0, 4), (1, 8)))
    documents = draw_documents(jax.random.fold_in(splits[13], 71), 0)
    positions = draw_positions(jax.random.fold_in(splits[13], 71), 0)
    project_weight = normal_values(splits[4], (D, 3 * D), D ** -0.5, 0.125, ((1, 4),))
    offsets = normal_values(splits[5], (3 * D,), 0.05, 0.75, ((0, 4),), jnp.float32)
    output_weight = normal_values(splits[6], (D, D), (D // 32) ** -0.5, 0.75, ((1, 4),))
    up_weight = normal_values(splits[7], (D, FF), D ** -0.5, 0.125, ((1, 4),))
    hidden_bias = normal_values(splits[8], (FF,), 0.5, 6.0, ((0, 4),), jnp.float32)
    down_weight = normal_values(splits[9], (D, FF), FF ** -0.5, 0.0625, ((1, 4),))
    norm_gain = jnp.clip(1.0 + 0.18 * jax.random.normal(splits[10], (2, D), jnp.float32), 0.1, 1.9)
    norm_bias = normal_values(splits[11], (2, D), 0.3, 4.0, ((0, 2),), jnp.float32)
    residual_bias = normal_values(splits[12], (2, D), 0.3, 4.0, ((0, 2),), jnp.float32)
    return dict(tokens=tokens, cotangent=cotangent, documents=documents, positions=positions, project_weight=project_weight, offsets=offsets, output_weight=output_weight, up_weight=up_weight, hidden_bias=hidden_bias, down_weight=down_weight, norm_gain=norm_gain, norm_bias=norm_bias, residual_bias=residual_bias)


norm_eps = 1e-05
rope_base = 10000.0
masked_score = -1e+30

@jax.custom_vjp
def low(v):
    return lax.optimization_barrier(v.astype(jnp.bfloat16)).astype(jnp.float32)

@jax.custom_vjp
def low_back(v):
    return v

def low_keep(v):
    return (low(v), None)

def low_pass(kept, grad):
    return (grad,)

def back_keep(v):
    return (v, None)

def back_low(kept, grad):
    return (low(grad),)
low.defvjp(low_keep, low_pass)
low_back.defvjp(back_keep, back_low)

def layer_norm(values, gain_row, shift_row):
    average = lax.optimization_barrier(jnp.mean(values, axis=-1, keepdims=True))
    centered = values - average
    variance = lax.optimization_barrier(jnp.mean(centered * centered, axis=-1, keepdims=True))
    return centered * lax.rsqrt(variance + norm_eps) * gain_row + shift_row

def rope_tables(places):
    half_rot = ROT // 2
    frequency = rope_base ** (-(2.0 * jnp.arange(half_rot, dtype=jnp.float32)) / ROT)
    angles = places.astype(jnp.float32)[:, None] * frequency[None, :]
    return (jnp.cos(angles), jnp.sin(angles))

def rotate(values, cosine, sine_rows, direction):
    half_rot = ROT // 2
    first_half = values[..., :half_rot]
    second_half = values[..., half_rot:ROT]
    cos_table = cosine[:, None, :]
    sin_table = direction * sine_rows[:, None, :]
    return jnp.concatenate([first_half * cos_table - second_half * sin_table, second_half * cos_table + first_half * sin_table, values[..., ROT:]], axis=-1)

def attend_block(keys, values, documents, query_part, part_ids, part_index):
    highest = lax.Precision.HIGHEST
    scores = low_back(jnp.einsum('qhd,khd->hqk', query_part, keys, precision=highest) * HEAD_DIM ** (-0.5))
    token_index = jnp.arange(TOKENS, dtype=jnp.int32)
    visible = (part_ids[:, None] == documents[None, :]) & (token_index[None, :] <= part_index[:, None])
    masked = jnp.where(visible[None], scores, masked_score)
    top_score = lax.optimization_barrier(jnp.max(masked, axis=-1, keepdims=True))
    weights = jnp.where(visible[None], jnp.exp(masked - top_score), 0.0)
    totals = lax.optimization_barrier(jnp.sum(weights, axis=-1))
    blended = jnp.einsum('hqk,khd->qhd', low(weights), values, precision=highest)
    return blended / totals.T[:, :, None]

def attention(queries, keys, values, documents):
    block_rows = 512 if TOKENS % 512 == 0 else TOKENS
    groups = TOKENS // block_rows
    token_index = jnp.arange(TOKENS, dtype=jnp.int32)

    def block_step(sliced):
        return attend_block(keys, values, documents, sliced[0], sliced[1], sliced[2])
    blocks = (queries.reshape(groups, block_rows, HEADS, HEAD_DIM), documents.reshape(groups, block_rows), token_index.reshape(groups, block_rows))
    return lax.map(jax.checkpoint(block_step), blocks).reshape(TOKENS, HEADS, HEAD_DIM)

def forward(tokens, project_weight, offsets, output_weight, up_weight, hidden_bias, down_weight, norm_gain, norm_bias, residual_bias, documents, positions):
    highest = lax.Precision.HIGHEST
    first_norm = low(layer_norm(tokens, norm_gain[0], norm_bias[0]))
    second_norm = low(layer_norm(tokens, norm_gain[1], norm_bias[1]))
    packed = low_back(jnp.dot(first_norm, project_weight, precision=highest) + offsets).reshape(TOKENS, HEADS, 3, HEAD_DIM)
    cosine, sine_rows = rope_tables(positions)
    queries = low(rotate(packed[:, :, 0], cosine, sine_rows, 1.0))
    keys = low(rotate(packed[:, :, 1], cosine, sine_rows, 1.0))
    values = low(packed[:, :, 2])
    attended = low(low_back(attention(queries, keys, values, documents))).reshape(TOKENS, D)
    attn_out = jnp.dot(attended, output_weight.T, precision=highest)
    up_rows = low_back(jnp.dot(second_norm, up_weight, precision=highest) + hidden_bias)
    active = low(jax.nn.gelu(up_rows, approximate=False))
    feed_out = jnp.dot(active, down_weight.T, precision=highest)
    return tokens + attn_out + feed_out + residual_bias[0] + residual_bias[1]

def reference(tokens, cotangent, documents, positions, project_weight, offsets, output_weight, up_weight, hidden_bias, down_weight, norm_gain, norm_bias, residual_bias):

    def wrapped(tokens_in, project_in, offsets_in, output_in, up_in, hidden_in, down_in, gain_in, shift_in, residual_in):
        return forward(tokens_in, project_in, offsets_in, output_in, up_in, hidden_in, down_in, gain_in, shift_in, residual_in, documents, positions)
    result, pullback = jax.vjp(wrapped, tokens.astype(jnp.float32), project_weight.astype(jnp.float32), offsets, output_weight.astype(jnp.float32), up_weight.astype(jnp.float32), hidden_bias, down_weight.astype(jnp.float32), norm_gain, norm_bias, residual_bias)
    gradients = pullback(cotangent.astype(jnp.float32))
    return (result.astype(jnp.bfloat16), gradients[0], gradients[1], gradients[3], gradients[4], gradients[6], gradients[2], gradients[5], gradients[7], gradients[8], gradients[9])
```

```python
from functools import partial

import jax
import jax.numpy as jnp
from jax import lax
from jax.experimental import pallas as pl
from jax.experimental.pallas import tpu as pltpu
from jax.sharding import PartitionSpec as P

HEAD_DIM = 128
ROT = 32


norm_eps = 1e-05
rope_base = 10000.0
masked_score = -1e30


def passed_along(value, axis, steps):
    count = lax.axis_size(axis)
    pairs = [(source, (source + steps) % count) for source in range(count)]
    return lax.ppermute(value, axis, pairs)


def shifted(array, axis, by):
    count = lax.axis_size(axis)
    pairs = [(i, i + by) for i in range(count) if 0 <= i + by < count]
    return lax.ppermute(array, axis, pairs)


def layer_norm(values, gain_row, shift_row):
    average = jnp.mean(values, axis=-1, keepdims=True)
    centered = values - average
    variance = jnp.mean(centered * centered, axis=-1, keepdims=True)
    return centered * lax.rsqrt(variance + norm_eps) * gain_row + shift_row


def rope_tables(places):
    half_rot = ROT // 2
    frequency = rope_base ** (-(2.0 * jnp.arange(half_rot, dtype=jnp.float32)) / ROT)
    angles = places.astype(jnp.float32)[:, None] * frequency[None, :]
    return (jnp.cos(angles), jnp.sin(angles))


def rotate(values, cosine, sine_rows, direction):
    half_rot = ROT // 2
    first_half = values[..., :half_rot]
    second_half = values[..., half_rot:ROT]
    cos_table = cosine[:, None, :]
    sin_table = direction * sine_rows[:, None, :]
    return jnp.concatenate(
        [
            first_half * cos_table - second_half * sin_table,
            second_half * cos_table + first_half * sin_table,
            values[..., ROT:],
        ],
        axis=-1,
    )


def contract_rows(first_side, second_side):
    return lax.dot_general(
        first_side, second_side, (((0,), (0,)), ((), ())), preferred_element_type=jnp.float32
    )


def contract_cols(first_side, second_side):
    return lax.dot_general(
        first_side, second_side, (((1,), (1,)), ((), ())), preferred_element_type=jnp.float32
    )


def on_device(
    tokens,
    cotangent,
    documents,
    positions,
    project_weight,
    offsets,
    output_weight,
    up_weight,
    hidden_bias,
    down_weight,
    norm_gain,
    norm_bias,
    residual_bias,
):
    tok_rows = tokens.shape[0]
    model_width = up_weight.shape[0]
    attn_width = output_weight.shape[1]
    local_heads = attn_width // HEAD_DIM
    hidden_local = up_weight.shape[1]
    seq_count = lax.axis_size("seq")
    seq_index = lax.axis_index("seq")
    branch_index = lax.axis_index("branch")
    tensor_index = lax.axis_index("tensor")
    is_attention = branch_index == 0
    lead_tensor = tensor_index == 0
    score_scale = HEAD_DIM ** (-0.5)
    local_index = jnp.arange(tok_rows, dtype=jnp.int32)
    query_index = seq_index * tok_rows + local_index
    full_tokens, full_cotangent = (
        lax.all_gather(tokens, ("branch", "tensor"), axis=1, tiled=True),
        lax.all_gather(cotangent, ("branch", "tensor"), axis=1, tiled=True),
    )
    gain_row = norm_gain[0]
    shift_row = norm_bias[0]
    normed, norm_pullback = jax.vjp(
        layer_norm, full_tokens.astype(jnp.float32), gain_row, shift_row
    )
    normed_low = normed.astype(jnp.bfloat16)
    cosine, sine_rows = rope_tables(positions)
    zeros_heads = jnp.zeros((tok_rows, attn_width), jnp.bfloat16)
    zeros_hidden = jnp.zeros((tok_rows, hidden_local), jnp.float32)
    hidden_zero = jnp.zeros((tok_rows, hidden_local), jnp.bfloat16)
    zeros_stats = jnp.zeros((local_heads, tok_rows), jnp.float32)
    grad_zero = jnp.zeros((tok_rows, local_heads, HEAD_DIM), jnp.float32)

    def attention_front(unused):
        packed = jnp.dot(normed_low, project_weight, preferred_element_type=jnp.float32) + offsets
        packed = packed.reshape(tok_rows, local_heads, 3, HEAD_DIM)
        query_rot = rotate(packed[:, :, 0], cosine, sine_rows, 1.0).reshape(tok_rows, attn_width)
        key_rot = rotate(packed[:, :, 1], cosine, sine_rows, 1.0).reshape(tok_rows, attn_width)
        value_rows = packed[:, :, 2].reshape(tok_rows, attn_width)
        return (
            query_rot.astype(jnp.bfloat16),
            key_rot.astype(jnp.bfloat16),
            value_rows.astype(jnp.bfloat16),
            zeros_hidden,
            hidden_zero,
        )

    def feed_front(unused):
        up_rows = jnp.dot(normed_low, up_weight, preferred_element_type=jnp.float32) + hidden_bias
        active = jax.nn.gelu(up_rows, approximate=False).astype(jnp.bfloat16)
        return (zeros_heads, zeros_heads, zeros_heads, up_rows, active)

    query_low, key_low, value_low, up_rows, active = lax.cond(
        is_attention, attention_front, feed_front, 0
    )
    query_heads = query_low.reshape(tok_rows, local_heads, HEAD_DIM)

    def absorb(totals, key_rows, value_rows, key_ids, offset):
        key_count = key_rows.shape[0]
        key_index = offset + jnp.arange(key_count, dtype=jnp.int32)
        visible = (documents[:, None] == key_ids[None, :]) & (
            key_index[None, :] <= query_index[:, None]
        )

        def update(running):
            run_max, run_sum, run_acc = running
            scores = (
                jnp.einsum(
                    "qhd,khd->hqk",
                    query_heads,
                    key_rows.reshape(key_count, local_heads, HEAD_DIM),
                    preferred_element_type=jnp.float32,
                )
                * score_scale
            )
            masked = jnp.where(visible[None], scores, masked_score)
            new_max = jnp.maximum(run_max, jnp.max(masked, axis=-1))
            weights = jnp.where(visible[None], jnp.exp(masked - new_max[:, :, None]), 0.0)
            factor = jnp.exp(run_max - new_max)
            blended = jnp.einsum(
                "hqk,khd->qhd",
                weights.astype(jnp.bfloat16),
                value_rows.reshape(key_count, local_heads, HEAD_DIM),
                preferred_element_type=jnp.float32,
            )
            return (
                new_max,
                run_sum * factor + jnp.sum(weights, axis=-1),
                run_acc * factor.T[:, :, None] + blended,
            )

        def unchanged(running):
            return running

        return lax.cond(is_attention & jnp.any(visible), update, unchanged, totals)

    initial = (jnp.full((local_heads, tok_rows), masked_score, jnp.float32), zeros_stats, grad_zero)
    totals = initial
    key_rows = lax.all_gather(key_low, "seq", axis=0, tiled=True)
    value_rows = lax.all_gather(value_low, "seq", axis=0, tiled=True)
    key_ids = lax.all_gather(documents, "seq", axis=0, tiled=True)
    key_count = key_rows.shape[0]
    groups = key_count // tok_rows

    def absorb_group(running, sliced):
        return (absorb(running, sliced[0], sliced[1], sliced[2], sliced[3]), None)

    starts = tok_rows * jnp.arange(groups, dtype=jnp.int32)
    stacked = (
        key_rows.reshape(groups, tok_rows, attn_width),
        value_rows.reshape(groups, tok_rows, attn_width),
        key_ids.reshape(groups, tok_rows),
        starts,
    )
    totals, unused = lax.scan(absorb_group, totals, stacked)
    run_max, run_sum, run_acc = totals

    def attention_out(unused):
        attended = run_acc / run_sum.T[:, :, None]
        attended_low = attended.reshape(tok_rows, attn_width).astype(jnp.bfloat16)
        return (
            contract_cols(attended_low, output_weight),
            attended,
            attended_low,
            run_max + jnp.log(run_sum),
        )

    def feed_out(unused):
        return (contract_cols(active, down_weight), grad_zero, zeros_heads, zeros_stats)

    branch_out, attended, attended_low, lse_rows = lax.cond(
        is_attention, attention_out, feed_out, 0
    )
    branch_out = branch_out + jnp.where(lead_tensor, residual_bias[0], 0.0)
    summed = lax.psum_scatter(
        branch_out.astype(jnp.bfloat16), ("branch", "tensor"), scatter_dimension=1, tiled=True
    ).astype(jnp.float32)
    layer_out = (tokens.astype(jnp.float32) + summed).astype(jnp.bfloat16)

    def attention_prep(unused):
        grad_low = jnp.dot(
            full_cotangent, output_weight, preferred_element_type=jnp.float32
        ).astype(jnp.bfloat16)
        delta_rows = jnp.sum(
            grad_low.reshape(tok_rows, local_heads, HEAD_DIM).astype(jnp.float32) * attended,
            axis=-1,
        ).T
        return (grad_low, delta_rows, hidden_zero)

    def feed_prep(unused):
        active_grad = jnp.dot(full_cotangent, down_weight, preferred_element_type=jnp.float32)
        gelu_value, gelu_pullback = jax.vjp(partial(jax.nn.gelu, approximate=False), up_rows)
        return (zeros_heads, zeros_stats, gelu_pullback(active_grad)[0].astype(jnp.bfloat16))

    grad_low, delta_rows, hidden_low = lax.cond(is_attention, attention_prep, feed_prep, 0)

    def block_grads(
        query_rows,
        grad_rows,
        query_lse,
        query_delta,
        query_ids,
        query_place,
        key_rows,
        value_rows,
        key_ids,
        key_place,
    ):
        visible = (query_ids[:, None] == key_ids[None, :]) & (
            key_place[None, :] <= query_place[:, None]
        )

        def compute(unused):
            query_part_heads = query_rows.reshape(tok_rows, local_heads, HEAD_DIM)
            grad_heads = grad_rows.reshape(tok_rows, local_heads, HEAD_DIM)
            key_heads = key_rows.reshape(tok_rows, local_heads, HEAD_DIM)
            value_heads = value_rows.reshape(tok_rows, local_heads, HEAD_DIM)
            scores = (
                jnp.einsum(
                    "qhd,khd->hqk", query_part_heads, key_heads, preferred_element_type=jnp.float32
                )
                * score_scale
            )
            weights = jnp.exp(
                jnp.where(visible[None], scores - query_lse[:, :, None], masked_score)
            )
            value_part = jnp.einsum(
                "hqk,qhd->khd",
                weights.astype(jnp.bfloat16),
                grad_heads,
                preferred_element_type=jnp.float32,
            )
            weight_grad = jnp.einsum(
                "qhd,khd->hqk", grad_heads, value_heads, preferred_element_type=jnp.float32
            )
            score_grad = (weights * (weight_grad - query_delta[:, :, None])).astype(jnp.bfloat16)
            query_part = (
                jnp.einsum(
                    "hqk,khd->qhd", score_grad, key_heads, preferred_element_type=jnp.float32
                )
                * score_scale
            )
            key_part = (
                jnp.einsum(
                    "hqk,qhd->khd", score_grad, query_part_heads, preferred_element_type=jnp.float32
                )
                * score_scale
            )
            return (query_part, key_part, value_part)

        def nothing(unused):
            return (grad_zero, grad_zero, grad_zero)

        return lax.cond(is_attention & jnp.any(visible), compute, nothing, 0)

    def send_grads(key_acc, value_acc):
        return (
            passed_along(key_acc.astype(jnp.bfloat16), "seq", 1).astype(key_acc.dtype),
            passed_along(value_acc.astype(jnp.bfloat16), "seq", 1).astype(value_acc.dtype),
        )

    def key_step(cycle_state, unused):
        key_rows, value_rows, key_ids, key_acc, value_acc, hop_count, query_acc = cycle_state
        source = (seq_index - hop_count) % seq_count
        partial_terms = block_grads(
            query_low,
            grad_low,
            lse_rows,
            delta_rows,
            documents,
            query_index,
            key_rows,
            value_rows,
            key_ids,
            source * tok_rows + local_index,
        )
        key_rows, value_rows, key_ids = shifted((key_rows, value_rows, key_ids), "seq", 1)
        key_acc, value_acc = send_grads(key_acc + partial_terms[1], value_acc + partial_terms[2])
        return (
            (
                key_rows,
                value_rows,
                key_ids,
                key_acc,
                value_acc,
                hop_count + 1,
                query_acc + partial_terms[0],
            ),
            None,
        )

    start_state = (key_low, value_low, documents, grad_zero, grad_zero, jnp.int32(0), grad_zero)
    cycle_state, unused = lax.scan(key_step, start_state, None, length=seq_count - 1)
    key_rows, value_rows, key_ids, key_acc, value_acc, hop_count, query_acc = cycle_state
    source = (seq_index - hop_count) % seq_count
    partial_terms = block_grads(
        query_low,
        grad_low,
        lse_rows,
        delta_rows,
        documents,
        query_index,
        key_rows,
        value_rows,
        key_ids,
        source * tok_rows + local_index,
    )
    key_grad, value_grad = send_grads(key_acc + partial_terms[1], value_acc + partial_terms[2])
    query_grad = query_acc + partial_terms[0]

    def attention_tail(unused):
        query_back = rotate(query_grad, cosine, sine_rows, -1.0)
        key_back = rotate(key_grad, cosine, sine_rows, -1.0)
        packed_grad = (
            jnp.stack([query_back, key_back, value_grad], axis=2)
            .reshape(tok_rows, 3 * attn_width)
            .astype(jnp.bfloat16)
        )
        return (contract_cols(packed_grad, project_weight), packed_grad)

    def feed_tail(unused):
        return (
            contract_cols(hidden_low, up_weight),
            jnp.zeros((tok_rows, 3 * attn_width), jnp.bfloat16),
        )

    norm_grad, packed_grad = lax.cond(is_attention, attention_tail, feed_tail, 0)
    input_part, gain_part, shift_part = norm_pullback(norm_grad)
    input_grad = lax.psum_scatter(
        input_part.astype(jnp.bfloat16), ("branch", "tensor"), scatter_dimension=1, tiled=True
    ).astype(jnp.float32) + cotangent.astype(jnp.float32)

    def attention_rows(unused):
        return jnp.concatenate(
            [
                contract_rows(normed_low, packed_grad),
                contract_rows(full_cotangent, attended_low),
                jnp.zeros(
                    (
                        model_width
                        // (seq_count * lax.axis_size("branch"))
                        * lax.axis_size(("seq", "branch")),
                        2 * hidden_local,
                    ),
                    jnp.float32,
                ),
            ],
            axis=1,
        )

    def feed_rows(unused):
        return jnp.concatenate(
            [
                jnp.zeros(
                    (
                        model_width
                        // (seq_count * lax.axis_size("branch"))
                        * lax.axis_size(("seq", "branch")),
                        4 * attn_width,
                    ),
                    jnp.float32,
                ),
                contract_rows(normed_low, hidden_low),
                contract_rows(full_cotangent, active),
            ],
            axis=1,
        )

    shares = lax.psum_scatter(
        lax.cond(is_attention, attention_rows, feed_rows, 0).astype(jnp.bfloat16),
        ("seq", "branch"),
        scatter_dimension=0,
        tiled=True,
    ).astype(jnp.float32)
    project_grad = shares[:, : 3 * attn_width]
    output_grad = shares[:, 3 * attn_width : 4 * attn_width]
    up_grad = shares[:, 4 * attn_width : 4 * attn_width + hidden_local]
    down_grad = shares[:, 4 * attn_width + hidden_local :]
    offsets_part = lax.dynamic_update_slice(
        jnp.zeros((3 * model_width,), jnp.float32),
        jnp.sum(packed_grad, axis=0, dtype=jnp.float32),
        (tensor_index * (3 * attn_width),),
    )
    hidden_part = lax.dynamic_update_slice(
        jnp.zeros((hidden_local * lax.axis_size("tensor"),), jnp.float32),
        jnp.sum(hidden_low, axis=0, dtype=jnp.float32),
        (tensor_index * hidden_local,),
    )
    pair_zero = jnp.zeros((2, model_width), jnp.float32)
    gain_rows = lax.dynamic_update_slice(
        pair_zero, gain_part[None, :], (branch_index, jnp.int32(0))
    )
    shift_rows = lax.dynamic_update_slice(
        pair_zero, shift_part[None, :], (branch_index, jnp.int32(0))
    )
    column_sums = jnp.where(lead_tensor, jnp.sum(full_cotangent, axis=0, dtype=jnp.float32), 0.0)
    residual_rows = lax.dynamic_update_slice(
        pair_zero, column_sums[None, :], (branch_index, jnp.int32(0))
    )
    offsets_grad, hidden_grad, gain_grad, center_grad, residual_grad = lax.psum(
        (offsets_part, hidden_part, gain_rows, shift_rows, residual_rows),
        ("seq", "branch", "tensor"),
    )
    return (
        layer_out,
        input_grad,
        project_grad,
        output_grad,
        up_grad,
        down_grad,
        offsets_grad,
        hidden_grad,
        gain_grad,
        center_grad,
        residual_grad,
    )


MESH = pl.DeviceIdType.MESH
ANY = pl.BlockSpec(memory_space=pl.ANY)


def place():
    s, b, t = lax.axis_index("seq"), lax.axis_index("branch"), lax.axis_index("tensor")
    return s, b, t, s // 2, s % 2


def flip(value, bit):
    return value + bit - 2 * bit * value


def flip4(value, k):
    return 2 * flip(value // 2, k // 2) + flip(value % 2, k % 2)


def plane_peer(k):
    s, b, t, x, c = place()
    return (2 * flip(x, k // 2) + c, flip(b, k % 2), t)


def grid_peer(k):
    s, b, t, x, c = place()
    return (s, flip(b, k // 4), flip4(t, k % 4))


def sibling():
    s, b, t, x, c = place()
    return (flip4(s, 1), b, t)


def meet(devices):
    barrier = pltpu.get_barrier_semaphore()
    for device in devices:
        pl.semaphore_signal(barrier, inc=1, device_id=device, device_id_type=MESH)
    pl.semaphore_wait(barrier, len(devices))


def remote(src, dst, sems, index, device):
    return pltpu.make_async_remote_copy(
        src_ref=src, dst_ref=dst, send_sem=sems.at[0, index], recv_sem=sems.at[1, index],
        device_id=device, device_id_type=MESH)


def gather_kernel(x_ref, g_ref, table_ref, rows_ref, xo, go, tables_o, rows_o, sems, local):
    s, b, t, x, c = place()
    j = 4 * b + t
    meet([grid_peer(k) for k in range(1, 8)] + [(flip4(s, k), b, t) for k in (1, 2, 3)])
    copies = []
    own = pl.ds(pl.multiple_of(j * 256, 256), 256)
    for i, (src, dst) in enumerate(((x_ref, xo), (g_ref, go))):
        for k in range(1, 8):
            peer = grid_peer(k)
            rows = pl.ds(pl.multiple_of(peer[1] * 128, 128), 128)
            copies.append(remote(src.at[rows], dst.at[:, own], sems, 8 * i + k, peer))
        mine = pl.ds(pl.multiple_of(b * 128, 128), 128)
        copies.append(pltpu.make_async_copy(src.at[mine], dst.at[:, own], local.at[i]))
    for k in (1, 2, 3):
        copies.append(remote(table_ref, tables_o.at[s], sems, 16 + k, (flip4(s, k), b, t)))
    copies.append(pltpu.make_async_copy(table_ref, tables_o.at[s], local.at[2]))
    copies.append(remote(rows_ref, rows_o.at[b], sems, 20, grid_peer(4)))
    copies.append(pltpu.make_async_copy(rows_ref, rows_o.at[b], local.at[3]))
    for copy in copies:
        copy.start()
    for copy in copies:
        copy.wait()


def plane_kernel(act, hid, heads, xhat, cot, act_o, hid_o, heads_o, xs_o, cs_o, sems, local):
    s, b, t, x, c = place()
    m = 2 * x + b
    meet([plane_peer(k) for k in (1, 2, 3)] + [sibling()])
    first, copies = [], []
    slot = 4 * x + 2 * c + b
    for k in (1, 2, 3):
        peer = plane_peer(k)
        first.append(remote(heads.at[flip4(m, k)], heads_o.at[slot], sems, k, peer))
    first.append(pltpu.make_async_copy(heads.at[m], heads_o.at[slot], local.at[0]))
    for copy in first:
        copy.start()
    for k in (1, 2, 3):
        peer = plane_peer(k)
        there = flip4(m, k)
        for i, (src, dst) in enumerate(((xhat, xs_o), (cot, cs_o))):
            for half in (0, 1):
                block = 4 * (there // 2) + 2 * half + there % 2
                columns = pl.ds(pl.multiple_of(block * 256, 256), 256)
                copies.append(remote(src.at[:, columns], dst.at[m, :, pl.ds(half * 256, 256)],
                                     sems, 4 + 4 * (2 * i + half) + k, peer))
        copies.append(remote(act, act_o.at[m], sems, 20 + k, peer))
        copies.append(remote(hid, hid_o.at[m], sems, 24 + k, peer))
    for i, (src, dst) in enumerate(((xhat, xs_o), (cot, cs_o))):
        for half in (0, 1):
            block = 4 * x + 2 * half + b
            columns = pl.ds(pl.multiple_of(block * 256, 256), 256)
            copies.append(pltpu.make_async_copy(
                src.at[:, columns], dst.at[m, :, pl.ds(half * 256, 256)], local.at[1 + 2 * i + half]))
    copies.append(pltpu.make_async_copy(act, act_o.at[m], local.at[5]))
    copies.append(pltpu.make_async_copy(hid, hid_o.at[m], local.at[6]))
    for copy in copies:
        copy.start()
    for copy in first:
        copy.wait()
    pair = []
    for i in (0, 1):
        span = pl.ds(4 * i + 2 * c, 2)
        pair.append(remote(heads_o.at[span], heads_o.at[span], sems, 28 + i, sibling()))
    for copy in pair:
        copy.start()
    for copy in copies + pair:
        copy.wait()


def heads_kernel(mine, heads_o, sems, local):
    s, b, t, x, c = place()
    m = 2 * x + b
    meet([plane_peer(k) for k in (1, 2, 3)])
    copies = []
    for i in (0, 1):
        src = mine.at[pl.ds(4 * i + 2 * c, 2)]
        dst = heads_o.at[m, pl.ds(2 * i, 2)]
        for k in (1, 2, 3):
            copies.append(remote(src, dst, sems, 4 * i + k, plane_peer(k)))
        copies.append(pltpu.make_async_copy(src, dst, local.at[i]))
    for copy in copies:
        copy.start()
    for copy in copies:
        copy.wait()


def finish_kernel(out, grad, share, sums, out_o, grad_o, share_o, sums_o, pair, near, sems, local):
    s, b, t, x, c = place()
    j = 4 * b + t
    meet([grid_peer(k) for k in range(1, 8)] + [plane_peer(k) for k in (2, 3)] + [sibling()])
    copies = []
    first = remote(sums, pair, sems, 0, sibling())
    first.start()
    copies.append(remote(share, share_o, sems, 1, sibling()))
    for i, (src, dst) in enumerate(((out, out_o), (grad, grad_o))):
        for k in range(1, 8):
            peer = grid_peer(k)
            columns = pl.ds(pl.multiple_of((4 * peer[1] + peer[2]) * 256, 256), 256)
            copies.append(remote(src.at[:, columns], dst.at[j], sems, 8 + 8 * i + k, peer))
        columns = pl.ds(pl.multiple_of(j * 256, 256), 256)
        copies.append(pltpu.make_async_copy(src.at[:, columns], dst.at[j], local.at[i]))
    for copy in copies:
        copy.start()
    first.wait()
    pair[...] += sums[...]
    seconds = [remote(pair, near.at[k - 1], sems, 1 + k, plane_peer(k)) for k in (1, 2, 3)]
    for copy in seconds:
        copy.start()
    for copy in seconds:
        copy.wait()
    sums_o[t] = pair[...] + near[0] + near[1] + near[2]
    thirds = [remote(sums_o.at[t], sums_o.at[t], sems, 4 + k, grid_peer(k)) for k in (1, 2, 3)]
    for copy in thirds:
        copy.start()
    for copy in thirds + copies:
        copy.wait()


def call(kernel, inputs, outputs, count, ident, scratch=(), in_specs=None, out_specs=None):
    return pl.pallas_call(
        kernel,
        out_shape=[jax.ShapeDtypeStruct(shape, kind) for shape, kind in outputs],
        in_specs=in_specs or [ANY] * len(inputs),
        out_specs=out_specs or [ANY] * len(outputs),
        scratch_shapes=list(scratch)
        + [pltpu.SemaphoreType.DMA((2, count)), pltpu.SemaphoreType.DMA((8,))],
        compiler_params=pltpu.CompilerParams(collective_id=ident, has_side_effects=True),
    )(*inputs)


def turned(values, tables, direction):
    lane = lax.broadcasted_iota(jnp.int32, values.shape, values.ndim - 1)
    swapped = jnp.where(lane < ROT // 2, jnp.roll(values, -(ROT // 2), -1), jnp.roll(values, ROT // 2, -1))
    sines = jnp.where(lane < ROT, tables[..., HEAD_DIM:], 0.0)
    return values * tables[..., :HEAD_DIM] + (direction * sines) * swapped


def fast_device(tokens, cotangent, documents, positions, project_weight, offsets, output_weight,
                up_weight, hidden_bias, down_weight, norm_gain, norm_bias, residual_bias):
    bf16, f32 = jnp.bfloat16, jnp.float32
    s, b, t, x, c = place()
    scale = HEAD_DIM ** -0.5
    cosine, sines = rope_tables(positions)
    token_index = s * 256 + jnp.arange(256, dtype=jnp.int32)
    start = (token_index - positions).astype(f32)
    table = jnp.concatenate([
        cosine, cosine, jnp.ones((256, HEAD_DIM - ROT), f32),
        -sines, sines, jnp.broadcast_to(start[:, None], (256, HEAD_DIM - ROT))], axis=1)
    rows = jnp.concatenate([norm_gain, norm_bias, residual_bias, jnp.zeros((5, 2048), f32)], axis=0)
    xg, cg, tables, rows2 = call(
        gather_kernel, (tokens, cotangent, table, rows),
        (((128, 2048), bf16), ((128, 2048), bf16), ((4, 256, 256), f32), ((2, 8, 2048), f32)), 24, 0)
    gains, biases, resid = rows2[:, 0], rows2[:, 1], rows2[:, 2]
    tables = tables.reshape(1024, 256)
    own_table = lax.dynamic_slice(tables, (s * 256 + b * 128, 0), (128, 256))
    xf = xg.astype(f32)
    average = jnp.mean(xf, axis=-1, keepdims=True)
    centered = xf - average
    inverse = lax.rsqrt(jnp.mean(centered * centered, axis=-1, keepdims=True) + norm_eps)
    xhat = centered * inverse
    n0 = (xhat * gains[0] + biases[0]).astype(bf16)
    n1 = (xhat * gains[1] + biases[1]).astype(bf16)
    packed = (jnp.dot(n0, project_weight, preferred_element_type=f32) + offsets).reshape(128, 4, 3, 128)
    up_rows = jnp.dot(n1, up_weight, preferred_element_type=f32) + hidden_bias
    active = jax.nn.gelu(up_rows, approximate=False).astype(bf16)
    head_grad = jnp.dot(cg, output_weight, preferred_element_type=f32).astype(bf16)
    active_grad = jnp.dot(cg, down_weight, preferred_element_type=f32)
    gelu_value, pullback = jax.vjp(partial(jax.nn.gelu, approximate=False), up_rows)
    hidden_low = pullback(active_grad)[0].astype(bf16)
    per_head = own_table[:, None, :]
    heads = jnp.concatenate([
        turned(packed[:, :, 0], per_head, 1.0), turned(packed[:, :, 1], per_head, 1.0),
        packed[:, :, 2], head_grad.reshape(128, 4, 128).astype(f32)], axis=-1).astype(bf16)
    heads = heads.transpose(1, 0, 2)
    act_all, hid_all, heads_all, xs, cs = call(
        plane_kernel, (active, hidden_low, heads, xhat.astype(bf16), cg),
        (((4, 128, 2048), bf16), ((4, 128, 2048), bf16), ((8, 128, 512), bf16),
         ((4, 128, 512), bf16), ((4, 128, 512), bf16)), 32, 1)
    flat = heads_all.reshape(1024, 512)
    query, key, value, up = (flat[:, i * 128:(i + 1) * 128] for i in range(4))
    index = jnp.arange(1024, dtype=f32)
    visible = (index[None, :] <= index[:, None]) & (index[None, :] >= tables[:, 255:256])
    scores = contract_cols(query, key) * scale
    masked = jnp.where(visible, scores, masked_score)
    top = jnp.max(masked, axis=-1, keepdims=True)
    weights = jnp.where(visible, jnp.exp(masked - top), 0.0)
    total = jnp.sum(weights, axis=-1, keepdims=True)
    attended = jnp.dot(weights.astype(bf16), value, preferred_element_type=f32) / total
    delta = jnp.sum(up.astype(f32) * attended, axis=-1, keepdims=True)
    probs = weights / total
    value_grad = contract_rows(probs.astype(bf16), up)
    score_grad = (probs * (contract_cols(up, value) - delta)).astype(bf16)
    query_grad = jnp.dot(score_grad, key, preferred_element_type=f32) * scale
    key_grad = contract_rows(score_grad, query) * scale
    mine = jnp.concatenate([
        attended, turned(query_grad, tables, -1.0), turned(key_grad, tables, -1.0), value_grad],
        axis=1).astype(bf16).reshape(8, 128, 512)
    (heads_back,) = call(heads_kernel, (mine,), (((4, 4, 128, 512), bf16),), 8, 2)
    att_all = heads_back[..., :128].transpose(1, 2, 0, 3).reshape(512, 512)
    pack_all = heads_back[..., 128:].transpose(1, 2, 0, 3).reshape(512, 1536)
    m = 2 * x + b
    att = lax.dynamic_slice(att_all, (m * 128, 0), (128, 512))
    pack = lax.dynamic_slice(pack_all, (m * 128, 0), (128, 1536))
    out = (contract_cols(att, output_weight) + contract_cols(active, down_weight)).astype(bf16)
    parts, gain_rows, shift_rows = [], [], []
    for i, norm_grad in enumerate((contract_cols(pack, project_weight), contract_cols(hidden_low, up_weight))):
        g = norm_grad * gains[i]
        parts.append(inverse * (g - jnp.mean(g, axis=-1, keepdims=True)
                                - xhat * jnp.mean(g * xhat, axis=-1, keepdims=True)))
        gain_rows.append(jnp.sum(norm_grad * xhat, axis=0))
        shift_rows.append(jnp.sum(norm_grad, axis=0))
    grad = (parts[0] + parts[1]).astype(bf16)
    pack_sum = jnp.concatenate([jnp.sum(pack, axis=0, dtype=f32), jnp.zeros((512,), f32)])
    sums = jnp.stack(gain_rows + shift_rows + [
        jnp.sum(cg, axis=0, dtype=f32), pack_sum, jnp.sum(hidden_low, axis=0, dtype=f32),
        jnp.zeros((2048,), f32)])
    blocks = jnp.stack([4 * x + b, 4 * x + 2 + b])
    spread = lambda row: row.reshape(8, 256)[blocks].reshape(512)
    xs = xs.reshape(512, 512).astype(f32)
    cs = cs.reshape(512, 512)
    n0s = (xs * spread(gains[0]) + spread(biases[0])).astype(bf16)
    n1s = (xs * spread(gains[1]) + spread(biases[1])).astype(bf16)
    act_all, hid_all = act_all.reshape(512, 2048), hid_all.reshape(512, 2048)
    shares = jnp.concatenate([
        contract_rows(n0s, pack_all), contract_rows(cs, att_all),
        contract_rows(n1s, hid_all), contract_rows(cs, act_all)], axis=1)
    own = lax.dynamic_slice(shares, (c * 256, 0), (256, 6144))
    other = lax.dynamic_slice(shares, ((1 - c) * 256, 0), (256, 6144)).astype(bf16)
    vmem = pl.BlockSpec(memory_space=pltpu.VMEM)
    out_parts, grad_parts, share, sums_all = call(
        finish_kernel, (out, grad, other, sums),
        (((8, 128, 256), bf16), ((8, 128, 256), bf16), ((256, 6144), bf16), ((4, 8, 2048), f32)),
        24, 3, scratch=[pltpu.VMEM((8, 2048), f32), pltpu.VMEM((3, 8, 2048), f32)],
        in_specs=[ANY, ANY, ANY, vmem], out_specs=[ANY, ANY, ANY, vmem])
    total_rows = own + share.astype(f32)
    out_sum = jnp.sum(out_parts.reshape(2, 4, 128, 256).astype(f32), axis=1).reshape(256, 256)
    grad_sum = jnp.sum(grad_parts.reshape(2, 4, 128, 256).astype(f32), axis=1).reshape(256, 256)
    j = 4 * b + t
    bias = lax.dynamic_slice(resid[0] + resid[1], (j * 256,), (256,))
    layer_out = (tokens.astype(f32) + out_sum + bias).astype(bf16)
    input_grad = cotangent.astype(f32) + grad_sum
    across = jnp.sum(sums_all[:, :4], axis=0)
    return (
        layer_out, input_grad, total_rows[:, :1536], total_rows[:, 1536:2048],
        total_rows[:, 2048:4096], total_rows[:, 4096:],
        sums_all[:, 5, :1536].reshape(6144), sums_all[:, 6].reshape(8192),
        across[:2], across[2:], jnp.broadcast_to(sums_all[0, 4], (2, 2048)))


def solution(mesh):
    fits = (mesh.shape["seq"], mesh.shape["branch"], mesh.shape["tensor"]) == (4, 2, 4)
    return jax.shard_map(
        fast_device if fits else on_device,
        mesh=mesh,
        in_specs=(
            P("seq", ("branch", "tensor")),
            P("seq", ("branch", "tensor")),
            P("seq"),
            P("seq"),
            P(None, "tensor"),
            P("tensor"),
            P(None, "tensor"),
            P(None, "tensor"),
            P("tensor"),
            P(None, "tensor"),
            P("branch", None),
            P("branch", None),
            P("branch", None),
        ),
        out_specs=(
            P("seq", ("branch", "tensor")),
            P("seq", ("branch", "tensor")),
            P(("seq", "branch"), "tensor"),
            P(("seq", "branch"), "tensor"),
            P(("seq", "branch"), "tensor"),
            P(("seq", "branch"), "tensor"),
            P(),
            P(),
            P(),
            P(),
            P(),
        ),
        check_vma=False,
    )
```

```python
from functools import partial

import jax
import jax.numpy as jnp
from jax import lax
from jax.experimental import pallas as pl
from jax.experimental.pallas import tpu as pltpu
from jax.sharding import PartitionSpec as P

HEAD_DIM = 128
ROT = 32


norm_eps = 1e-05
rope_base = 10000.0
masked_score = -1e30


def passed_along(value, axis, steps):
    count = lax.axis_size(axis)
    pairs = [(source, (source + steps) % count) for source in range(count)]
    return lax.ppermute(value, axis, pairs)


def shifted(array, axis, by):
    count = lax.axis_size(axis)
    pairs = [(i, i + by) for i in range(count) if 0 <= i + by < count]
    return lax.ppermute(array, axis, pairs)


def layer_norm(values, gain_row, shift_row):
    average = jnp.mean(values, axis=-1, keepdims=True)
    centered = values - average
    variance = jnp.mean(centered * centered, axis=-1, keepdims=True)
    return centered * lax.rsqrt(variance + norm_eps) * gain_row + shift_row


def rope_tables(places):
    half_rot = ROT // 2
    frequency = rope_base ** (-(2.0 * jnp.arange(half_rot, dtype=jnp.float32)) / ROT)
    angles = places.astype(jnp.float32)[:, None] * frequency[None, :]
    return (jnp.cos(angles), jnp.sin(angles))


def rotate(values, cosine, sine_rows, direction):
    half_rot = ROT // 2
    first_half = values[..., :half_rot]
    second_half = values[..., half_rot:ROT]
    cos_table = cosine[:, None, :]
    sin_table = direction * sine_rows[:, None, :]
    return jnp.concatenate(
        [
            first_half * cos_table - second_half * sin_table,
            second_half * cos_table + first_half * sin_table,
            values[..., ROT:],
        ],
        axis=-1,
    )


def contract_rows(first_side, second_side):
    return lax.dot_general(
        first_side, second_side, (((0,), (0,)), ((), ())), preferred_element_type=jnp.float32
    )


def contract_cols(first_side, second_side):
    return lax.dot_general(
        first_side, second_side, (((1,), (1,)), ((), ())), preferred_element_type=jnp.float32
    )


def on_device(
    tokens,
    cotangent,
    documents,
    positions,
    project_weight,
    offsets,
    output_weight,
    up_weight,
    hidden_bias,
    down_weight,
    norm_gain,
    norm_bias,
    residual_bias,
):
    tok_rows = tokens.shape[0]
    model_width = up_weight.shape[0]
    attn_width = output_weight.shape[1]
    local_heads = attn_width // HEAD_DIM
    hidden_local = up_weight.shape[1]
    seq_count = lax.axis_size("seq")
    seq_index = lax.axis_index("seq")
    branch_index = lax.axis_index("branch")
    tensor_index = lax.axis_index("tensor")
    is_attention = branch_index == 0
    lead_tensor = tensor_index == 0
    score_scale = HEAD_DIM ** (-0.5)
    local_index = jnp.arange(tok_rows, dtype=jnp.int32)
    query_index = seq_index * tok_rows + local_index
    full_tokens, full_cotangent = (
        lax.all_gather(tokens, ("branch", "tensor"), axis=1, tiled=True),
        lax.all_gather(cotangent, ("branch", "tensor"), axis=1, tiled=True),
    )
    gain_row = norm_gain[0]
    shift_row = norm_bias[0]
    normed, norm_pullback = jax.vjp(
        layer_norm, full_tokens.astype(jnp.float32), gain_row, shift_row
    )
    normed_low = normed.astype(jnp.bfloat16)
    cosine, sine_rows = rope_tables(positions)
    zeros_heads = jnp.zeros((tok_rows, attn_width), jnp.bfloat16)
    zeros_hidden = jnp.zeros((tok_rows, hidden_local), jnp.float32)
    hidden_zero = jnp.zeros((tok_rows, hidden_local), jnp.bfloat16)
    zeros_stats = jnp.zeros((local_heads, tok_rows), jnp.float32)
    grad_zero = jnp.zeros((tok_rows, local_heads, HEAD_DIM), jnp.float32)

    def attention_front(unused):
        packed = jnp.dot(normed_low, project_weight, preferred_element_type=jnp.float32) + offsets
        packed = packed.reshape(tok_rows, local_heads, 3, HEAD_DIM)
        query_rot = rotate(packed[:, :, 0], cosine, sine_rows, 1.0).reshape(tok_rows, attn_width)
        key_rot = rotate(packed[:, :, 1], cosine, sine_rows, 1.0).reshape(tok_rows, attn_width)
        value_rows = packed[:, :, 2].reshape(tok_rows, attn_width)
        return (
            query_rot.astype(jnp.bfloat16),
            key_rot.astype(jnp.bfloat16),
            value_rows.astype(jnp.bfloat16),
            zeros_hidden,
            hidden_zero,
        )

    def feed_front(unused):
        up_rows = jnp.dot(normed_low, up_weight, preferred_element_type=jnp.float32) + hidden_bias
        active = jax.nn.gelu(up_rows, approximate=False).astype(jnp.bfloat16)
        return (zeros_heads, zeros_heads, zeros_heads, up_rows, active)

    query_low, key_low, value_low, up_rows, active = lax.cond(
        is_attention, attention_front, feed_front, 0
    )
    query_heads = query_low.reshape(tok_rows, local_heads, HEAD_DIM)

    def absorb(totals, key_rows, value_rows, key_ids, offset):
        key_count = key_rows.shape[0]
        key_index = offset + jnp.arange(key_count, dtype=jnp.int32)
        visible = (documents[:, None] == key_ids[None, :]) & (
            key_index[None, :] <= query_index[:, None]
        )

        def update(running):
            run_max, run_sum, run_acc = running
            scores = (
                jnp.einsum(
                    "qhd,khd->hqk",
                    query_heads,
                    key_rows.reshape(key_count, local_heads, HEAD_DIM),
                    preferred_element_type=jnp.float32,
                )
                * score_scale
            )
            masked = jnp.where(visible[None], scores, masked_score)
            new_max = jnp.maximum(run_max, jnp.max(masked, axis=-1))
            weights = jnp.where(visible[None], jnp.exp(masked - new_max[:, :, None]), 0.0)
            factor = jnp.exp(run_max - new_max)
            blended = jnp.einsum(
                "hqk,khd->qhd",
                weights.astype(jnp.bfloat16),
                value_rows.reshape(key_count, local_heads, HEAD_DIM),
                preferred_element_type=jnp.float32,
            )
            return (
                new_max,
                run_sum * factor + jnp.sum(weights, axis=-1),
                run_acc * factor.T[:, :, None] + blended,
            )

        def unchanged(running):
            return running

        return lax.cond(is_attention & jnp.any(visible), update, unchanged, totals)

    initial = (jnp.full((local_heads, tok_rows), masked_score, jnp.float32), zeros_stats, grad_zero)
    totals = initial
    key_rows = lax.all_gather(key_low, "seq", axis=0, tiled=True)
    value_rows = lax.all_gather(value_low, "seq", axis=0, tiled=True)
    key_ids = lax.all_gather(documents, "seq", axis=0, tiled=True)
    key_count = key_rows.shape[0]
    groups = key_count // tok_rows

    def absorb_group(running, sliced):
        return (absorb(running, sliced[0], sliced[1], sliced[2], sliced[3]), None)

    starts = tok_rows * jnp.arange(groups, dtype=jnp.int32)
    stacked = (
        key_rows.reshape(groups, tok_rows, attn_width),
        value_rows.reshape(groups, tok_rows, attn_width),
        key_ids.reshape(groups, tok_rows),
        starts,
    )
    totals, unused = lax.scan(absorb_group, totals, stacked)
    run_max, run_sum, run_acc = totals

    def attention_out(unused):
        attended = run_acc / run_sum.T[:, :, None]
        attended_low = attended.reshape(tok_rows, attn_width).astype(jnp.bfloat16)
        return (
            contract_cols(attended_low, output_weight),
            attended,
            attended_low,
            run_max + jnp.log(run_sum),
        )

    def feed_out(unused):
        return (contract_cols(active, down_weight), grad_zero, zeros_heads, zeros_stats)

    branch_out, attended, attended_low, lse_rows = lax.cond(
        is_attention, attention_out, feed_out, 0
    )
    branch_out = branch_out + jnp.where(lead_tensor, residual_bias[0], 0.0)
    summed = lax.psum_scatter(
        branch_out.astype(jnp.bfloat16), ("branch", "tensor"), scatter_dimension=1, tiled=True
    ).astype(jnp.float32)
    layer_out = (tokens.astype(jnp.float32) + summed).astype(jnp.bfloat16)

    def attention_prep(unused):
        grad_low = jnp.dot(
            full_cotangent, output_weight, preferred_element_type=jnp.float32
        ).astype(jnp.bfloat16)
        delta_rows = jnp.sum(
            grad_low.reshape(tok_rows, local_heads, HEAD_DIM).astype(jnp.float32) * attended,
            axis=-1,
        ).T
        return (grad_low, delta_rows, hidden_zero)

    def feed_prep(unused):
        active_grad = jnp.dot(full_cotangent, down_weight, preferred_element_type=jnp.float32)
        gelu_value, gelu_pullback = jax.vjp(partial(jax.nn.gelu, approximate=False), up_rows)
        return (zeros_heads, zeros_stats, gelu_pullback(active_grad)[0].astype(jnp.bfloat16))

    grad_low, delta_rows, hidden_low = lax.cond(is_attention, attention_prep, feed_prep, 0)

    def block_grads(
        query_rows,
        grad_rows,
        query_lse,
        query_delta,
        query_ids,
        query_place,
        key_rows,
        value_rows,
        key_ids,
        key_place,
    ):
        visible = (query_ids[:, None] == key_ids[None, :]) & (
            key_place[None, :] <= query_place[:, None]
        )

        def compute(unused):
            query_part_heads = query_rows.reshape(tok_rows, local_heads, HEAD_DIM)
            grad_heads = grad_rows.reshape(tok_rows, local_heads, HEAD_DIM)
            key_heads = key_rows.reshape(tok_rows, local_heads, HEAD_DIM)
            value_heads = value_rows.reshape(tok_rows, local_heads, HEAD_DIM)
            scores = (
                jnp.einsum(
                    "qhd,khd->hqk", query_part_heads, key_heads, preferred_element_type=jnp.float32
                )
                * score_scale
            )
            weights = jnp.exp(
                jnp.where(visible[None], scores - query_lse[:, :, None], masked_score)
            )
            value_part = jnp.einsum(
                "hqk,qhd->khd",
                weights.astype(jnp.bfloat16),
                grad_heads,
                preferred_element_type=jnp.float32,
            )
            weight_grad = jnp.einsum(
                "qhd,khd->hqk", grad_heads, value_heads, preferred_element_type=jnp.float32
            )
            score_grad = (weights * (weight_grad - query_delta[:, :, None])).astype(jnp.bfloat16)
            query_part = (
                jnp.einsum(
                    "hqk,khd->qhd", score_grad, key_heads, preferred_element_type=jnp.float32
                )
                * score_scale
            )
            key_part = (
                jnp.einsum(
                    "hqk,qhd->khd", score_grad, query_part_heads, preferred_element_type=jnp.float32
                )
                * score_scale
            )
            return (query_part, key_part, value_part)

        def nothing(unused):
            return (grad_zero, grad_zero, grad_zero)

        return lax.cond(is_attention & jnp.any(visible), compute, nothing, 0)

    def send_grads(key_acc, value_acc):
        return (
            passed_along(key_acc.astype(jnp.bfloat16), "seq", 1).astype(key_acc.dtype),
            passed_along(value_acc.astype(jnp.bfloat16), "seq", 1).astype(value_acc.dtype),
        )

    def key_step(cycle_state, unused):
        key_rows, value_rows, key_ids, key_acc, value_acc, hop_count, query_acc = cycle_state
        source = (seq_index - hop_count) % seq_count
        partial_terms = block_grads(
            query_low,
            grad_low,
            lse_rows,
            delta_rows,
            documents,
            query_index,
            key_rows,
            value_rows,
            key_ids,
            source * tok_rows + local_index,
        )
        key_rows, value_rows, key_ids = shifted((key_rows, value_rows, key_ids), "seq", 1)
        key_acc, value_acc = send_grads(key_acc + partial_terms[1], value_acc + partial_terms[2])
        return (
            (
                key_rows,
                value_rows,
                key_ids,
                key_acc,
                value_acc,
                hop_count + 1,
                query_acc + partial_terms[0],
            ),
            None,
        )

    start_state = (key_low, value_low, documents, grad_zero, grad_zero, jnp.int32(0), grad_zero)
    cycle_state, unused = lax.scan(key_step, start_state, None, length=seq_count - 1)
    key_rows, value_rows, key_ids, key_acc, value_acc, hop_count, query_acc = cycle_state
    source = (seq_index - hop_count) % seq_count
    partial_terms = block_grads(
        query_low,
        grad_low,
        lse_rows,
        delta_rows,
        documents,
        query_index,
        key_rows,
        value_rows,
        key_ids,
        source * tok_rows + local_index,
    )
    key_grad, value_grad = send_grads(key_acc + partial_terms[1], value_acc + partial_terms[2])
    query_grad = query_acc + partial_terms[0]

    def attention_tail(unused):
        query_back = rotate(query_grad, cosine, sine_rows, -1.0)
        key_back = rotate(key_grad, cosine, sine_rows, -1.0)
        packed_grad = (
            jnp.stack([query_back, key_back, value_grad], axis=2)
            .reshape(tok_rows, 3 * attn_width)
            .astype(jnp.bfloat16)
        )
        return (contract_cols(packed_grad, project_weight), packed_grad)

    def feed_tail(unused):
        return (
            contract_cols(hidden_low, up_weight),
            jnp.zeros((tok_rows, 3 * attn_width), jnp.bfloat16),
        )

    norm_grad, packed_grad = lax.cond(is_attention, attention_tail, feed_tail, 0)
    input_part, gain_part, shift_part = norm_pullback(norm_grad)
    input_grad = lax.psum_scatter(
        input_part.astype(jnp.bfloat16), ("branch", "tensor"), scatter_dimension=1, tiled=True
    ).astype(jnp.float32) + cotangent.astype(jnp.float32)

    def attention_rows(unused):
        return jnp.concatenate(
            [
                contract_rows(normed_low, packed_grad),
                contract_rows(full_cotangent, attended_low),
                jnp.zeros(
                    (
                        model_width
                        // (seq_count * lax.axis_size("branch"))
                        * lax.axis_size(("seq", "branch")),
                        2 * hidden_local,
                    ),
                    jnp.float32,
                ),
            ],
            axis=1,
        )

    def feed_rows(unused):
        return jnp.concatenate(
            [
                jnp.zeros(
                    (
                        model_width
                        // (seq_count * lax.axis_size("branch"))
                        * lax.axis_size(("seq", "branch")),
                        4 * attn_width,
                    ),
                    jnp.float32,
                ),
                contract_rows(normed_low, hidden_low),
                contract_rows(full_cotangent, active),
            ],
            axis=1,
        )

    shares = lax.psum_scatter(
        lax.cond(is_attention, attention_rows, feed_rows, 0).astype(jnp.bfloat16),
        ("seq", "branch"),
        scatter_dimension=0,
        tiled=True,
    ).astype(jnp.float32)
    project_grad = shares[:, : 3 * attn_width]
    output_grad = shares[:, 3 * attn_width : 4 * attn_width]
    up_grad = shares[:, 4 * attn_width : 4 * attn_width + hidden_local]
    down_grad = shares[:, 4 * attn_width + hidden_local :]
    offsets_part = lax.dynamic_update_slice(
        jnp.zeros((3 * model_width,), jnp.float32),
        jnp.sum(packed_grad, axis=0, dtype=jnp.float32),
        (tensor_index * (3 * attn_width),),
    )
    hidden_part = lax.dynamic_update_slice(
        jnp.zeros((hidden_local * lax.axis_size("tensor"),), jnp.float32),
        jnp.sum(hidden_low, axis=0, dtype=jnp.float32),
        (tensor_index * hidden_local,),
    )
    pair_zero = jnp.zeros((2, model_width), jnp.float32)
    gain_rows = lax.dynamic_update_slice(
        pair_zero, gain_part[None, :], (branch_index, jnp.int32(0))
    )
    shift_rows = lax.dynamic_update_slice(
        pair_zero, shift_part[None, :], (branch_index, jnp.int32(0))
    )
    column_sums = jnp.where(lead_tensor, jnp.sum(full_cotangent, axis=0, dtype=jnp.float32), 0.0)
    residual_rows = lax.dynamic_update_slice(
        pair_zero, column_sums[None, :], (branch_index, jnp.int32(0))
    )
    offsets_grad, hidden_grad, gain_grad, center_grad, residual_grad = lax.psum(
        (offsets_part, hidden_part, gain_rows, shift_rows, residual_rows),
        ("seq", "branch", "tensor"),
    )
    return (
        layer_out,
        input_grad,
        project_grad,
        output_grad,
        up_grad,
        down_grad,
        offsets_grad,
        hidden_grad,
        gain_grad,
        center_grad,
        residual_grad,
    )


MESH = pl.DeviceIdType.MESH
bf16, f32 = jnp.bfloat16, jnp.float32


def place():
    s, b, t = lax.axis_index("seq"), lax.axis_index("branch"), lax.axis_index("tensor")
    return s, b, t, s // 2, s % 2


def flip(value, bit):
    return value + bit - 2 * bit * value


def flip4(value, k):
    return 2 * flip(value // 2, k // 2) + flip(value % 2, k % 2)


def plane_peer(k):
    s, b, t, x, c = place()
    return (2 * flip(x, k // 2) + c, flip(b, k % 2), t)


def grid_peer(k):
    s, b, t, x, c = place()
    return (s, flip(b, k // 4), flip4(t, k % 4))


def sibling():
    s, b, t, x, c = place()
    return (flip4(s, 1), b, t)


def meet(devices):
    barrier = pltpu.get_barrier_semaphore()
    for device in devices:
        pl.semaphore_signal(barrier, inc=1, device_id=device, device_id_type=MESH)
    pl.semaphore_wait(barrier, len(devices))


def at(index, size):
    return pl.ds(pl.multiple_of(index * size, size), size)


def dot(first, second):
    return jnp.dot(first, second, preferred_element_type=f32)


def turned(values, tables, direction):
    lane = lax.broadcasted_iota(jnp.int32, values.shape, 1)
    swapped = jnp.where(
        lane < ROT // 2,
        pltpu.roll(values, HEAD_DIM - ROT // 2, 1),
        pltpu.roll(values, ROT // 2, 1),
    )
    sines = jnp.where(lane < ROT, tables[:, HEAD_DIM:], 0.0)
    return values * tables[:, :HEAD_DIM] + (direction * sines) * swapped


def layer_kernel(
    tok, cot, table, rows, offs, hbias, wp_h, wo_h, wu_h, wd_h,
    layer_o, grad_o, project_o, output_o, up_o, down_o, sums_o,
    wp, wo, wu, wd, xg, cg, tables, rows2, xh, inv, n0, n1, xb, gd, act, hid, hs, heads, att, pack,
    attf, lse, dk_acc, dv_acc, ob, ro, gb, rg, acco, accg, xs, cs, n0t, n1t, ct, own, other, recv,
    usum, pair, near, sems, local,
):
    s, b, t, x, c = place()
    m, j = 2 * x + b, 4 * b + t
    slot = 4 * x + 2 * c + b
    scale = HEAD_DIM ** -0.5
    mine = at(m, 128)
    used = {"sem": 0, "local": 0}
    sent = []

    def send(src, dst, device):
        index = used["sem"]
        used["sem"] += 1
        copy = pltpu.make_async_remote_copy(
            src_ref=src, dst_ref=dst, send_sem=sems.at[0, index], recv_sem=sems.at[1, index],
            device_id=device, device_id_type=MESH)
        copy.start()
        sent.append(copy)
        return copy

    def move(src, dst):
        index = used["local"]
        used["local"] += 1
        copy = pltpu.make_async_copy(src, dst, local.at[index])
        copy.start()
        return copy

    def arrive(copies):
        for copy in copies:
            copy.wait_recv()

    def direct(view):
        return [send(view(m), view(m), plane_peer(k)) for k in (2, 1)]

    def relay(copies, half):
        out = []
        for i, k in enumerate((2, 1)):
            copies[i].wait_recv()
            part = half(flip4(m, k), i)
            out.append(send(part, part, plane_peer(3 - k)))
        return out

    def loop(count, body):
        def step(i, carry):
            body(i)
            return carry
        lax.fori_loop(0, count, step, 0)

    usum[...] = jnp.zeros_like(usum)
    wp_load, wu_load = move(wp_h, wp), move(wu_h, wu)
    wo_load, wd_load = move(wo_h, wo), move(wd_h, wd)
    meet([grid_peer(k) for k in range(1, 8)] + [plane_peer(2), plane_peer(3)]
         + [(flip4(s, k), b, t) for k in (1, 3)])

    def gather(src, dst):
        copies = []
        for k in (1, 2, 3, 4, 5, 6, 7):
            peer = grid_peer(k)
            copies.append(send(src.at[at(peer[1], 128)], dst.at[:, at(j, 256)], peer))
        return copies, move(src.at[at(b, 128)], dst.at[:, at(j, 256)])

    x_copies, x_own = gather(tok, xg)
    row_copy = send(rows, rows2.at[b], grid_peer(4))
    row_own = move(rows, rows2.at[b])
    table_copies = [send(table, tables.at[at(s, 256)], (flip4(s, k), b, t)) for k in (1, 2, 3)]
    table_own = move(table, tables.at[at(s, 256)])
    arrive(x_copies)
    x_own.wait()
    g_copies, g_own = gather(cot, cg)
    arrive([row_copy])
    row_own.wait()

    def norm(i):
        part = at(i, 16)
        v = xg[part, :].astype(f32)
        centered = v - jnp.mean(v, axis=-1, keepdims=True)
        inverse = lax.rsqrt(jnp.mean(centered * centered, axis=-1, keepdims=True) + norm_eps)
        hat = centered * inverse
        xh[part, :] = hat
        xb[part, :] = hat.astype(bf16)
        inv[part, :] = jnp.broadcast_to(inverse, (16, 128))
        n0[part, :] = (hat * rows2[0, 0:1, :] + rows2[0, 1:2, :]).astype(bf16)
        n1[part, :] = (hat * rows2[1, 0:1, :] + rows2[1, 1:2, :]).astype(bf16)

    loop(8, norm)

    def slices(src, dst):
        copies, kept = [], []
        for half in (0, 1):
            cols = pl.ds(half * 256, 256)
            for k in (1, 2, 3):
                there = flip4(m, k)
                block = 4 * (there // 2) + 2 * half + there % 2
                copies.append(send(src.at[:, at(block, 256)], dst.at[mine, cols], plane_peer(k)))
            kept.append(move(src.at[:, at(4 * x + 2 * half + b, 256)], dst.at[mine, cols]))
        return copies, kept

    wp_load.wait()

    def project(h):
        p = dot(n0[...], wp[:, at(h, 384)]) + offs[:, at(h, 384)]
        tab = table[at(b, 128), :]
        hs[h, :, 0:128] = turned(p[:, 0:128], tab, 1.0).astype(bf16)
        hs[h, :, 128:256] = turned(p[:, 128:256], tab, 1.0).astype(bf16)
        hs[h, :, 256:384] = p[:, 256:384].astype(bf16)

    loop(4, project)

    def to_heads(cols):
        copies = [send(hs.at[flip4(m, k), :, cols], heads.at[at(slot, 128), cols], plane_peer(k))
                  for k in (3, 2, 1)]
        return copies, move(hs.at[m, :, cols], heads.at[at(slot, 128), cols])

    def to_sibling(copies, kept, cols):
        arrive(copies)
        kept.wait()
        parts = [heads.at[pl.ds(512 * i + 256 * c, 256), cols] for i in (0, 1)]
        arrive([send(part, part, sibling()) for part in parts])

    qkv_cols, up_cols = pl.ds(0, 384), pl.ds(384, 128)
    qkv_copies, qkv_own = to_heads(qkv_cols)
    xs_copies, xs_own = slices(xb, xs)
    wu_load.wait()

    def feed(n):
        cols = at(n, 256)
        u = dot(n1[...], wu[:, cols]) + hbias[:, cols]
        phi = 0.5 + 0.5 * lax.erf(u * 0.7071067811865476)
        act[mine, cols] = (u * phi).astype(bf16)
        gd[:, cols] = phi + u * (0.3989422804014327 * jnp.exp(-0.5 * u * u))

    loop(8, feed)
    act_view = lambda i: act.at[at(i, 128)]
    act_half = lambda i, h: act.at[pl.ds(pl.multiple_of(128 * i + 64 * h, 64), 64)]
    hid_view = lambda i: hid.at[at(i, 128)]
    hid_half = lambda i, h: hid.at[pl.ds(pl.multiple_of(128 * i + 64 * h, 64), 64)]
    att_view = lambda i: att.at[:, at(i, 128)]
    att_half = lambda i, h: att.at[pl.ds(256 * h, 256), at(i, 128)]
    pack_view = lambda i: pack.at[:, at(i, 384)]
    pack_half = lambda i, h: pack.at[pl.ds(256 * h, 256), at(i, 384)]
    act_copies = direct(act_view)

    to_sibling(qkv_copies, qkv_own, qkv_cols)
    arrive(table_copies)
    table_own.wait()

    def score_rows(i):
        part = at(i, 256)
        scores = contract_cols(heads[part, 0:128], heads[:, 128:256]) * scale
        start = tables[part, 128:256][:, 127:128]
        query = (i * 256 + lax.broadcasted_iota(jnp.int32, (256, 1), 0)).astype(f32)
        key = lax.broadcasted_iota(jnp.int32, (256, 1024), 1).astype(f32)
        return scores, (key <= query) & (key >= start)

    def forward(i):
        part = at(i, 256)
        scores, visible = score_rows(i)
        masked = jnp.where(visible, scores, masked_score)
        top = jnp.max(masked, axis=-1, keepdims=True)
        weights = jnp.where(visible, jnp.exp(masked - top), 0.0)
        total = jnp.sum(weights, axis=-1, keepdims=True)
        attf[part, :] = dot(weights.astype(bf16), heads[:, 256:384]) / total
        lse[part, :] = jnp.broadcast_to(top + jnp.log(total), (256, 128))

    loop(4, forward)
    for i in (0, 1):
        att[pl.ds(256 * i, 256), at(m, 128)] = attf[pl.ds(512 * i + 256 * c, 256), :].astype(bf16)
    att_copies = direct(att_view)

    arrive(g_copies)
    g_own.wait()
    wo_load.wait()

    def head_grads(n):
        p = dot(cg[...], wo[:, at(n, 256)]).astype(bf16)
        hs[2 * n, :, 384:512] = p[:, :128]
        hs[2 * n + 1, :, 384:512] = p[:, 128:]

    loop(2, head_grads)
    up_copies, up_own = to_heads(up_cols)
    cs_copies, cs_own = slices(cg, cs)
    wd_load.wait()

    def hidden(n):
        cols = at(n, 256)
        low = (dot(cg[...], wd[:, cols]) * gd[:, cols]).astype(bf16)
        hid[mine, cols] = low
        usum[6:7, cols] = jnp.sum(low.astype(f32), axis=0, keepdims=True)
        usum[4:5, cols] = jnp.sum(cg[:, cols].astype(f32), axis=0, keepdims=True)

    loop(8, hidden)

    to_sibling(up_copies, up_own, up_cols)
    dk_acc[...] = jnp.zeros_like(dk_acc)
    dv_acc[...] = jnp.zeros_like(dv_acc)

    def backward(i):
        part = at(i, 256)
        scores, visible = score_rows(i)
        probs = jnp.where(visible, jnp.exp(jnp.where(visible, scores, masked_score) - lse[part, 0:1]), 0.0)
        up = heads[part, 384:512]
        delta = jnp.sum(up.astype(f32) * attf[part, :], axis=-1, keepdims=True)
        grads = (probs * (contract_cols(up, heads[:, 256:384]) - delta)).astype(bf16)
        dv_acc[...] += contract_rows(probs.astype(bf16), up)
        dk_acc[...] += contract_rows(grads, heads[part, 0:128])

        @pl.when(i % 2 == c)
        def _():
            back = dot(grads, heads[:, 128:256]) * scale
            pack[at(i // 2, 256), at(3 * m, 128)] = turned(back, tables[part, :], -1.0).astype(bf16)

    loop(4, backward)
    for i in (0, 1):
        part = pl.ds(512 * i + 256 * c, 256)
        key_back = turned(dk_acc[part, :] * scale, tables[part, :], -1.0)
        pack[pl.ds(256 * i, 256), at(3 * m + 1, 128)] = key_back.astype(bf16)
        pack[pl.ds(256 * i, 256), at(3 * m + 2, 128)] = dv_acc[part, :].astype(bf16)
    pack_copies = direct(pack_view)
    att_relays = relay(att_copies, att_half)
    act_relays = relay(act_copies, act_half)
    hid_copies = direct(hid_view)

    def feed_out(n):
        acco[n] = contract_cols(act[mine, :], wd[at(n, 256), :])

    loop(8, feed_out)

    def norm_grad(n, values, weight, which):
        cols = at(n, 256)
        ng = contract_cols(values, weight[cols, :])
        usum[which : which + 1, cols] = jnp.sum(ng * xh[:, cols], axis=0, keepdims=True)
        usum[which + 2 : which + 3, cols] = jnp.sum(ng, axis=0, keepdims=True)
        return ng * rows2[which, 0:1, cols]

    def feed_grad(n):
        accg[n] = norm_grad(n, hid[mine, :], wu, 1)

    loop(8, feed_grad)
    arrive(att_relays)

    def finish_out(n):
        ob[n] = (acco[n] + contract_cols(att[mine, :], wo[at(n, 256), :])).astype(bf16)

    loop(8, finish_out)

    def scatter(src, dst):
        copies = [send(src.at[4 * grid_peer(k)[1] + grid_peer(k)[2]], dst.at[j], grid_peer(k))
                  for k in range(1, 8)]
        return copies, move(src.at[j], dst.at[j])

    out_copies, out_own = scatter(ob, ro)
    arrive(xs_copies + cs_copies)
    for copy in xs_own + cs_own:
        copy.wait()

    def transpose_slices(i):
        part = at(i, 128)
        for half in (0, 1):
            cols = pl.ds(256 * half, 256)
            block = at(4 * x + 2 * half + b, 256)
            hat = xs[part, cols].astype(f32)
            for which, dst in ((0, n0t), (1, n1t)):
                low = hat * rows2[which, 0:1, block] + rows2[which, 1:2, block]
                dst[cols, part] = low.T.astype(bf16)
            ct[cols, part] = cs[part, cols].astype(f32).T.astype(bf16)

    loop(4, transpose_slices)

    pack_relays = relay(pack_copies, pack_half)
    arrive(pack_relays)

    def attention_grad(n):
        accg[n] += norm_grad(n, pack[mine, :], wp, 0)

    loop(8, attention_grad)
    usum[5:6, 0:1536] = jnp.sum(pack[mine, :].astype(f32), axis=0, keepdims=True)
    pair_copy = send(usum, pair, sibling())

    zero = jnp.zeros((128, 1), f32)

    def means(n, carry):
        g = accg[n]
        return (carry[0] + jnp.sum(g, axis=-1, keepdims=True),
                carry[1] + jnp.sum(g * xh[:, at(n, 256)], axis=-1, keepdims=True))

    mean, slope = lax.fori_loop(0, 8, means, (zero, zero))
    mean, slope = mean * (1.0 / 2048), slope * (1.0 / 2048)

    def finish_grad(n):
        gb[n] = (inv[:, 0:1] * (accg[n] - mean - xh[:, at(n, 256)] * slope)).astype(bf16)

    loop(8, finish_grad)
    grad_copies, grad_own = scatter(gb, rg)

    writes = []

    def matrix(lhs, rhs, count, out, base):
        for copy in writes[-1:]:
            for part in copy:
                part.wait()
        first = used["sem"]
        used["sem"] += count

        def swap(i):
            return pltpu.make_async_remote_copy(
                src_ref=other.at[base + i], dst_ref=recv.at[base + i],
                send_sem=sems.at[0, first + i], recv_sem=sems.at[1, first + i],
                device_id=sibling(), device_id_type=MESH)

        def produce(i):
            right = rhs[:, at(i, 512)]
            other[base + i] = dot(lhs[at(1 - c, 256), :], right).astype(bf16)
            swap(i).start()
            own[i] = dot(lhs[at(c, 256), :], right)

        loop(count, produce)
        done = []
        for i in range(count):
            swap(i).wait_recv()
            own[i] += recv[base + i].astype(f32)
            done.append(move(own.at[i], out.at[:, pl.ds(512 * i, 512)]))
            sent.append(swap(i))
        writes.append(done)

    arrive(act_relays)
    matrix(ct, act, 4, down_o, 0)
    hid_relays = relay(hid_copies, hid_half)
    matrix(ct, att, 1, output_o, 4)
    arrive([pair_copy])
    pair[...] += usum[...]
    near_copies = [send(pair, near.at[k - 1], plane_peer(k)) for k in (1, 2, 3)]
    matrix(n0t, pack, 3, project_o, 5)
    arrive(near_copies)
    sums_o[t] = pair[...] + near[0] + near[1] + near[2]
    sum_copies = [send(sums_o.at[t], sums_o.at[t], grid_peer(k)) for k in (1, 2, 3)]
    arrive(out_copies)
    out_own.wait()
    columns = at(j, 256)
    bias = rows2[0, 2:3, columns] + rows2[1, 2:3, columns]
    for h in (0, 1):
        part = pl.ds(128 * h, 128)
        total = bias + tok[part, :].astype(f32)
        for i in range(4):
            total = total + ro[4 * h + i].astype(f32)
        layer_o[part, :] = total.astype(bf16)
    arrive(grad_copies)
    grad_own.wait()
    for h in (0, 1):
        part = pl.ds(128 * h, 128)
        total = cot[part, :].astype(f32)
        for i in range(4):
            total = total + rg[4 * h + i].astype(f32)
        grad_o[part, :] = total
    arrive(hid_relays)
    matrix(n1t, hid, 4, up_o, 8)
    arrive(sum_copies)
    for part in writes[-1]:
        part.wait()
    for copy in sent:
        copy.wait_send()
    assert used["sem"] <= 100 and used["local"] <= 40, used


def fast_device(tokens, cotangent, documents, positions, project_weight, offsets, output_weight,
                up_weight, hidden_bias, down_weight, norm_gain, norm_bias, residual_bias):
    s = lax.axis_index("seq")
    cosine, sines = rope_tables(positions)
    token_index = s * 256 + jnp.arange(256, dtype=jnp.int32)
    start = (token_index - positions).astype(f32)
    table = jnp.concatenate([
        cosine, cosine, jnp.ones((256, HEAD_DIM - ROT), f32),
        -sines, sines, jnp.broadcast_to(start[:, None], (256, HEAD_DIM - ROT))], axis=1)
    rows = jnp.concatenate([norm_gain, norm_bias, residual_bias, jnp.zeros((5, 2048), f32)], axis=0)
    vmem, anywhere = pl.BlockSpec(memory_space=pltpu.VMEM), pl.BlockSpec(memory_space=pl.ANY)
    shape = jax.ShapeDtypeStruct
    low = lambda *size: pltpu.VMEM(size, bf16)
    full = lambda *size: pltpu.VMEM(size, f32)
    layer_out, input_grad, project_grad, output_grad, up_grad, down_grad, sums = pl.pallas_call(
        layer_kernel,
        out_shape=[
            shape((256, 256), bf16), shape((256, 256), f32), shape((256, 1536), f32),
            shape((256, 512), f32), shape((256, 2048), f32), shape((256, 2048), f32),
            shape((4, 8, 2048), f32)],
        in_specs=[vmem] * 6 + [anywhere] * 4,
        out_specs=[vmem] * 2 + [anywhere] * 4 + [vmem],
        scratch_shapes=[
            low(2048, 1536), low(2048, 512), low(2048, 2048), low(2048, 2048),
            low(128, 2048), low(128, 2048), full(1024, 256), full(2, 8, 2048),
            full(128, 2048), full(128, 128), low(128, 2048), low(128, 2048), low(128, 2048),
            full(128, 2048), low(512, 2048), low(512, 2048), low(4, 128, 512), low(1024, 512),
            low(512, 512), low(512, 1536), full(1024, 128), full(1024, 128), full(1024, 128),
            full(1024, 128), low(8, 128, 256), low(8, 128, 256), low(8, 128, 256),
            low(8, 128, 256), full(8, 128, 256), full(8, 128, 256), low(512, 512), low(512, 512),
            low(512, 512), low(512, 512), low(512, 512), full(4, 256, 512), low(12, 256, 512),
            low(12, 256, 512), full(8, 2048), full(8, 2048), full(3, 8, 2048),
            pltpu.SemaphoreType.DMA((2, 100)), pltpu.SemaphoreType.DMA((40,))],
        compiler_params=pltpu.CompilerParams(
            collective_id=0, has_side_effects=True, vmem_limit_bytes=LIMIT),
    )(tokens, cotangent, table, rows, offsets[None], hidden_bias[None], project_weight,
      output_weight, up_weight, down_weight)
    across = jnp.sum(sums[:, :4], axis=0)
    return (
        layer_out, input_grad, project_grad, output_grad, up_grad, down_grad,
        sums[:, 5, :1536].reshape(6144), sums[:, 6].reshape(8192),
        across[:2], across[2:], jnp.broadcast_to(sums[0, 4], (2, 2048)))


LIMIT = 62 << 20


def solution(mesh):
    fits = (mesh.shape["seq"], mesh.shape["branch"], mesh.shape["tensor"]) == (4, 2, 4)
    return jax.shard_map(
        fast_device if fits else on_device,
        mesh=mesh,
        in_specs=(
            P("seq", ("branch", "tensor")),
            P("seq", ("branch", "tensor")),
            P("seq"),
            P("seq"),
            P(None, "tensor"),
            P("tensor"),
            P(None, "tensor"),
            P(None, "tensor"),
            P("tensor"),
            P(None, "tensor"),
            P("branch", None),
            P("branch", None),
            P("branch", None),
        ),
        out_specs=(
            P("seq", ("branch", "tensor")),
            P("seq", ("branch", "tensor")),
            P(("seq", "branch"), "tensor"),
            P(("seq", "branch"), "tensor"),
            P(("seq", "branch"), "tensor"),
            P(("seq", "branch"), "tensor"),
            P(),
            P(),
            P(),
            P(),
            P(),
        ),
        check_vma=False,
    )
```

```python
from functools import partial

import jax
import jax.numpy as jnp
from jax import lax
from jax.experimental import pallas as pl
from jax.experimental.pallas import tpu as pltpu
from jax.sharding import PartitionSpec as P

HEAD_DIM = 128
ROT = 32


norm_eps = 1e-05
rope_base = 10000.0
masked_score = -1e30


def passed_along(value, axis, steps):
    count = lax.axis_size(axis)
    pairs = [(source, (source + steps) % count) for source in range(count)]
    return lax.ppermute(value, axis, pairs)


def shifted(array, axis, by):
    count = lax.axis_size(axis)
    pairs = [(i, i + by) for i in range(count) if 0 <= i + by < count]
    return lax.ppermute(array, axis, pairs)


def layer_norm(values, gain_row, shift_row):
    average = jnp.mean(values, axis=-1, keepdims=True)
    centered = values - average
    variance = jnp.mean(centered * centered, axis=-1, keepdims=True)
    return centered * lax.rsqrt(variance + norm_eps) * gain_row + shift_row


def rope_tables(places):
    half_rot = ROT // 2
    frequency = rope_base ** (-(2.0 * jnp.arange(half_rot, dtype=jnp.float32)) / ROT)
    angles = places.astype(jnp.float32)[:, None] * frequency[None, :]
    return (jnp.cos(angles), jnp.sin(angles))


def rotate(values, cosine, sine_rows, direction):
    half_rot = ROT // 2
    first_half = values[..., :half_rot]
    second_half = values[..., half_rot:ROT]
    cos_table = cosine[:, None, :]
    sin_table = direction * sine_rows[:, None, :]
    return jnp.concatenate(
        [
            first_half * cos_table - second_half * sin_table,
            second_half * cos_table + first_half * sin_table,
            values[..., ROT:],
        ],
        axis=-1,
    )


def contract_rows(first_side, second_side):
    return lax.dot_general(
        first_side, second_side, (((0,), (0,)), ((), ())), preferred_element_type=jnp.float32
    )


def contract_cols(first_side, second_side):
    return lax.dot_general(
        first_side, second_side, (((1,), (1,)), ((), ())), preferred_element_type=jnp.float32
    )


def on_device(
    tokens,
    cotangent,
    documents,
    positions,
    project_weight,
    offsets,
    output_weight,
    up_weight,
    hidden_bias,
    down_weight,
    norm_gain,
    norm_bias,
    residual_bias,
):
    tok_rows = tokens.shape[0]
    model_width = up_weight.shape[0]
    attn_width = output_weight.shape[1]
    local_heads = attn_width // HEAD_DIM
    hidden_local = up_weight.shape[1]
    seq_count = lax.axis_size("seq")
    seq_index = lax.axis_index("seq")
    branch_index = lax.axis_index("branch")
    tensor_index = lax.axis_index("tensor")
    is_attention = branch_index == 0
    lead_tensor = tensor_index == 0
    score_scale = HEAD_DIM ** (-0.5)
    local_index = jnp.arange(tok_rows, dtype=jnp.int32)
    query_index = seq_index * tok_rows + local_index
    full_tokens, full_cotangent = (
        lax.all_gather(tokens, ("branch", "tensor"), axis=1, tiled=True),
        lax.all_gather(cotangent, ("branch", "tensor"), axis=1, tiled=True),
    )
    gain_row = norm_gain[0]
    shift_row = norm_bias[0]
    normed, norm_pullback = jax.vjp(
        layer_norm, full_tokens.astype(jnp.float32), gain_row, shift_row
    )
    normed_low = normed.astype(jnp.bfloat16)
    cosine, sine_rows = rope_tables(positions)
    zeros_heads = jnp.zeros((tok_rows, attn_width), jnp.bfloat16)
    zeros_hidden = jnp.zeros((tok_rows, hidden_local), jnp.float32)
    hidden_zero = jnp.zeros((tok_rows, hidden_local), jnp.bfloat16)
    zeros_stats = jnp.zeros((local_heads, tok_rows), jnp.float32)
    grad_zero = jnp.zeros((tok_rows, local_heads, HEAD_DIM), jnp.float32)

    def attention_front(unused):
        packed = jnp.dot(normed_low, project_weight, preferred_element_type=jnp.float32) + offsets
        packed = packed.reshape(tok_rows, local_heads, 3, HEAD_DIM)
        query_rot = rotate(packed[:, :, 0], cosine, sine_rows, 1.0).reshape(tok_rows, attn_width)
        key_rot = rotate(packed[:, :, 1], cosine, sine_rows, 1.0).reshape(tok_rows, attn_width)
        value_rows = packed[:, :, 2].reshape(tok_rows, attn_width)
        return (
            query_rot.astype(jnp.bfloat16),
            key_rot.astype(jnp.bfloat16),
            value_rows.astype(jnp.bfloat16),
            zeros_hidden,
            hidden_zero,
        )

    def feed_front(unused):
        up_rows = jnp.dot(normed_low, up_weight, preferred_element_type=jnp.float32) + hidden_bias
        active = jax.nn.gelu(up_rows, approximate=False).astype(jnp.bfloat16)
        return (zeros_heads, zeros_heads, zeros_heads, up_rows, active)

    query_low, key_low, value_low, up_rows, active = lax.cond(
        is_attention, attention_front, feed_front, 0
    )
    query_heads = query_low.reshape(tok_rows, local_heads, HEAD_DIM)

    def absorb(totals, key_rows, value_rows, key_ids, offset):
        key_count = key_rows.shape[0]
        key_index = offset + jnp.arange(key_count, dtype=jnp.int32)
        visible = (documents[:, None] == key_ids[None, :]) & (
            key_index[None, :] <= query_index[:, None]
        )

        def update(running):
            run_max, run_sum, run_acc = running
            scores = (
                jnp.einsum(
                    "qhd,khd->hqk",
                    query_heads,
                    key_rows.reshape(key_count, local_heads, HEAD_DIM),
                    preferred_element_type=jnp.float32,
                )
                * score_scale
            )
            masked = jnp.where(visible[None], scores, masked_score)
            new_max = jnp.maximum(run_max, jnp.max(masked, axis=-1))
            weights = jnp.where(visible[None], jnp.exp(masked - new_max[:, :, None]), 0.0)
            factor = jnp.exp(run_max - new_max)
            blended = jnp.einsum(
                "hqk,khd->qhd",
                weights.astype(jnp.bfloat16),
                value_rows.reshape(key_count, local_heads, HEAD_DIM),
                preferred_element_type=jnp.float32,
            )
            return (
                new_max,
                run_sum * factor + jnp.sum(weights, axis=-1),
                run_acc * factor.T[:, :, None] + blended,
            )

        def unchanged(running):
            return running

        return lax.cond(is_attention & jnp.any(visible), update, unchanged, totals)

    initial = (jnp.full((local_heads, tok_rows), masked_score, jnp.float32), zeros_stats, grad_zero)
    totals = initial
    key_rows = lax.all_gather(key_low, "seq", axis=0, tiled=True)
    value_rows = lax.all_gather(value_low, "seq", axis=0, tiled=True)
    key_ids = lax.all_gather(documents, "seq", axis=0, tiled=True)
    key_count = key_rows.shape[0]
    groups = key_count // tok_rows

    def absorb_group(running, sliced):
        return (absorb(running, sliced[0], sliced[1], sliced[2], sliced[3]), None)

    starts = tok_rows * jnp.arange(groups, dtype=jnp.int32)
    stacked = (
        key_rows.reshape(groups, tok_rows, attn_width),
        value_rows.reshape(groups, tok_rows, attn_width),
        key_ids.reshape(groups, tok_rows),
        starts,
    )
    totals, unused = lax.scan(absorb_group, totals, stacked)
    run_max, run_sum, run_acc = totals

    def attention_out(unused):
        attended = run_acc / run_sum.T[:, :, None]
        attended_low = attended.reshape(tok_rows, attn_width).astype(jnp.bfloat16)
        return (
            contract_cols(attended_low, output_weight),
            attended,
            attended_low,
            run_max + jnp.log(run_sum),
        )

    def feed_out(unused):
        return (contract_cols(active, down_weight), grad_zero, zeros_heads, zeros_stats)

    branch_out, attended, attended_low, lse_rows = lax.cond(
        is_attention, attention_out, feed_out, 0
    )
    branch_out = branch_out + jnp.where(lead_tensor, residual_bias[0], 0.0)
    summed = lax.psum_scatter(
        branch_out.astype(jnp.bfloat16), ("branch", "tensor"), scatter_dimension=1, tiled=True
    ).astype(jnp.float32)
    layer_out = (tokens.astype(jnp.float32) + summed).astype(jnp.bfloat16)

    def attention_prep(unused):
        grad_low = jnp.dot(
            full_cotangent, output_weight, preferred_element_type=jnp.float32
        ).astype(jnp.bfloat16)
        delta_rows = jnp.sum(
            grad_low.reshape(tok_rows, local_heads, HEAD_DIM).astype(jnp.float32) * attended,
            axis=-1,
        ).T
        return (grad_low, delta_rows, hidden_zero)

    def feed_prep(unused):
        active_grad = jnp.dot(full_cotangent, down_weight, preferred_element_type=jnp.float32)
        gelu_value, gelu_pullback = jax.vjp(partial(jax.nn.gelu, approximate=False), up_rows)
        return (zeros_heads, zeros_stats, gelu_pullback(active_grad)[0].astype(jnp.bfloat16))

    grad_low, delta_rows, hidden_low = lax.cond(is_attention, attention_prep, feed_prep, 0)

    def block_grads(
        query_rows,
        grad_rows,
        query_lse,
        query_delta,
        query_ids,
        query_place,
        key_rows,
        value_rows,
        key_ids,
        key_place,
    ):
        visible = (query_ids[:, None] == key_ids[None, :]) & (
            key_place[None, :] <= query_place[:, None]
        )

        def compute(unused):
            query_part_heads = query_rows.reshape(tok_rows, local_heads, HEAD_DIM)
            grad_heads = grad_rows.reshape(tok_rows, local_heads, HEAD_DIM)
            key_heads = key_rows.reshape(tok_rows, local_heads, HEAD_DIM)
            value_heads = value_rows.reshape(tok_rows, local_heads, HEAD_DIM)
            scores = (
                jnp.einsum(
                    "qhd,khd->hqk", query_part_heads, key_heads, preferred_element_type=jnp.float32
                )
                * score_scale
            )
            weights = jnp.exp(
                jnp.where(visible[None], scores - query_lse[:, :, None], masked_score)
            )
            value_part = jnp.einsum(
                "hqk,qhd->khd",
                weights.astype(jnp.bfloat16),
                grad_heads,
                preferred_element_type=jnp.float32,
            )
            weight_grad = jnp.einsum(
                "qhd,khd->hqk", grad_heads, value_heads, preferred_element_type=jnp.float32
            )
            score_grad = (weights * (weight_grad - query_delta[:, :, None])).astype(jnp.bfloat16)
            query_part = (
                jnp.einsum(
                    "hqk,khd->qhd", score_grad, key_heads, preferred_element_type=jnp.float32
                )
                * score_scale
            )
            key_part = (
                jnp.einsum(
                    "hqk,qhd->khd", score_grad, query_part_heads, preferred_element_type=jnp.float32
                )
                * score_scale
            )
            return (query_part, key_part, value_part)

        def nothing(unused):
            return (grad_zero, grad_zero, grad_zero)

        return lax.cond(is_attention & jnp.any(visible), compute, nothing, 0)

    def send_grads(key_acc, value_acc):
        return (
            passed_along(key_acc.astype(jnp.bfloat16), "seq", 1).astype(key_acc.dtype),
            passed_along(value_acc.astype(jnp.bfloat16), "seq", 1).astype(value_acc.dtype),
        )

    def key_step(cycle_state, unused):
        key_rows, value_rows, key_ids, key_acc, value_acc, hop_count, query_acc = cycle_state
        source = (seq_index - hop_count) % seq_count
        partial_terms = block_grads(
            query_low,
            grad_low,
            lse_rows,
            delta_rows,
            documents,
            query_index,
            key_rows,
            value_rows,
            key_ids,
            source * tok_rows + local_index,
        )
        key_rows, value_rows, key_ids = shifted((key_rows, value_rows, key_ids), "seq", 1)
        key_acc, value_acc = send_grads(key_acc + partial_terms[1], value_acc + partial_terms[2])
        return (
            (
                key_rows,
                value_rows,
                key_ids,
                key_acc,
                value_acc,
                hop_count + 1,
                query_acc + partial_terms[0],
            ),
            None,
        )

    start_state = (key_low, value_low, documents, grad_zero, grad_zero, jnp.int32(0), grad_zero)
    cycle_state, unused = lax.scan(key_step, start_state, None, length=seq_count - 1)
    key_rows, value_rows, key_ids, key_acc, value_acc, hop_count, query_acc = cycle_state
    source = (seq_index - hop_count) % seq_count
    partial_terms = block_grads(
        query_low,
        grad_low,
        lse_rows,
        delta_rows,
        documents,
        query_index,
        key_rows,
        value_rows,
        key_ids,
        source * tok_rows + local_index,
    )
    key_grad, value_grad = send_grads(key_acc + partial_terms[1], value_acc + partial_terms[2])
    query_grad = query_acc + partial_terms[0]

    def attention_tail(unused):
        query_back = rotate(query_grad, cosine, sine_rows, -1.0)
        key_back = rotate(key_grad, cosine, sine_rows, -1.0)
        packed_grad = (
            jnp.stack([query_back, key_back, value_grad], axis=2)
            .reshape(tok_rows, 3 * attn_width)
            .astype(jnp.bfloat16)
        )
        return (contract_cols(packed_grad, project_weight), packed_grad)

    def feed_tail(unused):
        return (
            contract_cols(hidden_low, up_weight),
            jnp.zeros((tok_rows, 3 * attn_width), jnp.bfloat16),
        )

    norm_grad, packed_grad = lax.cond(is_attention, attention_tail, feed_tail, 0)
    input_part, gain_part, shift_part = norm_pullback(norm_grad)
    input_grad = lax.psum_scatter(
        input_part.astype(jnp.bfloat16), ("branch", "tensor"), scatter_dimension=1, tiled=True
    ).astype(jnp.float32) + cotangent.astype(jnp.float32)

    def attention_rows(unused):
        return jnp.concatenate(
            [
                contract_rows(normed_low, packed_grad),
                contract_rows(full_cotangent, attended_low),
                jnp.zeros(
                    (
                        model_width
                        // (seq_count * lax.axis_size("branch"))
                        * lax.axis_size(("seq", "branch")),
                        2 * hidden_local,
                    ),
                    jnp.float32,
                ),
            ],
            axis=1,
        )

    def feed_rows(unused):
        return jnp.concatenate(
            [
                jnp.zeros(
                    (
                        model_width
                        // (seq_count * lax.axis_size("branch"))
                        * lax.axis_size(("seq", "branch")),
                        4 * attn_width,
                    ),
                    jnp.float32,
                ),
                contract_rows(normed_low, hidden_low),
                contract_rows(full_cotangent, active),
            ],
            axis=1,
        )

    shares = lax.psum_scatter(
        lax.cond(is_attention, attention_rows, feed_rows, 0).astype(jnp.bfloat16),
        ("seq", "branch"),
        scatter_dimension=0,
        tiled=True,
    ).astype(jnp.float32)
    project_grad = shares[:, : 3 * attn_width]
    output_grad = shares[:, 3 * attn_width : 4 * attn_width]
    up_grad = shares[:, 4 * attn_width : 4 * attn_width + hidden_local]
    down_grad = shares[:, 4 * attn_width + hidden_local :]
    offsets_part = lax.dynamic_update_slice(
        jnp.zeros((3 * model_width,), jnp.float32),
        jnp.sum(packed_grad, axis=0, dtype=jnp.float32),
        (tensor_index * (3 * attn_width),),
    )
    hidden_part = lax.dynamic_update_slice(
        jnp.zeros((hidden_local * lax.axis_size("tensor"),), jnp.float32),
        jnp.sum(hidden_low, axis=0, dtype=jnp.float32),
        (tensor_index * hidden_local,),
    )
    pair_zero = jnp.zeros((2, model_width), jnp.float32)
    gain_rows = lax.dynamic_update_slice(
        pair_zero, gain_part[None, :], (branch_index, jnp.int32(0))
    )
    shift_rows = lax.dynamic_update_slice(
        pair_zero, shift_part[None, :], (branch_index, jnp.int32(0))
    )
    column_sums = jnp.where(lead_tensor, jnp.sum(full_cotangent, axis=0, dtype=jnp.float32), 0.0)
    residual_rows = lax.dynamic_update_slice(
        pair_zero, column_sums[None, :], (branch_index, jnp.int32(0))
    )
    offsets_grad, hidden_grad, gain_grad, center_grad, residual_grad = lax.psum(
        (offsets_part, hidden_part, gain_rows, shift_rows, residual_rows),
        ("seq", "branch", "tensor"),
    )
    return (
        layer_out,
        input_grad,
        project_grad,
        output_grad,
        up_grad,
        down_grad,
        offsets_grad,
        hidden_grad,
        gain_grad,
        center_grad,
        residual_grad,
    )


MESH = pl.DeviceIdType.MESH
bf16, f32 = jnp.bfloat16, jnp.float32


def place():
    s, b, t = lax.axis_index("seq"), lax.axis_index("branch"), lax.axis_index("tensor")
    return s, b, t, s // 2, s % 2


def flip(value, bit):
    return value + bit - 2 * bit * value


def flip4(value, k):
    return 2 * flip(value // 2, k // 2) + flip(value % 2, k % 2)


def plane_peer(k):
    s, b, t, x, c = place()
    return (2 * flip(x, k // 2) + c, flip(b, k % 2), t)


def grid_peer(k):
    s, b, t, x, c = place()
    return (s, flip(b, k // 4), flip4(t, k % 4))


def sibling():
    s, b, t, x, c = place()
    return (flip4(s, 1), b, t)


def meet(devices):
    barrier = pltpu.get_barrier_semaphore()
    for device in devices:
        pl.semaphore_signal(barrier, inc=1, device_id=device, device_id_type=MESH)
    pl.semaphore_wait(barrier, len(devices))


def at(index, size):
    return pl.ds(pl.multiple_of(index * size, size), size)


def dot(first, second):
    return jnp.dot(first, second, preferred_element_type=f32)


def turned(values, cosine, sines):
    lane = lax.broadcasted_iota(jnp.int32, values.shape, 1)
    swapped = jnp.where(
        lane < ROT // 2,
        pltpu.roll(values, HEAD_DIM - ROT // 2, 1),
        pltpu.roll(values, ROT // 2, 1),
    )
    return values * cosine + sines * swapped


def layer_kernel(
    tok, cot, places, waves, gain, shift, residual, offs, hbias, wp_h, wo_h, wu_h, wd_h,
    layer_o, grad_o, project_o, output_o, up_o, down_o, sums_o,
    wp, wo, wu, wd, xg, cg, posr, starts, cosr, sinr, rows2, xh, mean_s, inv_s, n0, n1, gd, act, hid,
    hs, heads, att, pack, attf, lse, dk_acc, dv_acc, ob, ro, gb, rg, swap_b, back_b, acco, accg,
    n0t, n1t, ct, own, low_own, other, recv, usum, pair, near, sems, local,
):
    s, b, t, x, c = place()
    m, j = 2 * x + b, 4 * b + t
    slot = 4 * x + 2 * c + b
    scale = HEAD_DIM ** -0.5
    mine = at(m, 128)
    used = {"sem": 0, "local": 0}
    sent = []

    def send(src, dst, device):
        index = used["sem"]
        used["sem"] += 1
        copy = pltpu.make_async_remote_copy(
            src_ref=src, dst_ref=dst, send_sem=sems.at[0, index], recv_sem=sems.at[1, index],
            device_id=device, device_id_type=MESH)
        copy.start()
        sent.append(copy)
        return copy

    def move(src, dst):
        index = used["local"]
        used["local"] += 1
        copy = pltpu.make_async_copy(src, dst, local.at[index])
        copy.start()
        return copy

    def arrive(copies):
        for copy in copies:
            copy.wait_recv()

    def direct(view):
        return [send(view(m), view(m), plane_peer(k)) for k in (2, 1)]

    def relay(copies, half):
        out = []
        for i, k in enumerate((2, 1)):
            copies[i].wait_recv()
            part = half(flip4(m, k), i)
            out.append(send(part, part, plane_peer(3 - k)))
        return out

    def loop(count, body):
        def step(i, carry):
            body(i)
            return carry
        lax.fori_loop(0, count, step, 0)

    def block(k):
        return at(4 * flip(b, k // 4) + flip4(t, k % 4), 256)

    usum[...] = jnp.zeros_like(usum)
    wp_load, wo_load = move(wp_h, wp), move(wo_h, wo)
    wu_load, wd_load = move(wu_h, wu), move(wd_h, wd)
    rows2[b] = jnp.zeros((8, 2048), f32)
    rows2[b, 0:1, :] = gain[...]
    rows2[b, 1:2, :] = shift[...]
    rows2[b, 2:3, :] = residual[...]
    posr[s] = jnp.broadcast_to(places[...].astype(f32), (8, 256))
    meet([grid_peer(k) for k in (1, 2, 3, 4)] + [plane_peer(2), plane_peer(3)]
         + [(flip4(s, k), b, t) for k in (1, 3)])

    def gather_first(src, dst):
        over = send(src.at[at(1 - b, 128)], dst.at[at(flip4(m, 1), 128), at(j, 256)], grid_peer(4))
        half = src.at[at(b, 128)]
        copies = [send(half, dst.at[mine, at(j, 256)], grid_peer(k)) for k in (1, 3, 2)]
        return over, copies, move(half, dst.at[mine, at(j, 256)])

    def gather_second(over, dst):
        over.wait_recv()
        part = dst.at[mine, block(4)]
        return [send(part, part, grid_peer(k)) for k in (1, 3, 2)]

    x_over, x_near, x_own = gather_first(tok, xg)
    row_copy = send(rows2.at[b], rows2.at[b], grid_peer(4))
    place_copies = [send(posr.at[s], posr.at[s], (flip4(s, k), b, t)) for k in (1, 2, 3)]
    spread = {}

    def on_plane(k):
        part = xg.at[mine, block(k)]
        spread[k] = [send(part, part, plane_peer(i)) for i in (2, 1)]

    x_own.wait()
    on_plane(0)
    x_far = gather_second(x_over, xg)
    on_plane(4)
    arrive(place_copies)
    for i in range(4):
        row = jnp.broadcast_to(posr[i, 0:1, :], (128, 256))
        index = (256 * i + lax.broadcasted_iota(jnp.int32, (256, 128), 0)).astype(f32)
        starts[pl.ds(256 * i, 256), :] = index - row.T
    for i in (0, 1):
        angle = posr[2 * i + c, 0:1, :] * waves[...]
        part = pl.ds(256 * i, 256)
        sign = jnp.where(lax.broadcasted_iota(jnp.int32, (ROT, 256), 0) < ROT // 2, -1.0, 1.0)
        rest = jnp.zeros((HEAD_DIM - ROT, 256), f32)
        cosr[part, :] = jnp.concatenate([jnp.cos(angle), rest + 1.0], axis=0).T
        sinr[part, :] = jnp.concatenate([jnp.sin(angle) * sign, rest], axis=0).T
    for i, k in enumerate((1, 3, 2)):
        x_near[i].wait_recv()
        on_plane(k)
        x_far[i].wait_recv()
        on_plane(k + 4)
    g_over, g_near, g_own = gather_first(cot, cg)
    arrive([row_copy])

    def norm(which, whole):
        def rows(i):
            part = pl.ds(pl.multiple_of(which * 128 + 16 * i, 16), 16)
            v = xg[part, :].astype(f32)
            mean = jnp.mean(v, axis=-1, keepdims=True)
            centered = v - mean
            inverse = lax.rsqrt(jnp.mean(centered * centered, axis=-1, keepdims=True) + norm_eps)
            hat = centered * inverse
            mean_s[part, :] = jnp.broadcast_to(mean, (16, 128))
            inv_s[part, :] = jnp.broadcast_to(inverse, (16, 128))
            n1_part = pl.ds(pl.multiple_of((which % 2) * 128 + 16 * i, 16), 16)
            n1[n1_part, :] = (hat * rows2[1, 0:1, :] + rows2[1, 1:2, :]).astype(bf16)
            if whole:
                xh[at(i, 16), :] = hat
                n0[at(i, 16), :] = (hat * rows2[0, 0:1, :] + rows2[0, 1:2, :]).astype(bf16)

        loop(8, rows)

    norm(m, True)
    g_far = gather_second(g_over, cg)
    wp_load.wait()
    turn = pl.ds(pl.multiple_of(256 * x + 128 * b, 128), 128)

    def project(h):
        p = dot(n0[...], wp[:, at(h, 384)]) + offs[:, at(h, 384)]
        hs[h, :, 0:128] = turned(p[:, 0:128], cosr[turn, :], sinr[turn, :]).astype(bf16)
        hs[h, :, 128:256] = turned(p[:, 128:256], cosr[turn, :], sinr[turn, :]).astype(bf16)
        hs[h, :, 256:384] = p[:, 256:384].astype(bf16)

    loop(4, project)

    def to_heads(cols):
        copies = [send(hs.at[flip4(m, k), :, cols], heads.at[at(slot, 128), cols], plane_peer(k))
                  for k in (3, 2, 1)]
        return copies, move(hs.at[m, :, cols], heads.at[at(slot, 128), cols])

    def to_sibling(copies, kept, cols):
        arrive(copies)
        kept.wait()
        parts = [heads.at[pl.ds(512 * i + 256 * c, 256), cols] for i in (0, 1)]
        return [send(part, part, sibling()) for part in parts]

    qkv_cols, up_cols = pl.ds(0, 384), pl.ds(384, 128)
    qkv_copies, qkv_own = to_heads(qkv_cols)
    x_relays, x_rest = [], []
    for k in range(4):
        spread[k][0].wait_recv()
        part = xg.at[at(flip4(m, 2), 128), block(k)]
        x_relays.append(send(part, part, plane_peer(1)))
        spread[k + 4][1].wait_recv()
        part = xg.at[at(flip4(m, 1), 128), block(k)]
        x_relays.append(send(part, part, plane_peer(2)))
        x_rest.append(spread[k + 4][0])
    arrive([spread[k][1] for k in range(4)])
    norm(flip4(m, 1), False)
    wu_load.wait()

    def feed(pair_index):
        rows = at(pair_index, 256)

        def tile(n):
            cols = at(n, 256)
            u = dot(n1[...], wu[:, cols]) + hbias[:, cols]
            phi = 0.5 + 0.5 * lax.erf(u * 0.7071067811865476)
            act[rows, cols] = (u * phi).astype(bf16)
            gd[rows, cols] = (phi + u * (0.3989422804014327 * jnp.exp(-0.5 * u * u))).astype(gd.dtype)

        loop(8, tile)

    feed(x)
    qkv_pair = to_sibling(qkv_copies, qkv_own, qkv_cols)
    cg_view = lambda i: cg.at[at(i, 128)]
    cg_half = lambda i, h: cg.at[pl.ds(pl.multiple_of(128 * i + 64 * h, 64), 64)]
    att_view = lambda i: att.at[:, at(i, 128)]
    att_half = lambda i, h: att.at[pl.ds(256 * h, 256), at(i, 128)]
    pack_view = lambda i: pack.at[:, at(i, 384)]
    pack_half = lambda i, h: pack.at[pl.ds(256 * h, 256), at(i, 384)]

    arrive(g_near + g_far)
    g_own.wait()
    wo_load.wait()

    def head_grads(n):
        p = dot(cg[mine, :], wo[:, at(n, 256)]).astype(bf16)
        hs[2 * n, :, 384:512] = p[:, :128]
        hs[2 * n + 1, :, 384:512] = p[:, 128:]

    loop(2, head_grads)
    up_copies, up_own = to_heads(up_cols)
    g_copies = direct(cg_view)
    arrive(qkv_pair)

    def score_rows(i):
        part = at(i, 256)
        scores = contract_cols(heads[part, 0:128], heads[:, 128:256]) * scale
        query = (i * 256 + lax.broadcasted_iota(jnp.int32, (256, 1), 0)).astype(f32)
        key = lax.broadcasted_iota(jnp.int32, (256, 1024), 1).astype(f32)
        return scores, (key <= query) & (key >= starts[part, 0:1])

    def forward(i):
        part = at(i, 256)
        scores, visible = score_rows(i)
        masked = jnp.where(visible, scores, masked_score)
        top = jnp.max(masked, axis=-1, keepdims=True)
        weights = jnp.where(visible, jnp.exp(masked - top), 0.0)
        total = jnp.sum(weights, axis=-1, keepdims=True)
        attf[part, :] = dot(weights.astype(bf16), heads[:, 256:384]) / total
        lse[part, :] = jnp.broadcast_to(top + jnp.log(total), (256, 128))

    loop(4, forward)
    for i in (0, 1):
        att[pl.ds(256 * i, 256), at(m, 128)] = attf[pl.ds(512 * i + 256 * c, 256), :].astype(bf16)
    att_copies = direct(att_view)
    up_pair = to_sibling(up_copies, up_own, up_cols)
    dk_acc[...] = jnp.zeros_like(dk_acc)
    dv_acc[...] = jnp.zeros_like(dv_acc)
    arrive(up_pair)

    def backward(i):
        part = at(i, 256)
        scores, visible = score_rows(i)
        probs = jnp.where(visible, jnp.exp(jnp.where(visible, scores, masked_score) - lse[part, 0:1]), 0.0)
        up = heads[part, 384:512]
        delta = jnp.sum(up.astype(f32) * attf[part, :], axis=-1, keepdims=True)
        grads = (probs * (contract_cols(up, heads[:, 256:384]) - delta)).astype(bf16)
        dv_acc[...] += contract_rows(probs.astype(bf16), up)
        dk_acc[...] += contract_rows(grads, heads[part, 0:128])

        @pl.when(i % 2 == c)
        def _():
            here = at(i // 2, 256)
            back = dot(grads, heads[:, 128:256]) * scale
            pack[here, at(3 * m, 128)] = turned(back, cosr[here, :], -sinr[here, :]).astype(bf16)

    loop(4, backward)
    for i in (0, 1):
        part, here = pl.ds(512 * i + 256 * c, 256), pl.ds(256 * i, 256)
        key_back = turned(dk_acc[part, :] * scale, cosr[here, :], -sinr[here, :])
        pack[here, at(3 * m + 1, 128)] = key_back.astype(bf16)
        pack[here, at(3 * m + 2, 128)] = dv_acc[part, :].astype(bf16)
    pack_copies = direct(pack_view)
    g_relays = relay(g_copies, cg_half)
    att_relays = relay(att_copies, att_half)
    arrive(x_relays + x_rest)
    norm(flip4(m, 2), False)
    norm(flip4(m, 3), False)
    feed(1 - x)
    pack_relays = relay(pack_copies, pack_half)
    wd_load.wait()

    def feed_out(n):
        acco[n] = contract_cols(act[mine, :], wd[at(n, 256), :])

    loop(8, feed_out)
    arrive(att_relays)

    def finish_out(n):
        ob[n % 4, n // 4] = (acco[n] + contract_cols(att[mine, :], wo[at(n, 256), :])).astype(bf16)

    loop(8, finish_out)

    def scatter(src, dst):
        copies = [send(src.at[flip4(t, k)], dst.at[t], grid_peer(k)) for k in (1, 3, 2)]
        return copies, move(src.at[t], dst.at[t])

    def across(copies, kept, src, which):
        arrive(copies)
        kept.wait()
        sums = [sum(src[i, half].astype(f32) for i in range(4)) for half in (0, 1)]
        keep = jnp.where(b == 0, sums[0], sums[1])
        swap_b[which] = jnp.where(b == 0, sums[1], sums[0]).astype(bf16)
        return keep, send(swap_b.at[which], back_b.at[which], grid_peer(4))

    out_copies, out_own = scatter(ob, ro)
    arrive(g_relays)

    def hidden(n):
        cols = at(n, 256)
        low = (dot(cg[...], wd[:, cols]) * gd[:, cols].astype(f32)).astype(bf16)
        hid[:, cols] = low

    loop(8, hidden)

    def norm_grad(n, values, weight, which):
        cols = at(n, 256)
        ng = contract_cols(values, weight[cols, :])
        usum[which : which + 1, cols] = jnp.sum(ng * xh[:, cols], axis=0, keepdims=True)
        usum[which + 2 : which + 3, cols] = jnp.sum(ng, axis=0, keepdims=True)
        return ng * rows2[which, 0:1, cols]

    def feed_grad(n):
        cols = at(n, 256)
        accg[n] = norm_grad(n, hid[mine, :], wu, 1)
        usum[6:7, cols] = jnp.sum(hid[mine, cols].astype(f32), axis=0, keepdims=True)
        usum[4:5, cols] = jnp.sum(cg[mine, cols].astype(f32), axis=0, keepdims=True)

    loop(8, feed_grad)
    arrive(pack_relays)

    def attention_grad(n):
        accg[n] += norm_grad(n, pack[mine, :], wp, 0)

    loop(8, attention_grad)
    usum[5:6, 0:1536] = jnp.sum(pack[mine, :].astype(f32), axis=0, keepdims=True)
    pair_copy = send(usum, pair, sibling())
    zero = jnp.zeros((128, 1), f32)

    def means(n, carry):
        g = accg[n]
        return (carry[0] + jnp.sum(g, axis=-1, keepdims=True),
                carry[1] + jnp.sum(g * xh[:, at(n, 256)], axis=-1, keepdims=True))

    mean, slope = lax.fori_loop(0, 8, means, (zero, zero))
    mean, slope = mean * (1.0 / 2048), slope * (1.0 / 2048)

    def finish_grad(n):
        gb[n % 4, n // 4] = (inv_s[mine, 0:1] * (accg[n] - mean - xh[:, at(n, 256)] * slope)).astype(bf16)

    loop(8, finish_grad)
    grad_copies, grad_own = scatter(gb, rg)

    def transpose_slices(i):
        part = at(i, 128)
        for half in (0, 1):
            cols = pl.ds(256 * half, 256)
            features = at(4 * x + 2 * half + b, 256)
            hat = (xg[part, features].astype(f32) - mean_s[part, 0:1]) * inv_s[part, 0:1]
            for which, dst in ((0, n0t), (1, n1t)):
                low = hat * rows2[which, 0:1, features] + rows2[which, 1:2, features]
                dst[cols, part] = low.T.astype(bf16)
            ct[cols, part] = cg[part, features].astype(f32).T.astype(bf16)

    loop(4, transpose_slices)
    arrive([pair_copy])
    pair[...] += usum[...]
    near_copies = [send(pair, near.at[k - 1], plane_peer(k)) for k in (1, 2, 3)]
    writes = []

    def matrix(lhs, rhs, count, out, base):
        for copy in writes[-1:]:
            for part in copy:
                part.wait()
        first = used["sem"]
        used["sem"] += count

        def swap(i):
            return pltpu.make_async_remote_copy(
                src_ref=other.at[base + i], dst_ref=recv.at[base + i],
                send_sem=sems.at[0, first + i], recv_sem=sems.at[1, first + i],
                device_id=sibling(), device_id_type=MESH)

        def produce(i):
            right = rhs[:, at(i, 512)]
            other[base + i] = dot(lhs[at(1 - c, 256), :], right).astype(bf16)
            swap(i).start()
            own[i] = dot(lhs[at(c, 256), :], right)

        loop(count, produce)
        done = []
        for i in range(count):
            swap(i).wait_recv()
            low_own[i] = (own[i] + recv[base + i].astype(f32)).astype(bf16)
            done.append(move(low_own.at[i], out.at[:, pl.ds(512 * i, 512)]))
            sent.append(swap(i))
        writes.append(done)

    matrix(ct, act, 4, down_o, 0)
    arrive(near_copies)
    sums_o[t] = pair[...] + near[0] + near[1] + near[2]
    sum_copies = [send(sums_o.at[t], sums_o.at[t], grid_peer(k)) for k in (1, 2, 3)]
    out_keep, out_swap = across(out_copies, out_own, ro, 0)
    matrix(n1t, hid, 4, up_o, 4)
    matrix(ct, att, 1, output_o, 8)
    matrix(n0t, pack, 3, project_o, 9)
    columns = at(j, 256)
    bias = rows2[0, 2:3, columns] + rows2[1, 2:3, columns]
    here, there = at(b, 128), at(1 - b, 128)
    layer_o[here, :] = (bias + tok[here, :].astype(f32) + out_keep).astype(bf16)
    arrive([out_swap])
    layer_o[there, :] = (bias + tok[there, :].astype(f32) + back_b[0].astype(f32)).astype(bf16)
    grad_keep, grad_swap = across(grad_copies, grad_own, rg, 1)
    grad_o[here, :] = cot[here, :].astype(f32) + grad_keep
    arrive(sum_copies + [grad_swap])
    grad_o[there, :] = cot[there, :].astype(f32) + back_b[1].astype(f32)
    for part in writes[-1]:
        part.wait()
    for copy in sent:
        copy.wait_send()
    assert used["sem"] <= 100 and used["local"] <= 40, used


def emit_kernel(layer, grad, project, output, up, down, sums, layer_o, grad_o, project_o, output_o,
                up_o, down_o, offs_o, hidden_o, gain_o, center_o, residual_o):
    project_o[...] = project[...].astype(f32)
    output_o[...] = output[...].astype(f32)
    up_o[...] = up[...].astype(f32)
    down_o[...] = down[...].astype(f32)

    @pl.when(pl.program_id(0) == 0)
    def _():
        layer_o[...] = layer[...]
        grad_o[...] = grad[...]
        gain_o[...] = sums[0, 0:2] + sums[1, 0:2] + sums[2, 0:2] + sums[3, 0:2]
        center_o[...] = sums[0, 2:4] + sums[1, 2:4] + sums[2, 2:4] + sums[3, 2:4]
        residual_o[...] = jnp.broadcast_to(sums[0, 4:5], (2, 2048))
        for i in range(4):
            offs_o[pl.ds(1536 * i, 1536)] = sums[i, 5, 0:1536]
            hidden_o[pl.ds(2048 * i, 2048)] = sums[i, 6]


def fast_device(tokens, cotangent, documents, positions, project_weight, offsets, output_weight,
                up_weight, hidden_bias, down_weight, norm_gain, norm_bias, residual_bias):
    half = ROT // 2
    frequency = rope_base ** (-(2.0 * jnp.arange(half, dtype=f32)) / ROT)
    waves = jnp.broadcast_to(jnp.concatenate([frequency, frequency])[:, None], (ROT, 256))
    vmem, anywhere = pl.BlockSpec(memory_space=pltpu.VMEM), pl.BlockSpec(memory_space=pl.ANY)
    shape = jax.ShapeDtypeStruct
    low = lambda *size: pltpu.VMEM(size, bf16)
    full = lambda *size: pltpu.VMEM(size, f32)
    widths = (1536, 512, 2048, 2048)
    results = pl.pallas_call(
        layer_kernel,
        out_shape=[shape((256, 256), bf16), shape((256, 256), f32)]
        + [shape((256, width), bf16) for width in widths] + [shape((4, 8, 2048), f32)],
        in_specs=[vmem] * 9 + [anywhere] * 4,
        out_specs=[vmem] * 2 + [anywhere] * 4 + [vmem],
        scratch_shapes=[
            low(2048, 1536), low(2048, 512), low(2048, 2048), low(2048, 2048),
            low(512, 2048), low(512, 2048), full(4, 8, 256), full(1024, 128), full(512, 128),
            full(512, 128), full(2, 8, 2048), full(128, 2048), full(512, 128), full(512, 128),
            low(128, 2048), low(256, 2048), GD(512, 2048), low(512, 2048), low(512, 2048),
            low(4, 128, 512), low(1024, 512), low(512, 512), low(512, 1536), full(1024, 128),
            full(1024, 128), full(1024, 128), full(1024, 128), low(4, 2, 128, 256),
            low(4, 2, 128, 256), low(4, 2, 128, 256), low(4, 2, 128, 256), low(2, 128, 256),
            low(2, 128, 256), full(8, 128, 256), full(8, 128, 256), low(512, 512), low(512, 512),
            low(512, 512), full(4, 256, 512), low(4, 256, 512), low(12, 256, 512),
            low(12, 256, 512), full(8, 2048), full(8, 2048), full(3, 8, 2048),
            pltpu.SemaphoreType.DMA((2, 100)), pltpu.SemaphoreType.DMA((40,))],
        compiler_params=pltpu.CompilerParams(
            collective_id=0, has_side_effects=True, vmem_limit_bytes=LIMIT),
    )(tokens, cotangent, positions[None], waves, norm_gain, norm_bias, residual_bias,
      offsets[None], hidden_bias[None], project_weight, output_weight, up_weight, down_weight)
    steps = 4
    whole = lambda *size: pl.BlockSpec(size, lambda i: (0,) * len(size))
    band = lambda width: pl.BlockSpec((256 // steps, width), lambda i: (i, 0))
    layer_out, input_grad, *rest = pl.pallas_call(
        emit_kernel,
        grid=(steps,),
        out_shape=[shape((256, 256), bf16), shape((256, 256), f32)]
        + [shape((256, width), f32) for width in widths]
        + [shape((6144,), f32), shape((8192,), f32)] + [shape((2, 2048), f32)] * 3,
        in_specs=[whole(256, 256)] * 2 + [band(width) for width in widths] + [whole(4, 8, 2048)],
        out_specs=[whole(256, 256)] * 2 + [band(width) for width in widths]
        + [whole(6144), whole(8192)] + [whole(2, 2048)] * 3,
        compiler_params=pltpu.CompilerParams(vmem_limit_bytes=32 << 20),
    )(*results)
    return (layer_out, input_grad, *rest)


LIMIT = 63 << 20
GD = lambda *size: pltpu.VMEM(size, bf16)


def solution(mesh):
    fits = (mesh.shape["seq"], mesh.shape["branch"], mesh.shape["tensor"]) == (4, 2, 4)
    return jax.shard_map(
        fast_device if fits else on_device,
        mesh=mesh,
        in_specs=(
            P("seq", ("branch", "tensor")),
            P("seq", ("branch", "tensor")),
            P("seq"),
            P("seq"),
            P(None, "tensor"),
            P("tensor"),
            P(None, "tensor"),
            P(None, "tensor"),
            P("tensor"),
            P(None, "tensor"),
            P("branch", None),
            P("branch", None),
            P("branch", None),
        ),
        out_specs=(
            P("seq", ("branch", "tensor")),
            P("seq", ("branch", "tensor")),
            P(("seq", "branch"), "tensor"),
            P(("seq", "branch"), "tensor"),
            P(("seq", "branch"), "tensor"),
            P(("seq", "branch"), "tensor"),
            P(),
            P(),
            P(),
            P(),
            P(),
        ),
        check_vma=False,
    )
```

```python
from functools import partial

import jax
import jax.numpy as jnp
from jax import lax
from jax.experimental import pallas as pl
from jax.experimental.pallas import tpu as pltpu
from jax.sharding import PartitionSpec as P

HEAD_DIM = 128
ROT = 32


norm_eps = 1e-05
rope_base = 10000.0
masked_score = -1e30


def passed_along(value, axis, steps):
    count = lax.axis_size(axis)
    pairs = [(source, (source + steps) % count) for source in range(count)]
    return lax.ppermute(value, axis, pairs)


def shifted(array, axis, by):
    count = lax.axis_size(axis)
    pairs = [(i, i + by) for i in range(count) if 0 <= i + by < count]
    return lax.ppermute(array, axis, pairs)


def layer_norm(values, gain_row, shift_row):
    average = jnp.mean(values, axis=-1, keepdims=True)
    centered = values - average
    variance = jnp.mean(centered * centered, axis=-1, keepdims=True)
    return centered * lax.rsqrt(variance + norm_eps) * gain_row + shift_row


def rope_tables(places):
    half_rot = ROT // 2
    frequency = rope_base ** (-(2.0 * jnp.arange(half_rot, dtype=jnp.float32)) / ROT)
    angles = places.astype(jnp.float32)[:, None] * frequency[None, :]
    return (jnp.cos(angles), jnp.sin(angles))


def rotate(values, cosine, sine_rows, direction):
    half_rot = ROT // 2
    first_half = values[..., :half_rot]
    second_half = values[..., half_rot:ROT]
    cos_table = cosine[:, None, :]
    sin_table = direction * sine_rows[:, None, :]
    return jnp.concatenate(
        [
            first_half * cos_table - second_half * sin_table,
            second_half * cos_table + first_half * sin_table,
            values[..., ROT:],
        ],
        axis=-1,
    )


def contract_rows(first_side, second_side):
    return lax.dot_general(
        first_side, second_side, (((0,), (0,)), ((), ())), preferred_element_type=jnp.float32
    )


def contract_cols(first_side, second_side):
    return lax.dot_general(
        first_side, second_side, (((1,), (1,)), ((), ())), preferred_element_type=jnp.float32
    )


def on_device(
    tokens,
    cotangent,
    documents,
    positions,
    project_weight,
    offsets,
    output_weight,
    up_weight,
    hidden_bias,
    down_weight,
    norm_gain,
    norm_bias,
    residual_bias,
):
    tok_rows = tokens.shape[0]
    model_width = up_weight.shape[0]
    attn_width = output_weight.shape[1]
    local_heads = attn_width // HEAD_DIM
    hidden_local = up_weight.shape[1]
    seq_count = lax.axis_size("seq")
    seq_index = lax.axis_index("seq")
    branch_index = lax.axis_index("branch")
    tensor_index = lax.axis_index("tensor")
    is_attention = branch_index == 0
    lead_tensor = tensor_index == 0
    score_scale = HEAD_DIM ** (-0.5)
    local_index = jnp.arange(tok_rows, dtype=jnp.int32)
    query_index = seq_index * tok_rows + local_index
    full_tokens, full_cotangent = (
        lax.all_gather(tokens, ("branch", "tensor"), axis=1, tiled=True),
        lax.all_gather(cotangent, ("branch", "tensor"), axis=1, tiled=True),
    )
    gain_row = norm_gain[0]
    shift_row = norm_bias[0]
    normed, norm_pullback = jax.vjp(
        layer_norm, full_tokens.astype(jnp.float32), gain_row, shift_row
    )
    normed_low = normed.astype(jnp.bfloat16)
    cosine, sine_rows = rope_tables(positions)
    zeros_heads = jnp.zeros((tok_rows, attn_width), jnp.bfloat16)
    zeros_hidden = jnp.zeros((tok_rows, hidden_local), jnp.float32)
    hidden_zero = jnp.zeros((tok_rows, hidden_local), jnp.bfloat16)
    zeros_stats = jnp.zeros((local_heads, tok_rows), jnp.float32)
    grad_zero = jnp.zeros((tok_rows, local_heads, HEAD_DIM), jnp.float32)

    def attention_front(unused):
        packed = jnp.dot(normed_low, project_weight, preferred_element_type=jnp.float32) + offsets
        packed = packed.reshape(tok_rows, local_heads, 3, HEAD_DIM)
        query_rot = rotate(packed[:, :, 0], cosine, sine_rows, 1.0).reshape(tok_rows, attn_width)
        key_rot = rotate(packed[:, :, 1], cosine, sine_rows, 1.0).reshape(tok_rows, attn_width)
        value_rows = packed[:, :, 2].reshape(tok_rows, attn_width)
        return (
            query_rot.astype(jnp.bfloat16),
            key_rot.astype(jnp.bfloat16),
            value_rows.astype(jnp.bfloat16),
            zeros_hidden,
            hidden_zero,
        )

    def feed_front(unused):
        up_rows = jnp.dot(normed_low, up_weight, preferred_element_type=jnp.float32) + hidden_bias
        active = jax.nn.gelu(up_rows, approximate=False).astype(jnp.bfloat16)
        return (zeros_heads, zeros_heads, zeros_heads, up_rows, active)

    query_low, key_low, value_low, up_rows, active = lax.cond(
        is_attention, attention_front, feed_front, 0
    )
    query_heads = query_low.reshape(tok_rows, local_heads, HEAD_DIM)

    def absorb(totals, key_rows, value_rows, key_ids, offset):
        key_count = key_rows.shape[0]
        key_index = offset + jnp.arange(key_count, dtype=jnp.int32)
        visible = (documents[:, None] == key_ids[None, :]) & (
            key_index[None, :] <= query_index[:, None]
        )

        def update(running):
            run_max, run_sum, run_acc = running
            scores = (
                jnp.einsum(
                    "qhd,khd->hqk",
                    query_heads,
                    key_rows.reshape(key_count, local_heads, HEAD_DIM),
                    preferred_element_type=jnp.float32,
                )
                * score_scale
            )
            masked = jnp.where(visible[None], scores, masked_score)
            new_max = jnp.maximum(run_max, jnp.max(masked, axis=-1))
            weights = jnp.where(visible[None], jnp.exp(masked - new_max[:, :, None]), 0.0)
            factor = jnp.exp(run_max - new_max)
            blended = jnp.einsum(
                "hqk,khd->qhd",
                weights.astype(jnp.bfloat16),
                value_rows.reshape(key_count, local_heads, HEAD_DIM),
                preferred_element_type=jnp.float32,
            )
            return (
                new_max,
                run_sum * factor + jnp.sum(weights, axis=-1),
                run_acc * factor.T[:, :, None] + blended,
            )

        def unchanged(running):
            return running

        return lax.cond(is_attention & jnp.any(visible), update, unchanged, totals)

    initial = (jnp.full((local_heads, tok_rows), masked_score, jnp.float32), zeros_stats, grad_zero)
    totals = initial
    key_rows = lax.all_gather(key_low, "seq", axis=0, tiled=True)
    value_rows = lax.all_gather(value_low, "seq", axis=0, tiled=True)
    key_ids = lax.all_gather(documents, "seq", axis=0, tiled=True)
    key_count = key_rows.shape[0]
    groups = key_count // tok_rows

    def absorb_group(running, sliced):
        return (absorb(running, sliced[0], sliced[1], sliced[2], sliced[3]), None)

    starts = tok_rows * jnp.arange(groups, dtype=jnp.int32)
    stacked = (
        key_rows.reshape(groups, tok_rows, attn_width),
        value_rows.reshape(groups, tok_rows, attn_width),
        key_ids.reshape(groups, tok_rows),
        starts,
    )
    totals, unused = lax.scan(absorb_group, totals, stacked)
    run_max, run_sum, run_acc = totals

    def attention_out(unused):
        attended = run_acc / run_sum.T[:, :, None]
        attended_low = attended.reshape(tok_rows, attn_width).astype(jnp.bfloat16)
        return (
            contract_cols(attended_low, output_weight),
            attended,
            attended_low,
            run_max + jnp.log(run_sum),
        )

    def feed_out(unused):
        return (contract_cols(active, down_weight), grad_zero, zeros_heads, zeros_stats)

    branch_out, attended, attended_low, lse_rows = lax.cond(
        is_attention, attention_out, feed_out, 0
    )
    branch_out = branch_out + jnp.where(lead_tensor, residual_bias[0], 0.0)
    summed = lax.psum_scatter(
        branch_out.astype(jnp.bfloat16), ("branch", "tensor"), scatter_dimension=1, tiled=True
    ).astype(jnp.float32)
    layer_out = (tokens.astype(jnp.float32) + summed).astype(jnp.bfloat16)

    def attention_prep(unused):
        grad_low = jnp.dot(
            full_cotangent, output_weight, preferred_element_type=jnp.float32
        ).astype(jnp.bfloat16)
        delta_rows = jnp.sum(
            grad_low.reshape(tok_rows, local_heads, HEAD_DIM).astype(jnp.float32) * attended,
            axis=-1,
        ).T
        return (grad_low, delta_rows, hidden_zero)

    def feed_prep(unused):
        active_grad = jnp.dot(full_cotangent, down_weight, preferred_element_type=jnp.float32)
        gelu_value, gelu_pullback = jax.vjp(partial(jax.nn.gelu, approximate=False), up_rows)
        return (zeros_heads, zeros_stats, gelu_pullback(active_grad)[0].astype(jnp.bfloat16))

    grad_low, delta_rows, hidden_low = lax.cond(is_attention, attention_prep, feed_prep, 0)

    def block_grads(
        query_rows,
        grad_rows,
        query_lse,
        query_delta,
        query_ids,
        query_place,
        key_rows,
        value_rows,
        key_ids,
        key_place,
    ):
        visible = (query_ids[:, None] == key_ids[None, :]) & (
            key_place[None, :] <= query_place[:, None]
        )

        def compute(unused):
            query_part_heads = query_rows.reshape(tok_rows, local_heads, HEAD_DIM)
            grad_heads = grad_rows.reshape(tok_rows, local_heads, HEAD_DIM)
            key_heads = key_rows.reshape(tok_rows, local_heads, HEAD_DIM)
            value_heads = value_rows.reshape(tok_rows, local_heads, HEAD_DIM)
            scores = (
                jnp.einsum(
                    "qhd,khd->hqk", query_part_heads, key_heads, preferred_element_type=jnp.float32
                )
                * score_scale
            )
            weights = jnp.exp(
                jnp.where(visible[None], scores - query_lse[:, :, None], masked_score)
            )
            value_part = jnp.einsum(
                "hqk,qhd->khd",
                weights.astype(jnp.bfloat16),
                grad_heads,
                preferred_element_type=jnp.float32,
            )
            weight_grad = jnp.einsum(
                "qhd,khd->hqk", grad_heads, value_heads, preferred_element_type=jnp.float32
            )
            score_grad = (weights * (weight_grad - query_delta[:, :, None])).astype(jnp.bfloat16)
            query_part = (
                jnp.einsum(
                    "hqk,khd->qhd", score_grad, key_heads, preferred_element_type=jnp.float32
                )
                * score_scale
            )
            key_part = (
                jnp.einsum(
                    "hqk,qhd->khd", score_grad, query_part_heads, preferred_element_type=jnp.float32
                )
                * score_scale
            )
            return (query_part, key_part, value_part)

        def nothing(unused):
            return (grad_zero, grad_zero, grad_zero)

        return lax.cond(is_attention & jnp.any(visible), compute, nothing, 0)

    def send_grads(key_acc, value_acc):
        return (
            passed_along(key_acc.astype(jnp.bfloat16), "seq", 1).astype(key_acc.dtype),
            passed_along(value_acc.astype(jnp.bfloat16), "seq", 1).astype(value_acc.dtype),
        )

    def key_step(cycle_state, unused):
        key_rows, value_rows, key_ids, key_acc, value_acc, hop_count, query_acc = cycle_state
        source = (seq_index - hop_count) % seq_count
        partial_terms = block_grads(
            query_low,
            grad_low,
            lse_rows,
            delta_rows,
            documents,
            query_index,
            key_rows,
            value_rows,
            key_ids,
            source * tok_rows + local_index,
        )
        key_rows, value_rows, key_ids = shifted((key_rows, value_rows, key_ids), "seq", 1)
        key_acc, value_acc = send_grads(key_acc + partial_terms[1], value_acc + partial_terms[2])
        return (
            (
                key_rows,
                value_rows,
                key_ids,
                key_acc,
                value_acc,
                hop_count + 1,
                query_acc + partial_terms[0],
            ),
            None,
        )

    start_state = (key_low, value_low, documents, grad_zero, grad_zero, jnp.int32(0), grad_zero)
    cycle_state, unused = lax.scan(key_step, start_state, None, length=seq_count - 1)
    key_rows, value_rows, key_ids, key_acc, value_acc, hop_count, query_acc = cycle_state
    source = (seq_index - hop_count) % seq_count
    partial_terms = block_grads(
        query_low,
        grad_low,
        lse_rows,
        delta_rows,
        documents,
        query_index,
        key_rows,
        value_rows,
        key_ids,
        source * tok_rows + local_index,
    )
    key_grad, value_grad = send_grads(key_acc + partial_terms[1], value_acc + partial_terms[2])
    query_grad = query_acc + partial_terms[0]

    def attention_tail(unused):
        query_back = rotate(query_grad, cosine, sine_rows, -1.0)
        key_back = rotate(key_grad, cosine, sine_rows, -1.0)
        packed_grad = (
            jnp.stack([query_back, key_back, value_grad], axis=2)
            .reshape(tok_rows, 3 * attn_width)
            .astype(jnp.bfloat16)
        )
        return (contract_cols(packed_grad, project_weight), packed_grad)

    def feed_tail(unused):
        return (
            contract_cols(hidden_low, up_weight),
            jnp.zeros((tok_rows, 3 * attn_width), jnp.bfloat16),
        )

    norm_grad, packed_grad = lax.cond(is_attention, attention_tail, feed_tail, 0)
    input_part, gain_part, shift_part = norm_pullback(norm_grad)
    input_grad = lax.psum_scatter(
        input_part.astype(jnp.bfloat16), ("branch", "tensor"), scatter_dimension=1, tiled=True
    ).astype(jnp.float32) + cotangent.astype(jnp.float32)

    def attention_rows(unused):
        return jnp.concatenate(
            [
                contract_rows(normed_low, packed_grad),
                contract_rows(full_cotangent, attended_low),
                jnp.zeros(
                    (
                        model_width
                        // (seq_count * lax.axis_size("branch"))
                        * lax.axis_size(("seq", "branch")),
                        2 * hidden_local,
                    ),
                    jnp.float32,
                ),
            ],
            axis=1,
        )

    def feed_rows(unused):
        return jnp.concatenate(
            [
                jnp.zeros(
                    (
                        model_width
                        // (seq_count * lax.axis_size("branch"))
                        * lax.axis_size(("seq", "branch")),
                        4 * attn_width,
                    ),
                    jnp.float32,
                ),
                contract_rows(normed_low, hidden_low),
                contract_rows(full_cotangent, active),
            ],
            axis=1,
        )

    shares = lax.psum_scatter(
        lax.cond(is_attention, attention_rows, feed_rows, 0).astype(jnp.bfloat16),
        ("seq", "branch"),
        scatter_dimension=0,
        tiled=True,
    ).astype(jnp.float32)
    project_grad = shares[:, : 3 * attn_width]
    output_grad = shares[:, 3 * attn_width : 4 * attn_width]
    up_grad = shares[:, 4 * attn_width : 4 * attn_width + hidden_local]
    down_grad = shares[:, 4 * attn_width + hidden_local :]
    offsets_part = lax.dynamic_update_slice(
        jnp.zeros((3 * model_width,), jnp.float32),
        jnp.sum(packed_grad, axis=0, dtype=jnp.float32),
        (tensor_index * (3 * attn_width),),
    )
    hidden_part = lax.dynamic_update_slice(
        jnp.zeros((hidden_local * lax.axis_size("tensor"),), jnp.float32),
        jnp.sum(hidden_low, axis=0, dtype=jnp.float32),
        (tensor_index * hidden_local,),
    )
    pair_zero = jnp.zeros((2, model_width), jnp.float32)
    gain_rows = lax.dynamic_update_slice(
        pair_zero, gain_part[None, :], (branch_index, jnp.int32(0))
    )
    shift_rows = lax.dynamic_update_slice(
        pair_zero, shift_part[None, :], (branch_index, jnp.int32(0))
    )
    column_sums = jnp.where(lead_tensor, jnp.sum(full_cotangent, axis=0, dtype=jnp.float32), 0.0)
    residual_rows = lax.dynamic_update_slice(
        pair_zero, column_sums[None, :], (branch_index, jnp.int32(0))
    )
    offsets_grad, hidden_grad, gain_grad, center_grad, residual_grad = lax.psum(
        (offsets_part, hidden_part, gain_rows, shift_rows, residual_rows),
        ("seq", "branch", "tensor"),
    )
    return (
        layer_out,
        input_grad,
        project_grad,
        output_grad,
        up_grad,
        down_grad,
        offsets_grad,
        hidden_grad,
        gain_grad,
        center_grad,
        residual_grad,
    )


MESH = pl.DeviceIdType.MESH
bf16, f32 = jnp.bfloat16, jnp.float32


def place():
    s, b, t = lax.axis_index("seq"), lax.axis_index("branch"), lax.axis_index("tensor")
    return s, b, t, s // 2, s % 2


def flip(value, bit):
    return value + bit - 2 * bit * value


def flip4(value, k):
    return 2 * flip(value // 2, k // 2) + flip(value % 2, k % 2)


def plane_peer(k):
    s, b, t, x, c = place()
    return (2 * flip(x, k // 2) + c, flip(b, k % 2), t)


def grid_peer(k):
    s, b, t, x, c = place()
    return (s, flip(b, k // 4), flip4(t, k % 4))


def sibling():
    s, b, t, x, c = place()
    return (flip4(s, 1), b, t)


def meet(devices):
    barrier = pltpu.get_barrier_semaphore()
    for device in devices:
        pl.semaphore_signal(barrier, inc=1, device_id=device, device_id_type=MESH)
    pl.semaphore_wait(barrier, len(devices))


def at(index, size):
    return pl.ds(pl.multiple_of(index * size, size), size)


def dot(first, second):
    return jnp.dot(first, second, preferred_element_type=f32)


def turned(values, cosine, sines):
    lane = lax.broadcasted_iota(jnp.int32, values.shape, 1)
    swapped = jnp.where(
        lane < ROT // 2,
        pltpu.roll(values, HEAD_DIM - ROT // 2, 1),
        pltpu.roll(values, ROT // 2, 1),
    )
    return values * cosine + sines * swapped


def layer_kernel(
    tok, cot, places_h, gain_h, shift_h, residual_h, offs_h, hbias_h, wp_h, wo_h, wu_h, wd_h,
    layer_o, grad_o, project_o, output_o, up_o, down_o, sums_o,
    wp, wo, wu, wd, tok_v, cot_v, places, gain, shift, residual, offs, hbias, xg, cg, posr, starts, cosr, sinr, rows2, xh, mean_s, inv_s, n0, n1, gd, act, hid,
    hs, heads, att, pack, attf, lse, dk_acc, dv_acc, ob, ro, gb, rg, swap_b, back_b, accg,
    n0t, n1t, ct, other, recv, usum, pair, near, sems, local,
):
    s, b, t, x, c = place()
    m, j = 2 * x + b, 4 * b + t
    slot = 4 * x + 2 * c + b
    scale = HEAD_DIM ** -0.5
    mine = at(m, 128)
    used = {"sem": 0, "local": 0}
    sent, inner_sent = [], []
    inner = (t == 1) | (t == 2)

    def describe(src, dst, device, there=None):
        index = used["sem"]
        used["sem"] += 1
        return pltpu.make_async_remote_copy(
            src_ref=src, dst_ref=dst, send_sem=sems.at[0, index],
            recv_sem=sems.at[1, index if there is None else there],
            device_id=device, device_id_type=MESH)

    def send(src, dst, device):
        copy = describe(src, dst, device)
        copy.start()
        sent.append(copy)
        return copy

    def send_inner(src, dst, device, there=None):
        copy = describe(src, dst, device, there)
        pl.when(inner)(copy.start)
        inner_sent.append(copy)
        return copy

    def move(src, dst):
        index = used["local"]
        used["local"] += 1
        copy = pltpu.make_async_copy(src, dst, local.at[index])
        copy.start()
        return copy

    def arrive(copies):
        for copy in copies:
            copy.wait_recv()

    def direct(view):
        return [send(view(m), view(m), plane_peer(k)) for k in (2, 1)]

    def relay(copies, half):
        out = []
        for i, k in enumerate((2, 1)):
            copies[i].wait_recv()
            part = half(flip4(m, k), i)
            out.append(send(part, part, plane_peer(3 - k)))
        return out

    def loop(count, body):
        def step(i, carry):
            body(i)
            return carry
        lax.fori_loop(0, count, step, 0)

    def block(k):
        return at(4 * flip(b, k // 4) + flip4(t, k % 4), 256)

    def gather(src, dst):
        over = send(src.at[at(1 - b, 128)], dst.at[at(flip4(m, 1), 128), at(j, 256)], grid_peer(4))
        half = src.at[at(b, 128)]
        near = to_tensor(half, dst.at[mine, at(j, 256)])
        return {"over": over, "near": near, "own": move(half, dst.at[mine, at(j, 256)]), "dst": dst,
                "plane": {}}

    def to_tensor(src, dst):
        last = used["sem"]
        third = send_inner(src, dst, grid_peer(3))
        return {2: send(src, dst, grid_peer(2)), 1: send(src, dst, grid_peer(1)), 3: third, "last": last}

    def on_plane(state, k):
        part = state["dst"].at[mine, block(k)]
        state["plane"][k] = [send(part, part, plane_peer(i)) for i in (2, 1)]

    def gather_over(state):
        state["own"].wait()
        state["over"].wait_recv()
        part = state["dst"].at[mine, block(4)]
        state["far"] = to_tensor(part, part)

    def gather_step(state, k):
        for which, first in (("near", 0), ("far", 4)):
            state[which][k].wait_recv()
            if k == 2:
                part = state["dst"].at[mine, block(first + 2)]
                send_inner(part, part, grid_peer(1), state[which]["last"])

    def both_on_plane(state, k):
        on_plane(state, k)
        on_plane(state, k + 4)

    def plane_relay(state, k, here=False):
        dst, plane = state["dst"], state["plane"]
        plane[k][0].wait_recv()
        part = dst.at[at(flip4(m, 2), 128), block(k)]
        first = send(part, part, plane_peer(1))
        if not here:
            plane[k + 4][1].wait_recv()
        part = dst.at[at(flip4(m, 1), 128), block(k)]
        return [first, send(part, part, plane_peer(2)), plane[k + 4][0]]

    meet([grid_peer(k) for k in (1, 2, 3, 4)] + [plane_peer(2), plane_peer(3)]
         + [(flip4(s, k), b, t) for k in (1, 3)])
    x_state = gather(tok, xg)
    small = [move(src, dst) for src, dst in (
        (places_h, places), (gain_h, gain), (shift_h, shift), (residual_h, residual),
        (offs_h, offs), (hbias_h, hbias))]
    wp_load, wu_load = move(wp_h, wp), move(wu_h, wu)
    wo_load, wd_load = move(wo_h, wo), move(wd_h, wd)
    late = [move(tok, tok_v), move(cot, cot_v)]
    for copy in small:
        copy.wait()
    rows2[b] = jnp.zeros((8, 2048), f32)
    rows2[b, 0:1, :] = gain[...]
    rows2[b, 1:2, :] = shift[...]
    rows2[b, 2:3, :] = residual[...]
    posr[s] = jnp.broadcast_to(places[...].astype(f32)[None, :], (8, 256))
    row_copy = send(rows2.at[b], rows2.at[b], grid_peer(4))
    place_copies = [send(posr.at[s], posr.at[s], (flip4(s, k), b, t)) for k in (1, 2, 3)]
    gather_over(x_state)
    both_on_plane(x_state, 0)
    usum[...] = jnp.zeros_like(usum)
    dk_acc[...] = jnp.zeros_like(dk_acc)
    dv_acc[...] = jnp.zeros_like(dv_acc)
    arrive(place_copies)
    for i in range(4):
        row = jnp.broadcast_to(posr[i, 0:1, :], (128, 256))
        index = (256 * i + lax.broadcasted_iota(jnp.int32, (256, 128), 0)).astype(f32)
        starts[pl.ds(256 * i, 256), :] = index - row.T
    line = lax.broadcasted_iota(jnp.int32, (ROT, 256), 0)
    waves = jnp.zeros((ROT, 256), f32)
    for i in range(ROT // 2):
        waves = jnp.where(line % (ROT // 2) == i, rope_base ** (-2.0 * i / ROT), waves)
    for i in (0, 1):
        angle = posr[2 * i + c, 0:1, :] * waves
        part = pl.ds(256 * i, 256)
        sign = jnp.where(line < ROT // 2, -1.0, 1.0)
        rest = jnp.zeros((HEAD_DIM - ROT, 256), f32)
        cosr[part, :] = jnp.concatenate([jnp.cos(angle), rest + 1.0], axis=0).T
        sinr[part, :] = jnp.concatenate([jnp.sin(angle) * sign, rest], axis=0).T
    for k in (1, 2, 3):
        gather_step(x_state, k)
        both_on_plane(x_state, k)
    g_state = gather(cot, cg)
    arrive([row_copy])

    def norm(which, whole):
        def rows(i):
            part = pl.ds(pl.multiple_of(which * 128 + 16 * i, 16), 16)
            v = xg[part, :].astype(f32)
            mean = jnp.mean(v, axis=-1, keepdims=True)
            centered = v - mean
            inverse = lax.rsqrt(jnp.mean(centered * centered, axis=-1, keepdims=True) + norm_eps)
            hat = centered * inverse
            mean_s[part, :] = jnp.broadcast_to(mean, (16, 128))
            inv_s[part, :] = jnp.broadcast_to(inverse, (16, 128))
            n1_part = pl.ds(pl.multiple_of((which % 2) * 128 + 16 * i, 16), 16)
            n1[n1_part, :] = (hat * rows2[1, 0:1, :] + rows2[1, 1:2, :]).astype(bf16)
            if whole:
                xh[at(i, 16), :] = hat
                n0[at(i, 16), :] = (hat * rows2[0, 0:1, :] + rows2[0, 1:2, :]).astype(bf16)

        loop(8, rows)

    norm(m, True)
    gather_over(g_state)
    x_relays = []
    for k in (0, 1, 2):
        x_relays += plane_relay(x_state, k)
    wp_load.wait()
    turn = pl.ds(pl.multiple_of(256 * x + 128 * b, 128), 128)

    def project(h):
        p = dot(n0[...], wp[:, at(h, 384)]) + offs[at(h, 384)][None, :]
        hs[h, :, 0:128] = turned(p[:, 0:128], cosr[turn, :], sinr[turn, :]).astype(bf16)
        hs[h, :, 128:256] = turned(p[:, 128:256], cosr[turn, :], sinr[turn, :]).astype(bf16)
        hs[h, :, 256:384] = p[:, 256:384].astype(bf16)

    loop(4, project)

    def to_heads(cols):
        copies = [send(hs.at[flip4(m, k), :, cols], heads.at[at(slot, 128), cols], plane_peer(k))
                  for k in (3, 2, 1)]
        return copies, move(hs.at[m, :, cols], heads.at[at(slot, 128), cols])

    def to_sibling(copies, kept, cols):
        arrive(copies)
        kept.wait()
        parts = [heads.at[pl.ds(512 * i + 256 * c, 256), cols] for i in (0, 1)]
        return [send(part, part, sibling()) for part in parts]

    qkv_cols, up_cols = pl.ds(0, 384), pl.ds(384, 128)
    qkv_copies, qkv_own = to_heads(qkv_cols)
    x_relays += plane_relay(x_state, 3)
    gather_step(g_state, 1)
    arrive([x_state["plane"][k][1] for k in range(4)])
    norm(flip4(m, 1), False)
    wu_load.wait()

    def feed(pair_index, first, count):
        rows = at(pair_index, 256)

        def tile(n):
            cols = at(first + n, 512)
            u = dot(n1[...], wu[:, cols]) + hbias[cols][None, :]
            phi = 0.5 + 0.5 * lax.erf(u * 0.7071067811865476)
            act[rows, cols] = (u * phi).astype(bf16)
            gd[rows, cols] = (phi + u * (0.3989422804014327 * jnp.exp(-0.5 * u * u))).astype(gd.dtype)

        loop(count, tile)

    feed(x, 0, 2)
    gather_step(g_state, 2)
    feed(x, 2, 2)
    qkv_pair = to_sibling(qkv_copies, qkv_own, qkv_cols)
    att_view = lambda i: att.at[:, at(i, 128)]
    att_half = lambda i, h: att.at[pl.ds(256 * h, 256), at(i, 128)]
    pack_view = lambda i: pack.at[:, at(i, 384)]
    pack_half = lambda i, h: pack.at[pl.ds(256 * h, 256), at(i, 384)]

    def score_rows(i):
        width = 256 * (i + 1)
        part = pl.ds(256 * i, 256)
        scores = contract_cols(heads[part, 0:128], heads[0:width, 128:256]) * scale
        query = (256 * i + lax.broadcasted_iota(jnp.int32, (256, 1), 0)).astype(f32)
        key = lax.broadcasted_iota(jnp.int32, (256, width), 1).astype(f32)
        visible = (key <= query) & (key >= starts[part, 0:1])
        return part, width, jnp.where(visible, scores, masked_score), visible

    gather_step(g_state, 3)
    wo_load.wait()

    head_low = dot(cg[mine, :], wo[...]).astype(bf16)
    for h in range(4):
        hs[h, :, 384:512] = head_low[:, 128 * h : 128 * (h + 1)]
    up_copies, up_own = to_heads(up_cols)
    for k in range(4):
        both_on_plane(g_state, k)
    arrive(qkv_pair)
    for i in range(4):
        part, width, masked, visible = score_rows(i)
        top = jnp.max(masked, axis=-1, keepdims=True)
        weights = jnp.where(visible, jnp.exp(masked - top), 0.0)
        total = jnp.sum(weights, axis=-1, keepdims=True)
        attf[part, :] = dot(weights.astype(bf16), heads[0:width, 256:384]) / total
        lse[part, :] = jnp.broadcast_to(top + jnp.log(total), (256, 128))

    for i in (0, 1):
        att[pl.ds(256 * i, 256), at(m, 128)] = attf[pl.ds(512 * i + 256 * c, 256), :].astype(bf16)
    att_copies = direct(att_view)
    arrive(x_relays)
    norm(flip4(m, 2), False)
    up_pair = to_sibling(up_copies, up_own, up_cols)
    norm(flip4(m, 3), False)
    wd_load.wait()

    def feed_out(n):
        accg[:, at(n, 1024)] = contract_cols(act[mine, :], wd[at(n, 1024), :])

    loop(2, feed_out)
    att_relays = relay(att_copies, att_half)
    arrive(up_pair)

    for i in range(4):
        part, width, masked, visible = score_rows(i)
        probs = jnp.where(visible, jnp.exp(masked - lse[part, 0:1]), 0.0)
        up = heads[part, 384:512]
        delta = jnp.sum(up.astype(f32) * attf[part, :], axis=-1, keepdims=True)
        grads = (probs * (contract_cols(up, heads[0:width, 256:384]) - delta)).astype(bf16)
        dv_acc[0:width, :] += contract_rows(probs.astype(bf16), up)
        dk_acc[0:width, :] += contract_rows(grads, heads[part, 0:128])

        @pl.when(i % 2 == c)
        def _():
            here = pl.ds(256 * (i // 2), 256)
            back = dot(grads, heads[0:width, 128:256]) * scale
            pack[here, at(3 * m, 128)] = turned(back, cosr[here, :], -sinr[here, :]).astype(bf16)

    for i in (0, 1):
        part, here = pl.ds(512 * i + 256 * c, 256), pl.ds(256 * i, 256)
        key_back = turned(dk_acc[part, :] * scale, cosr[here, :], -sinr[here, :])
        pack[here, at(3 * m + 1, 128)] = key_back.astype(bf16)
        pack[here, at(3 * m + 2, 128)] = dv_acc[part, :].astype(bf16)
    pack_copies = direct(pack_view)
    arrive(att_relays)

    def finish_out(n):
        total = accg[:, at(n, 1024)] + contract_cols(att[mine, :], wo[at(n, 1024), :])
        for i in range(4):
            ob[i, n] = total[:, 256 * i : 256 * (i + 1)].astype(bf16)

    loop(2, finish_out)

    def scatter(src, dst):
        copies = [send(src.at[flip4(t, k)], dst.at[t], grid_peer(k)) for k in (3, 2, 1)]
        return copies, move(src.at[t], dst.at[t])

    def across(copies, kept, src, which):
        arrive(copies)
        kept.wait()
        sums = [sum(src[i, half].astype(f32) for i in range(4)) for half in (0, 1)]
        keep = jnp.where(b == 0, sums[0], sums[1])
        swap_b[which] = jnp.where(b == 0, sums[1], sums[0]).astype(bf16)
        return keep, send(swap_b.at[which], back_b.at[which], grid_peer(4))

    out_copies, out_own = scatter(ob, ro)

    def hidden(pair_index):
        rows = at(pair_index, 256)

        def tile(n):
            cols = at(n, 512)
            hid[rows, cols] = (dot(cg[rows, :], wd[:, cols]) * gd[rows, cols].astype(f32)).astype(bf16)

        loop(4, tile)

    arrive([g_state["plane"][k][1] for k in range(8)])
    hidden(x)
    feed(1 - x, 0, 4)
    pack_relays = relay(pack_copies, pack_half)
    g_relays = []
    for k in range(4):
        g_relays += plane_relay(g_state, k, True)

    def norm_grad(n, values, weight, which):
        cols = at(n, 512)
        ng = contract_cols(values, weight[cols, :])
        usum[which : which + 1, cols] = jnp.sum(ng * xh[:, cols], axis=0, keepdims=True)
        usum[which + 2 : which + 3, cols] = jnp.sum(ng, axis=0, keepdims=True)
        return ng * rows2[which, 0:1, cols]

    def feed_grad(n):
        cols = at(n, 512)
        accg[:, cols] = norm_grad(n, hid[mine, :], wu, 1)
        usum[6:7, cols] = jnp.sum(hid[mine, cols].astype(f32), axis=0, keepdims=True)
        usum[4:5, cols] = jnp.sum(cg[mine, cols].astype(f32), axis=0, keepdims=True)

    loop(4, feed_grad)
    arrive(pack_relays)

    def attention_grad(n):
        accg[:, at(n, 512)] += norm_grad(n, pack[mine, :], wp, 0)

    loop(4, attention_grad)
    usum[5:6, 0:1536] = jnp.sum(pack[mine, :].astype(f32), axis=0, keepdims=True)
    pair_copy = send(usum, pair, sibling())
    zero = jnp.zeros((128, 1), f32)

    def means(n, carry):
        g = accg[:, at(n, 256)]
        return (carry[0] + jnp.sum(g, axis=-1, keepdims=True),
                carry[1] + jnp.sum(g * xh[:, at(n, 256)], axis=-1, keepdims=True))

    mean, slope = lax.fori_loop(0, 8, means, (zero, zero))
    mean, slope = mean * (1.0 / 2048), slope * (1.0 / 2048)

    def finish_grad(n):
        gb[n % 4, n // 4] = (inv_s[mine, 0:1] * (accg[:, at(n, 256)] - mean - xh[:, at(n, 256)] * slope)).astype(bf16)

    loop(8, finish_grad)
    grad_copies, grad_own = scatter(gb, rg)
    arrive(g_relays)
    hidden(1 - x)

    def transpose_slices(i):
        part = at(i, 128)
        for half in (0, 1):
            cols = pl.ds(256 * half, 256)
            features = at(4 * x + 2 * half + b, 256)
            hat = (xg[part, features].astype(f32) - mean_s[part, 0:1]) * inv_s[part, 0:1]
            for which, dst in ((0, n0t), (1, n1t)):
                low = hat * rows2[which, 0:1, features] + rows2[which, 1:2, features]
                dst[cols, part] = low.T.astype(bf16)
            ct[cols, part] = cg[part, features].astype(f32).T.astype(bf16)

    loop(4, transpose_slices)
    arrive([pair_copy])
    pair[...] += usum[...]
    near_copies = [send(pair, near.at[k - 1], plane_peer(k)) for k in (1, 2, 3)]
    writes = []

    def matrix(lhs, rhs, count, out, base):
        first = used["sem"]
        used["sem"] += count

        def swap(i):
            return pltpu.make_async_remote_copy(
                src_ref=other.at[base + i], dst_ref=recv.at[base + i],
                send_sem=sems.at[0, first + i], recv_sem=sems.at[1, first + i],
                device_id=sibling(), device_id_type=MESH)

        def produce(i):
            right = rhs[:, at(i, 512)]
            other[base + i] = dot(lhs[at(1 - c, 256), :], right).astype(bf16)
            swap(i).start()
            kept = dot(lhs[at(c, 256), :], right)
            xh[:, at(i, 512)] = kept[:128]
            accg[:, at(i, 512)] = kept[128:]

        loop(count, produce)
        for i in range(count):
            swap(i).wait_recv()
            for part, kept in ((pl.ds(0, 128), xh), (pl.ds(128, 128), accg)):
                total = kept[:, pl.ds(512 * i, 512)] + recv[base + i, part, :].astype(f32)
                recv[base + i, part, :] = total.astype(bf16)
            writes.append(move(recv.at[base + i], out.at[:, pl.ds(512 * i, 512)]))
            sent.append(swap(i))

    matrix(ct, act, 4, down_o, 0)
    arrive(near_copies)
    sums_o[t] = pair[...] + near[0] + near[1] + near[2]
    sum_copies = [send(sums_o.at[t], sums_o.at[t], grid_peer(k)) for k in (1, 2, 3)]
    out_keep, out_swap = across(out_copies, out_own, ro, 0)
    matrix(n1t, hid, 4, up_o, 4)
    matrix(ct, att, 1, output_o, 8)
    matrix(n0t, pack, 3, project_o, 9)
    for copy in late:
        copy.wait()
    columns = at(j, 256)
    bias = rows2[0, 2:3, columns] + rows2[1, 2:3, columns]
    here, there = at(b, 128), at(1 - b, 128)
    layer_o[here, :] = (bias + tok_v[here, :].astype(f32) + out_keep).astype(bf16)
    arrive([out_swap])
    layer_o[there, :] = (bias + tok_v[there, :].astype(f32) + back_b[0].astype(f32)).astype(bf16)
    grad_keep, grad_swap = across(grad_copies, grad_own, rg, 1)
    grad_o[here, :] = cot_v[here, :].astype(f32) + grad_keep
    arrive(sum_copies + [grad_swap])
    grad_o[there, :] = cot_v[there, :].astype(f32) + back_b[1].astype(f32)
    for copy in writes:
        copy.wait()
    for copy in sent:
        copy.wait_send()
    for copy in inner_sent:
        pl.when(inner)(copy.wait_send)
    assert used["sem"] <= 150 and used["local"] <= 40, used


def emit_kernel(layer, grad, project, output, up, down, sums, layer_o, grad_o, project_o, output_o,
                up_o, down_o, offs_o, hidden_o, gain_o, center_o, residual_o):
    project_o[...] = project[...].astype(f32)
    output_o[...] = output[...].astype(f32)
    up_o[...] = up[...].astype(f32)
    down_o[...] = down[...].astype(f32)

    @pl.when(pl.program_id(0) == 0)
    def _():
        layer_o[...] = layer[...]
        grad_o[...] = grad[...]
        gain_o[...] = sums[0, 0:2] + sums[1, 0:2] + sums[2, 0:2] + sums[3, 0:2]
        center_o[...] = sums[0, 2:4] + sums[1, 2:4] + sums[2, 2:4] + sums[3, 2:4]
        residual_o[...] = jnp.broadcast_to(sums[0, 4:5], (2, 2048))
        for i in range(4):
            offs_o[pl.ds(1536 * i, 1536)] = sums[i, 5, 0:1536]
            hidden_o[pl.ds(2048 * i, 2048)] = sums[i, 6]


def fast_device(tokens, cotangent, documents, positions, project_weight, offsets, output_weight,
                up_weight, hidden_bias, down_weight, norm_gain, norm_bias, residual_bias):
    vmem, anywhere = pl.BlockSpec(memory_space=pltpu.VMEM), pl.BlockSpec(memory_space=pl.ANY)
    shape = jax.ShapeDtypeStruct
    low = lambda *size: pltpu.VMEM(size, bf16)
    full = lambda *size: pltpu.VMEM(size, f32)
    widths = (1536, 512, 2048, 2048)
    results = pl.pallas_call(
        layer_kernel,
        out_shape=[shape((256, 256), bf16), shape((256, 256), f32)]
        + [shape((256, width), bf16) for width in widths] + [shape((4, 8, 2048), f32)],
        in_specs=[anywhere] * 12,
        out_specs=[vmem] * 2 + [anywhere] * 4 + [vmem],
        scratch_shapes=[
            low(2048, 1536), low(2048, 512), low(2048, 2048), low(2048, 2048),
            low(256, 256), low(256, 256), pltpu.VMEM((256,), jnp.int32), full(1, 2048), full(1, 2048),
            full(1, 2048), full(1536), full(2048),
            low(512, 2048), low(512, 2048), full(4, 8, 256), full(1024, 128), full(512, 128),
            full(512, 128), full(2, 8, 2048), full(128, 2048), full(512, 128), full(512, 128),
            low(128, 2048), low(256, 2048), GD(512, 2048), low(512, 2048), low(512, 2048),
            low(4, 128, 512), low(1024, 512), low(512, 512), low(512, 1536), full(1024, 128),
            full(1024, 128), full(1024, 128), full(1024, 128), low(4, 2, 128, 256),
            low(4, 2, 128, 256), low(4, 2, 128, 256), low(4, 2, 128, 256), low(2, 128, 256),
            low(2, 128, 256), full(128, 2048), low(512, 512), low(512, 512),
            low(512, 512), low(12, 256, 512),
            low(12, 256, 512), full(8, 2048), full(8, 2048), full(3, 8, 2048),
            pltpu.SemaphoreType.DMA((2, 150)), pltpu.SemaphoreType.DMA((40,))],
        compiler_params=pltpu.CompilerParams(
            collective_id=0, has_side_effects=True, vmem_limit_bytes=LIMIT),
    )(tokens, cotangent, positions, norm_gain, norm_bias, residual_bias,
      offsets, hidden_bias, project_weight, output_weight, up_weight, down_weight)
    steps = 2
    whole = lambda *size: pl.BlockSpec(size, lambda i: (0,) * len(size))
    band = lambda width: pl.BlockSpec((256 // steps, width), lambda i: (i, 0))
    layer_out, input_grad, *rest = pl.pallas_call(
        emit_kernel,
        grid=(steps,),
        out_shape=[shape((256, 256), bf16), shape((256, 256), f32)]
        + [shape((256, width), f32) for width in widths]
        + [shape((6144,), f32), shape((8192,), f32)] + [shape((2, 2048), f32)] * 3,
        in_specs=[whole(256, 256)] * 2 + [band(width) for width in widths] + [whole(4, 8, 2048)],
        out_specs=[whole(256, 256)] * 2 + [band(width) for width in widths]
        + [whole(6144), whole(8192)] + [whole(2, 2048)] * 3,
        compiler_params=pltpu.CompilerParams(vmem_limit_bytes=LIMIT),
    )(*results)
    return (layer_out, input_grad, *rest)


LIMIT = 63 << 20
GD = lambda *size: pltpu.VMEM(size, bf16)


def solution(mesh):
    fits = (mesh.shape["seq"], mesh.shape["branch"], mesh.shape["tensor"]) == (4, 2, 4)
    return jax.shard_map(
        fast_device if fits else on_device,
        mesh=mesh,
        in_specs=(
            P("seq", ("branch", "tensor")),
            P("seq", ("branch", "tensor")),
            P("seq"),
            P("seq"),
            P(None, "tensor"),
            P("tensor"),
            P(None, "tensor"),
            P(None, "tensor"),
            P("tensor"),
            P(None, "tensor"),
            P("branch", None),
            P("branch", None),
            P("branch", None),
        ),
        out_specs=(
            P("seq", ("branch", "tensor")),
            P("seq", ("branch", "tensor")),
            P(("seq", "branch"), "tensor"),
            P(("seq", "branch"), "tensor"),
            P(("seq", "branch"), "tensor"),
            P(("seq", "branch"), "tensor"),
            P(),
            P(),
            P(),
            P(),
            P(),
        ),
        check_vma=False,
    )
```

```python
from functools import partial

import jax
import jax.numpy as jnp
from jax import lax
from jax.experimental import pallas as pl
from jax.experimental.pallas import tpu as pltpu
from jax.sharding import PartitionSpec as P

HEAD_DIM = 128
ROT = 32


norm_eps = 1e-05
rope_base = 10000.0
masked_score = -1e30


def passed_along(value, axis, steps):
    count = lax.axis_size(axis)
    pairs = [(source, (source + steps) % count) for source in range(count)]
    return lax.ppermute(value, axis, pairs)


def shifted(array, axis, by):
    count = lax.axis_size(axis)
    pairs = [(i, i + by) for i in range(count) if 0 <= i + by < count]
    return lax.ppermute(array, axis, pairs)


def layer_norm(values, gain_row, shift_row):
    average = jnp.mean(values, axis=-1, keepdims=True)
    centered = values - average
    variance = jnp.mean(centered * centered, axis=-1, keepdims=True)
    return centered * lax.rsqrt(variance + norm_eps) * gain_row + shift_row


def rope_tables(places):
    half_rot = ROT // 2
    frequency = rope_base ** (-(2.0 * jnp.arange(half_rot, dtype=jnp.float32)) / ROT)
    angles = places.astype(jnp.float32)[:, None] * frequency[None, :]
    return (jnp.cos(angles), jnp.sin(angles))


def rotate(values, cosine, sine_rows, direction):
    half_rot = ROT // 2
    first_half = values[..., :half_rot]
    second_half = values[..., half_rot:ROT]
    cos_table = cosine[:, None, :]
    sin_table = direction * sine_rows[:, None, :]
    return jnp.concatenate(
        [
            first_half * cos_table - second_half * sin_table,
            second_half * cos_table + first_half * sin_table,
            values[..., ROT:],
        ],
        axis=-1,
    )


def contract_rows(first_side, second_side):
    return lax.dot_general(
        first_side, second_side, (((0,), (0,)), ((), ())), preferred_element_type=jnp.float32
    )


def contract_cols(first_side, second_side):
    return lax.dot_general(
        first_side, second_side, (((1,), (1,)), ((), ())), preferred_element_type=jnp.float32
    )


def on_device(
    tokens,
    cotangent,
    documents,
    positions,
    project_weight,
    offsets,
    output_weight,
    up_weight,
    hidden_bias,
    down_weight,
    norm_gain,
    norm_bias,
    residual_bias,
):
    tok_rows = tokens.shape[0]
    model_width = up_weight.shape[0]
    attn_width = output_weight.shape[1]
    local_heads = attn_width // HEAD_DIM
    hidden_local = up_weight.shape[1]
    seq_count = lax.axis_size("seq")
    seq_index = lax.axis_index("seq")
    branch_index = lax.axis_index("branch")
    tensor_index = lax.axis_index("tensor")
    is_attention = branch_index == 0
    lead_tensor = tensor_index == 0
    score_scale = HEAD_DIM ** (-0.5)
    local_index = jnp.arange(tok_rows, dtype=jnp.int32)
    query_index = seq_index * tok_rows + local_index
    full_tokens, full_cotangent = (
        lax.all_gather(tokens, ("branch", "tensor"), axis=1, tiled=True),
        lax.all_gather(cotangent, ("branch", "tensor"), axis=1, tiled=True),
    )
    gain_row = norm_gain[0]
    shift_row = norm_bias[0]
    normed, norm_pullback = jax.vjp(
        layer_norm, full_tokens.astype(jnp.float32), gain_row, shift_row
    )
    normed_low = normed.astype(jnp.bfloat16)
    cosine, sine_rows = rope_tables(positions)
    zeros_heads = jnp.zeros((tok_rows, attn_width), jnp.bfloat16)
    zeros_hidden = jnp.zeros((tok_rows, hidden_local), jnp.float32)
    hidden_zero = jnp.zeros((tok_rows, hidden_local), jnp.bfloat16)
    zeros_stats = jnp.zeros((local_heads, tok_rows), jnp.float32)
    grad_zero = jnp.zeros((tok_rows, local_heads, HEAD_DIM), jnp.float32)

    def attention_front(unused):
        packed = jnp.dot(normed_low, project_weight, preferred_element_type=jnp.float32) + offsets
        packed = packed.reshape(tok_rows, local_heads, 3, HEAD_DIM)
        query_rot = rotate(packed[:, :, 0], cosine, sine_rows, 1.0).reshape(tok_rows, attn_width)
        key_rot = rotate(packed[:, :, 1], cosine, sine_rows, 1.0).reshape(tok_rows, attn_width)
        value_rows = packed[:, :, 2].reshape(tok_rows, attn_width)
        return (
            query_rot.astype(jnp.bfloat16),
            key_rot.astype(jnp.bfloat16),
            value_rows.astype(jnp.bfloat16),
            zeros_hidden,
            hidden_zero,
        )

    def feed_front(unused):
        up_rows = jnp.dot(normed_low, up_weight, preferred_element_type=jnp.float32) + hidden_bias
        active = jax.nn.gelu(up_rows, approximate=False).astype(jnp.bfloat16)
        return (zeros_heads, zeros_heads, zeros_heads, up_rows, active)

    query_low, key_low, value_low, up_rows, active = lax.cond(
        is_attention, attention_front, feed_front, 0
    )
    query_heads = query_low.reshape(tok_rows, local_heads, HEAD_DIM)

    def absorb(totals, key_rows, value_rows, key_ids, offset):
        key_count = key_rows.shape[0]
        key_index = offset + jnp.arange(key_count, dtype=jnp.int32)
        visible = (documents[:, None] == key_ids[None, :]) & (
            key_index[None, :] <= query_index[:, None]
        )

        def update(running):
            run_max, run_sum, run_acc = running
            scores = (
                jnp.einsum(
                    "qhd,khd->hqk",
                    query_heads,
                    key_rows.reshape(key_count, local_heads, HEAD_DIM),
                    preferred_element_type=jnp.float32,
                )
                * score_scale
            )
            masked = jnp.where(visible[None], scores, masked_score)
            new_max = jnp.maximum(run_max, jnp.max(masked, axis=-1))
            weights = jnp.where(visible[None], jnp.exp(masked - new_max[:, :, None]), 0.0)
            factor = jnp.exp(run_max - new_max)
            blended = jnp.einsum(
                "hqk,khd->qhd",
                weights.astype(jnp.bfloat16),
                value_rows.reshape(key_count, local_heads, HEAD_DIM),
                preferred_element_type=jnp.float32,
            )
            return (
                new_max,
                run_sum * factor + jnp.sum(weights, axis=-1),
                run_acc * factor.T[:, :, None] + blended,
            )

        def unchanged(running):
            return running

        return lax.cond(is_attention & jnp.any(visible), update, unchanged, totals)

    initial = (jnp.full((local_heads, tok_rows), masked_score, jnp.float32), zeros_stats, grad_zero)
    totals = initial
    key_rows = lax.all_gather(key_low, "seq", axis=0, tiled=True)
    value_rows = lax.all_gather(value_low, "seq", axis=0, tiled=True)
    key_ids = lax.all_gather(documents, "seq", axis=0, tiled=True)
    key_count = key_rows.shape[0]
    groups = key_count // tok_rows

    def absorb_group(running, sliced):
        return (absorb(running, sliced[0], sliced[1], sliced[2], sliced[3]), None)

    starts = tok_rows * jnp.arange(groups, dtype=jnp.int32)
    stacked = (
        key_rows.reshape(groups, tok_rows, attn_width),
        value_rows.reshape(groups, tok_rows, attn_width),
        key_ids.reshape(groups, tok_rows),
        starts,
    )
    totals, unused = lax.scan(absorb_group, totals, stacked)
    run_max, run_sum, run_acc = totals

    def attention_out(unused):
        attended = run_acc / run_sum.T[:, :, None]
        attended_low = attended.reshape(tok_rows, attn_width).astype(jnp.bfloat16)
        return (
            contract_cols(attended_low, output_weight),
            attended,
            attended_low,
            run_max + jnp.log(run_sum),
        )

    def feed_out(unused):
        return (contract_cols(active, down_weight), grad_zero, zeros_heads, zeros_stats)

    branch_out, attended, attended_low, lse_rows = lax.cond(
        is_attention, attention_out, feed_out, 0
    )
    branch_out = branch_out + jnp.where(lead_tensor, residual_bias[0], 0.0)
    summed = lax.psum_scatter(
        branch_out.astype(jnp.bfloat16), ("branch", "tensor"), scatter_dimension=1, tiled=True
    ).astype(jnp.float32)
    layer_out = (tokens.astype(jnp.float32) + summed).astype(jnp.bfloat16)

    def attention_prep(unused):
        grad_low = jnp.dot(
            full_cotangent, output_weight, preferred_element_type=jnp.float32
        ).astype(jnp.bfloat16)
        delta_rows = jnp.sum(
            grad_low.reshape(tok_rows, local_heads, HEAD_DIM).astype(jnp.float32) * attended,
            axis=-1,
        ).T
        return (grad_low, delta_rows, hidden_zero)

    def feed_prep(unused):
        active_grad = jnp.dot(full_cotangent, down_weight, preferred_element_type=jnp.float32)
        gelu_value, gelu_pullback = jax.vjp(partial(jax.nn.gelu, approximate=False), up_rows)
        return (zeros_heads, zeros_stats, gelu_pullback(active_grad)[0].astype(jnp.bfloat16))

    grad_low, delta_rows, hidden_low = lax.cond(is_attention, attention_prep, feed_prep, 0)

    def block_grads(
        query_rows,
        grad_rows,
        query_lse,
        query_delta,
        query_ids,
        query_place,
        key_rows,
        value_rows,
        key_ids,
        key_place,
    ):
        visible = (query_ids[:, None] == key_ids[None, :]) & (
            key_place[None, :] <= query_place[:, None]
        )

        def compute(unused):
            query_part_heads = query_rows.reshape(tok_rows, local_heads, HEAD_DIM)
            grad_heads = grad_rows.reshape(tok_rows, local_heads, HEAD_DIM)
            key_heads = key_rows.reshape(tok_rows, local_heads, HEAD_DIM)
            value_heads = value_rows.reshape(tok_rows, local_heads, HEAD_DIM)
            scores = (
                jnp.einsum(
                    "qhd,khd->hqk", query_part_heads, key_heads, preferred_element_type=jnp.float32
                )
                * score_scale
            )
            weights = jnp.exp(
                jnp.where(visible[None], scores - query_lse[:, :, None], masked_score)
            )
            value_part = jnp.einsum(
                "hqk,qhd->khd",
                weights.astype(jnp.bfloat16),
                grad_heads,
                preferred_element_type=jnp.float32,
            )
            weight_grad = jnp.einsum(
                "qhd,khd->hqk", grad_heads, value_heads, preferred_element_type=jnp.float32
            )
            score_grad = (weights * (weight_grad - query_delta[:, :, None])).astype(jnp.bfloat16)
            query_part = (
                jnp.einsum(
                    "hqk,khd->qhd", score_grad, key_heads, preferred_element_type=jnp.float32
                )
                * score_scale
            )
            key_part = (
                jnp.einsum(
                    "hqk,qhd->khd", score_grad, query_part_heads, preferred_element_type=jnp.float32
                )
                * score_scale
            )
            return (query_part, key_part, value_part)

        def nothing(unused):
            return (grad_zero, grad_zero, grad_zero)

        return lax.cond(is_attention & jnp.any(visible), compute, nothing, 0)

    def send_grads(key_acc, value_acc):
        return (
            passed_along(key_acc.astype(jnp.bfloat16), "seq", 1).astype(key_acc.dtype),
            passed_along(value_acc.astype(jnp.bfloat16), "seq", 1).astype(value_acc.dtype),
        )

    def key_step(cycle_state, unused):
        key_rows, value_rows, key_ids, key_acc, value_acc, hop_count, query_acc = cycle_state
        source = (seq_index - hop_count) % seq_count
        partial_terms = block_grads(
            query_low,
            grad_low,
            lse_rows,
            delta_rows,
            documents,
            query_index,
            key_rows,
            value_rows,
            key_ids,
            source * tok_rows + local_index,
        )
        key_rows, value_rows, key_ids = shifted((key_rows, value_rows, key_ids), "seq", 1)
        key_acc, value_acc = send_grads(key_acc + partial_terms[1], value_acc + partial_terms[2])
        return (
            (
                key_rows,
                value_rows,
                key_ids,
                key_acc,
                value_acc,
                hop_count + 1,
                query_acc + partial_terms[0],
            ),
            None,
        )

    start_state = (key_low, value_low, documents, grad_zero, grad_zero, jnp.int32(0), grad_zero)
    cycle_state, unused = lax.scan(key_step, start_state, None, length=seq_count - 1)
    key_rows, value_rows, key_ids, key_acc, value_acc, hop_count, query_acc = cycle_state
    source = (seq_index - hop_count) % seq_count
    partial_terms = block_grads(
        query_low,
        grad_low,
        lse_rows,
        delta_rows,
        documents,
        query_index,
        key_rows,
        value_rows,
        key_ids,
        source * tok_rows + local_index,
    )
    key_grad, value_grad = send_grads(key_acc + partial_terms[1], value_acc + partial_terms[2])
    query_grad = query_acc + partial_terms[0]

    def attention_tail(unused):
        query_back = rotate(query_grad, cosine, sine_rows, -1.0)
        key_back = rotate(key_grad, cosine, sine_rows, -1.0)
        packed_grad = (
            jnp.stack([query_back, key_back, value_grad], axis=2)
            .reshape(tok_rows, 3 * attn_width)
            .astype(jnp.bfloat16)
        )
        return (contract_cols(packed_grad, project_weight), packed_grad)

    def feed_tail(unused):
        return (
            contract_cols(hidden_low, up_weight),
            jnp.zeros((tok_rows, 3 * attn_width), jnp.bfloat16),
        )

    norm_grad, packed_grad = lax.cond(is_attention, attention_tail, feed_tail, 0)
    input_part, gain_part, shift_part = norm_pullback(norm_grad)
    input_grad = lax.psum_scatter(
        input_part.astype(jnp.bfloat16), ("branch", "tensor"), scatter_dimension=1, tiled=True
    ).astype(jnp.float32) + cotangent.astype(jnp.float32)

    def attention_rows(unused):
        return jnp.concatenate(
            [
                contract_rows(normed_low, packed_grad),
                contract_rows(full_cotangent, attended_low),
                jnp.zeros(
                    (
                        model_width
                        // (seq_count * lax.axis_size("branch"))
                        * lax.axis_size(("seq", "branch")),
                        2 * hidden_local,
                    ),
                    jnp.float32,
                ),
            ],
            axis=1,
        )

    def feed_rows(unused):
        return jnp.concatenate(
            [
                jnp.zeros(
                    (
                        model_width
                        // (seq_count * lax.axis_size("branch"))
                        * lax.axis_size(("seq", "branch")),
                        4 * attn_width,
                    ),
                    jnp.float32,
                ),
                contract_rows(normed_low, hidden_low),
                contract_rows(full_cotangent, active),
            ],
            axis=1,
        )

    shares = lax.psum_scatter(
        lax.cond(is_attention, attention_rows, feed_rows, 0).astype(jnp.bfloat16),
        ("seq", "branch"),
        scatter_dimension=0,
        tiled=True,
    ).astype(jnp.float32)
    project_grad = shares[:, : 3 * attn_width]
    output_grad = shares[:, 3 * attn_width : 4 * attn_width]
    up_grad = shares[:, 4 * attn_width : 4 * attn_width + hidden_local]
    down_grad = shares[:, 4 * attn_width + hidden_local :]
    offsets_part = lax.dynamic_update_slice(
        jnp.zeros((3 * model_width,), jnp.float32),
        jnp.sum(packed_grad, axis=0, dtype=jnp.float32),
        (tensor_index * (3 * attn_width),),
    )
    hidden_part = lax.dynamic_update_slice(
        jnp.zeros((hidden_local * lax.axis_size("tensor"),), jnp.float32),
        jnp.sum(hidden_low, axis=0, dtype=jnp.float32),
        (tensor_index * hidden_local,),
    )
    pair_zero = jnp.zeros((2, model_width), jnp.float32)
    gain_rows = lax.dynamic_update_slice(
        pair_zero, gain_part[None, :], (branch_index, jnp.int32(0))
    )
    shift_rows = lax.dynamic_update_slice(
        pair_zero, shift_part[None, :], (branch_index, jnp.int32(0))
    )
    column_sums = jnp.where(lead_tensor, jnp.sum(full_cotangent, axis=0, dtype=jnp.float32), 0.0)
    residual_rows = lax.dynamic_update_slice(
        pair_zero, column_sums[None, :], (branch_index, jnp.int32(0))
    )
    offsets_grad, hidden_grad, gain_grad, center_grad, residual_grad = lax.psum(
        (offsets_part, hidden_part, gain_rows, shift_rows, residual_rows),
        ("seq", "branch", "tensor"),
    )
    return (
        layer_out,
        input_grad,
        project_grad,
        output_grad,
        up_grad,
        down_grad,
        offsets_grad,
        hidden_grad,
        gain_grad,
        center_grad,
        residual_grad,
    )


MESH = pl.DeviceIdType.MESH
bf16, f32 = jnp.bfloat16, jnp.float32


def place():
    s, b, t = lax.axis_index("seq"), lax.axis_index("branch"), lax.axis_index("tensor")
    return s, b, t, s // 2, s % 2


def flip(value, bit):
    return value + bit - 2 * bit * value


def flip4(value, k):
    return 2 * flip(value // 2, k // 2) + flip(value % 2, k % 2)


def plane_peer(k):
    s, b, t, x, c = place()
    return (2 * flip(x, k // 2) + c, flip(b, k % 2), t)


def grid_peer(k):
    s, b, t, x, c = place()
    return (s, flip(b, k // 4), flip4(t, k % 4))


def sibling():
    s, b, t, x, c = place()
    return (flip4(s, 1), b, t)


def meet(devices):
    barrier = pltpu.get_barrier_semaphore()
    for device in devices:
        pl.semaphore_signal(barrier, inc=1, device_id=device, device_id_type=MESH)
    pl.semaphore_wait(barrier, len(devices))


def at(index, size):
    return pl.ds(pl.multiple_of(index * size, size), size)


def dot(first, second):
    return jnp.dot(first, second, preferred_element_type=f32)


def turned(values, cosine, sines):
    lane = lax.broadcasted_iota(jnp.int32, values.shape, 1)
    swapped = jnp.where(
        lane < ROT // 2,
        pltpu.roll(values, HEAD_DIM - ROT // 2, 1),
        pltpu.roll(values, ROT // 2, 1),
    )
    return values * cosine + sines * swapped


def layer_kernel(
    tok, cot, places_h, gain_h, shift_h, residual_h, offs_h, hbias_h, wp_h, wo_h, wu_h, wd_h,
    layer_o, grad_o, kept_o, came_o, sums_o,
    wp, wo, wu, wd, tok_v, cot_v, places, gain, shift, residual, offs, hbias, xg, cg, posr, starts, cosr, sinr, rows2, xh, mean_s, inv_s, n0, n1, gd, act, hid,
    hs, heads, att, pack, attf, lse, dk_acc, dv_acc, ob, ro, gb, rg, swap_b, back_b, accg,
    n0t, n1t, ct, other, kept, usum, pair, near, sems, local,
):
    s, b, t, x, c = place()
    m, j = 2 * x + b, 4 * b + t
    slot = 4 * x + 2 * c + b
    scale = HEAD_DIM ** -0.5
    mine = at(m, 128)
    used = {"sem": 0, "local": 0}
    sent, inner_sent = [], []
    inner = (t == 1) | (t == 2)

    def describe(src, dst, device, there=None):
        index = used["sem"]
        used["sem"] += 1
        return pltpu.make_async_remote_copy(
            src_ref=src, dst_ref=dst, send_sem=sems.at[0, index],
            recv_sem=sems.at[1, index if there is None else there],
            device_id=device, device_id_type=MESH)

    def send(src, dst, device):
        copy = describe(src, dst, device)
        copy.start()
        sent.append(copy)
        return copy

    def send_inner(src, dst, device, there=None):
        copy = describe(src, dst, device, there)
        pl.when(inner)(copy.start)
        inner_sent.append(copy)
        return copy

    def move(src, dst):
        index = used["local"]
        used["local"] += 1
        copy = pltpu.make_async_copy(src, dst, local.at[index])
        copy.start()
        return copy

    def arrive(copies):
        for copy in copies:
            copy.wait_recv()

    def direct(view):
        return [send(view(m), view(m), plane_peer(k)) for k in (2, 1)]

    def relay(copies, half):
        out = []
        for i, k in enumerate((2, 1)):
            copies[i].wait_recv()
            part = half(flip4(m, k), i)
            out.append(send(part, part, plane_peer(3 - k)))
        return out

    def loop(count, body):
        def step(i, carry):
            body(i)
            return carry
        lax.fori_loop(0, count, step, 0)

    def block(k):
        return at(4 * flip(b, k // 4) + flip4(t, k % 4), 256)

    def gather(src, dst):
        half, place = src.at[at(b, 128)], dst.at[mine, at(j, 256)]
        over = send(src.at[at(1 - b, 128)], dst.at[at(flip4(m, 1), 128), at(j, 256)], grid_peer(4))
        return {"over": over, "half": half, "place": place, "own": move(half, place), "dst": dst,
                "plane": {}}

    def gather_near(state):
        state["near"] = to_tensor(state["half"], state["place"])

    def to_tensor(src, dst):
        last = used["sem"]
        third = send_inner(src, dst, grid_peer(3))
        return {2: send(src, dst, grid_peer(2)), 1: send(src, dst, grid_peer(1)), 3: third, "last": last}

    def on_plane(state, k):
        part = state["dst"].at[mine, block(k)]
        state["plane"][k] = [send(part, part, plane_peer(i)) for i in (2, 1)]

    def gather_over(state):
        state["own"].wait()
        state["over"].wait_recv()
        part = state["dst"].at[mine, block(4)]
        state["far"] = to_tensor(part, part)

    def gather_step(state, k):
        for which, first in (("near", 0), ("far", 4)):
            state[which][k].wait_recv()
            if k == 2:
                part = state["dst"].at[mine, block(first + 2)]
                send_inner(part, part, grid_peer(1), state[which]["last"])

    def both_on_plane(state, k):
        on_plane(state, k)
        on_plane(state, k + 4)

    def plane_relay(state, k, here=False):
        dst, plane = state["dst"], state["plane"]
        plane[k][0].wait_recv()
        part = dst.at[at(flip4(m, 2), 128), block(k)]
        first = send(part, part, plane_peer(1))
        if not here:
            plane[k + 4][1].wait_recv()
        part = dst.at[at(flip4(m, 1), 128), block(k)]
        return [first, send(part, part, plane_peer(2)), plane[k + 4][0]]

    meet([grid_peer(k) for k in (1, 2, 3, 4)] + [plane_peer(2), plane_peer(3)]
         + [(flip4(s, k), b, t) for k in (1, 3)])
    x_state = gather(tok, xg)
    gather_near(x_state)
    g_state = gather(cot, cg)
    small = [move(src, dst) for src, dst in (
        (places_h, places), (gain_h, gain), (shift_h, shift), (residual_h, residual),
        (offs_h, offs), (hbias_h, hbias))]
    wp_load, wu_load = move(wp_h, wp), move(wu_h, wu)
    wo_load, wd_load = move(wo_h, wo), move(wd_h, wd)
    late = [move(tok, tok_v), move(cot, cot_v)]
    for copy in small:
        copy.wait()
    rows2[b] = jnp.zeros((8, 2048), f32)
    rows2[b, 0:1, :] = gain[...]
    rows2[b, 1:2, :] = shift[...]
    rows2[b, 2:3, :] = residual[...]
    posr[s] = jnp.broadcast_to(places[...].astype(f32)[None, :], (8, 256))
    row_copy = send(rows2.at[b], rows2.at[b], grid_peer(4))
    place_copies = [send(posr.at[s], posr.at[s], (flip4(s, k), b, t)) for k in (1, 2, 3)]
    gather_over(x_state)
    both_on_plane(x_state, 0)
    usum[...] = jnp.zeros_like(usum)
    dk_acc[...] = jnp.zeros_like(dk_acc)
    dv_acc[...] = jnp.zeros_like(dv_acc)
    arrive(place_copies)
    for i in range(4):
        row = jnp.broadcast_to(posr[i, 0:1, :], (128, 256))
        index = (256 * i + lax.broadcasted_iota(jnp.int32, (256, 128), 0)).astype(f32)
        starts[pl.ds(256 * i, 256), :] = index - row.T
    line = lax.broadcasted_iota(jnp.int32, (ROT, 256), 0)
    waves = jnp.zeros((ROT, 256), f32)
    for i in range(ROT // 2):
        waves = jnp.where(line % (ROT // 2) == i, rope_base ** (-2.0 * i / ROT), waves)
    for i in (0, 1):
        angle = posr[2 * i + c, 0:1, :] * waves
        part = pl.ds(256 * i, 256)
        sign = jnp.where(line < ROT // 2, -1.0, 1.0)
        rest = jnp.zeros((HEAD_DIM - ROT, 256), f32)
        cosr[part, :] = jnp.concatenate([jnp.cos(angle), rest + 1.0], axis=0).T
        sinr[part, :] = jnp.concatenate([jnp.sin(angle) * sign, rest], axis=0).T
    for k in (1, 2, 3):
        gather_step(x_state, k)
        both_on_plane(x_state, k)
        if k == 2:
            gather_near(g_state)
            gather_over(g_state)
    arrive([row_copy])

    def norm(which, whole):
        def rows(i):
            part = pl.ds(pl.multiple_of(which * 128 + 16 * i, 16), 16)
            v = xg[part, :].astype(f32)
            mean = jnp.mean(v, axis=-1, keepdims=True)
            centered = v - mean
            inverse = lax.rsqrt(jnp.mean(centered * centered, axis=-1, keepdims=True) + norm_eps)
            hat = centered * inverse
            mean_s[part, :] = jnp.broadcast_to(mean, (16, 128))
            inv_s[part, :] = jnp.broadcast_to(inverse, (16, 128))
            n1_part = pl.ds(pl.multiple_of((which % 2) * 128 + 16 * i, 16), 16)
            n1[n1_part, :] = (hat * rows2[1, 0:1, :] + rows2[1, 1:2, :]).astype(bf16)
            if whole:
                xh[at(i, 16), :] = hat
                n0[at(i, 16), :] = (hat * rows2[0, 0:1, :] + rows2[0, 1:2, :]).astype(bf16)

        loop(8, rows)

    norm(m, True)
    x_relays = []
    for k in (0, 1, 2):
        x_relays += plane_relay(x_state, k)
    wp_load.wait()
    turn = pl.ds(pl.multiple_of(256 * x + 128 * b, 128), 128)

    def project(h):
        p = dot(n0[...], wp[:, at(h, 384)]) + offs[at(h, 384)][None, :]
        hs[h, :, 0:128] = turned(p[:, 0:128], cosr[turn, :], sinr[turn, :]).astype(bf16)
        hs[h, :, 128:256] = turned(p[:, 128:256], cosr[turn, :], sinr[turn, :]).astype(bf16)
        hs[h, :, 256:384] = p[:, 256:384].astype(bf16)

    loop(4, project)

    def to_heads(cols):
        copies = [send(hs.at[flip4(m, k), :, cols], heads.at[at(slot, 128), cols], plane_peer(k))
                  for k in (3, 2, 1)]
        return copies, move(hs.at[m, :, cols], heads.at[at(slot, 128), cols])

    def to_sibling(copies, kept, cols):
        arrive(copies)
        kept.wait()
        parts = [heads.at[pl.ds(512 * i + 256 * c, 256), cols] for i in (0, 1)]
        return [send(part, part, sibling()) for part in parts]

    qkv_cols, up_cols = pl.ds(0, 384), pl.ds(384, 128)
    qkv_copies, qkv_own = to_heads(qkv_cols)
    x_relays += plane_relay(x_state, 3)
    gather_step(g_state, 1)
    arrive([x_state["plane"][k][1] for k in range(4)])
    norm(flip4(m, 1), False)
    wu_load.wait()

    def feed(pair_index, first, count):
        rows = at(pair_index, 256)

        def tile(n):
            cols = at(first + n, 512)
            u = dot(n1[...], wu[:, cols]) + hbias[cols][None, :]
            phi = 0.5 + 0.5 * lax.erf(u * 0.7071067811865476)
            act[rows, cols] = (u * phi).astype(bf16)
            gd[rows, cols] = (phi + u * (0.3989422804014327 * jnp.exp(-0.5 * u * u))).astype(gd.dtype)

        loop(count, tile)

    feed(x, 0, 2)
    gather_step(g_state, 2)
    qkv_pair = to_sibling(qkv_copies, qkv_own, qkv_cols)
    att_view = lambda i: att.at[:, at(i, 128)]
    att_half = lambda i, h: att.at[pl.ds(256 * h, 256), at(i, 128)]
    pack_view = lambda i: pack.at[:, at(i, 384)]
    pack_half = lambda i, h: pack.at[pl.ds(256 * h, 256), at(i, 384)]

    def score_rows(i):
        width = 256 * (i + 1)
        part = pl.ds(256 * i, 256)
        scores = contract_cols(heads[part, 0:128], heads[0:width, 128:256]) * scale
        query = (256 * i + lax.broadcasted_iota(jnp.int32, (256, 1), 0)).astype(f32)
        key = lax.broadcasted_iota(jnp.int32, (256, width), 1).astype(f32)
        visible = (key <= query) & (key >= starts[part, 0:1])
        return part, width, jnp.where(visible, scores, masked_score), visible

    arrive(qkv_pair)
    for i in range(4):
        part, width, masked, visible = score_rows(i)
        top = jnp.max(masked, axis=-1, keepdims=True)
        weights = jnp.where(visible, jnp.exp(masked - top), 0.0)
        total = jnp.sum(weights, axis=-1, keepdims=True)
        attf[part, :] = dot(weights.astype(bf16), heads[0:width, 256:384]) / total
        lse[part, :] = jnp.broadcast_to(top + jnp.log(total), (256, 128))

    for i in (0, 1):
        att[pl.ds(256 * i, 256), at(m, 128)] = attf[pl.ds(512 * i + 256 * c, 256), :].astype(bf16)
    gather_step(g_state, 3)
    wo_load.wait()

    head_low = dot(cg[mine, :], wo[...]).astype(bf16)
    for h in range(4):
        hs[h, :, 384:512] = head_low[:, 128 * h : 128 * (h + 1)]
    up_copies, up_own = to_heads(up_cols)
    att_copies = direct(att_view)
    both_on_plane(g_state, 0)
    both_on_plane(g_state, 1)
    feed(x, 2, 2)
    up_pair = to_sibling(up_copies, up_own, up_cols)
    arrive(up_pair)

    for i in range(4):
        part, width, masked, visible = score_rows(i)
        probs = jnp.where(visible, jnp.exp(masked - lse[part, 0:1]), 0.0)
        up = heads[part, 384:512]
        delta = jnp.sum(up.astype(f32) * attf[part, :], axis=-1, keepdims=True)
        grads = (probs * (contract_cols(up, heads[0:width, 256:384]) - delta)).astype(bf16)
        dv_acc[0:width, :] += contract_rows(probs.astype(bf16), up)
        dk_acc[0:width, :] += contract_rows(grads, heads[part, 0:128])

        @pl.when(i % 2 == c)
        def _():
            here = pl.ds(256 * (i // 2), 256)
            back = dot(grads, heads[0:width, 128:256]) * scale
            pack[here, at(3 * m, 128)] = turned(back, cosr[here, :], -sinr[here, :]).astype(bf16)

    for i in (0, 1):
        part, here = pl.ds(512 * i + 256 * c, 256), pl.ds(256 * i, 256)
        key_back = turned(dk_acc[part, :] * scale, cosr[here, :], -sinr[here, :])
        pack[here, at(3 * m + 1, 128)] = key_back.astype(bf16)
        pack[here, at(3 * m + 2, 128)] = dv_acc[part, :].astype(bf16)
    att_relays = relay(att_copies, att_half)
    pack_copies = direct(pack_view)
    both_on_plane(g_state, 2)
    both_on_plane(g_state, 3)
    arrive(x_relays)
    norm(flip4(m, 2), False)
    norm(flip4(m, 3), False)
    wd_load.wait()

    def feed_out(n):
        accg[:, at(n, 1024)] = contract_cols(act[mine, :], wd[at(n, 1024), :])

    loop(2, feed_out)
    arrive(att_relays)

    def finish_out(n):
        total = accg[:, at(n, 1024)] + contract_cols(att[mine, :], wo[at(n, 1024), :])
        for i in range(4):
            ob[i, n] = total[:, 256 * i : 256 * (i + 1)].astype(bf16)

    loop(2, finish_out)

    def scatter(src, dst):
        copies = [send(src.at[flip4(t, k)], dst.at[t], grid_peer(k)) for k in (3, 2, 1)]
        return copies, move(src.at[t], dst.at[t])

    def across(copies, kept, src, which):
        arrive(copies)
        kept.wait()
        sums = [sum(src[i, half].astype(f32) for i in range(4)) for half in (0, 1)]
        keep = jnp.where(b == 0, sums[0], sums[1])
        swap_b[which] = jnp.where(b == 0, sums[1], sums[0]).astype(bf16)
        return keep, send(swap_b.at[which], back_b.at[which], grid_peer(4))

    out_copies, out_own = scatter(ob, ro)

    def hidden(rows):
        def tile(n):
            cols = at(n, 512)
            hid[rows, cols] = (dot(cg[rows, :], wd[:, cols]) * gd[rows, cols].astype(f32)).astype(bf16)

        loop(4, tile)

    hidden(mine)

    def norm_grad(n, values, weight, which):
        cols = at(n, 512)
        ng = contract_cols(values, weight[cols, :])
        usum[which : which + 1, cols] = jnp.sum(ng * xh[:, cols], axis=0, keepdims=True)
        usum[which + 2 : which + 3, cols] = jnp.sum(ng, axis=0, keepdims=True)
        return ng * rows2[which, 0:1, cols]

    def feed_grad(n):
        cols = at(n, 512)
        accg[:, cols] = norm_grad(n, hid[mine, :], wu, 1)
        usum[6:7, cols] = jnp.sum(hid[mine, cols].astype(f32), axis=0, keepdims=True)
        usum[4:5, cols] = jnp.sum(cg[mine, cols].astype(f32), axis=0, keepdims=True)

    loop(4, feed_grad)
    pack_relays = relay(pack_copies, pack_half)
    feed(1 - x, 0, 4)
    arrive([g_state["plane"][k][1] for k in range(8)])
    g_relays = []
    for k in range(4):
        g_relays += plane_relay(g_state, k, True)
    def transpose_tokens(i):
        part = at(i, 128)
        for half in (0, 1):
            cols = pl.ds(256 * half, 256)
            features = at(4 * x + 2 * flip(c, half) + b, 256)
            hat = (xg[part, features].astype(f32) - mean_s[part, 0:1]) * inv_s[part, 0:1]
            for which, dst in ((0, n0t), (1, n1t)):
                low = hat * rows2[which, 0:1, features] + rows2[which, 1:2, features]
                dst[cols, part] = low.T.astype(bf16)

    loop(4, transpose_tokens)
    hidden(at(flip4(m, 1), 128))
    arrive(pack_relays)

    def attention_grad(n):
        accg[:, at(n, 512)] += norm_grad(n, pack[mine, :], wp, 0)

    loop(4, attention_grad)
    usum[5:6, 0:1536] = jnp.sum(pack[mine, :].astype(f32), axis=0, keepdims=True)
    pair_copy = send(usum, pair, sibling())
    zero = jnp.zeros((128, 1), f32)

    def means(n, carry):
        g = accg[:, at(n, 256)]
        return (carry[0] + jnp.sum(g, axis=-1, keepdims=True),
                carry[1] + jnp.sum(g * xh[:, at(n, 256)], axis=-1, keepdims=True))

    mean, slope = lax.fori_loop(0, 8, means, (zero, zero))
    mean, slope = mean * (1.0 / 2048), slope * (1.0 / 2048)

    def finish_grad(n):
        gb[n % 4, n // 4] = (inv_s[mine, 0:1] * (accg[:, at(n, 256)] - mean - xh[:, at(n, 256)] * slope)).astype(bf16)

    loop(8, finish_grad)
    grad_copies, grad_own = scatter(gb, rg)
    writes, swaps = [], []

    def matrix(lhs, rhs, count, base):
        first, here = used["sem"], used["local"]
        used["sem"] += count
        used["local"] += count

        def swap(i):
            return pltpu.make_async_remote_copy(
                src_ref=other.at[base + i], dst_ref=came_o.at[base + i],
                send_sem=sems.at[0, first + i], recv_sem=sems.at[1, first + i],
                device_id=sibling(), device_id_type=MESH)

        def keep(i):
            return pltpu.make_async_copy(kept.at[base + i], kept_o.at[base + i], local.at[here + i])

        def produce(i):
            both = dot(lhs[...], rhs[:, at(i, 512)]).astype(bf16)
            other[base + i] = both[256:]
            swap(i).start()
            kept[base + i] = both[:256]
            keep(i).start()

        loop(count, produce)
        for i in range(count):
            writes.append(keep(i))
            swaps.append(swap(i))

    matrix(n0t, pack, 3, 9)
    arrive(g_relays)
    hidden(at(1 - x, 256))

    def transpose_grads(i):
        part = at(i, 128)
        for half in (0, 1):
            features = at(4 * x + 2 * flip(c, half) + b, 256)
            ct[pl.ds(256 * half, 256), part] = cg[part, features].astype(f32).T.astype(bf16)

    loop(4, transpose_grads)
    arrive([pair_copy])
    pair[...] += usum[...]
    near_copies = [send(pair, near.at[k - 1], plane_peer(k)) for k in (1, 2, 3)]
    matrix(ct, act, 4, 0)
    arrive(near_copies)
    sums_o[t] = pair[...] + near[0] + near[1] + near[2]
    sum_copies = [send(sums_o.at[t], sums_o.at[t], grid_peer(k)) for k in (1, 2, 3)]
    out_keep, out_swap = across(out_copies, out_own, ro, 0)
    matrix(n1t, hid, 4, 4)
    matrix(ct, att, 1, 8)
    for copy in late:
        copy.wait()
    columns = at(j, 256)
    bias = rows2[0, 2:3, columns] + rows2[1, 2:3, columns]
    here, there = at(b, 128), at(1 - b, 128)
    layer_o[here, :] = (bias + tok_v[here, :].astype(f32) + out_keep).astype(bf16)
    arrive([out_swap])
    layer_o[there, :] = (bias + tok_v[there, :].astype(f32) + back_b[0].astype(f32)).astype(bf16)
    grad_keep, grad_swap = across(grad_copies, grad_own, rg, 1)
    grad_o[here, :] = cot_v[here, :].astype(f32) + grad_keep
    arrive(sum_copies + [grad_swap])
    grad_o[there, :] = cot_v[there, :].astype(f32) + back_b[1].astype(f32)
    for copy in writes + swaps:
        copy.wait()
    for copy in sent:
        copy.wait_send()
    for copy in inner_sent:
        pl.when(inner)(copy.wait_send)
    assert used["sem"] <= 150 and used["local"] <= 40, used


def emit_kernel(layer, grad, kept, came, sums, layer_o, grad_o, project_o, output_o,
                up_o, down_o, offs_o, hidden_o, gain_o, center_o, residual_o):
    for out, base, count in ((down_o, 0, 4), (up_o, 4, 4), (output_o, 8, 1), (project_o, 9, 3)):
        for i in range(count):
            out[:, pl.ds(512 * i, 512)] = kept[base + i].astype(f32) + came[base + i].astype(f32)

    @pl.when(pl.program_id(0) == 0)
    def _():
        layer_o[...] = layer[...]
        grad_o[...] = grad[...]
        gain_o[...] = sums[0, 0:2] + sums[1, 0:2] + sums[2, 0:2] + sums[3, 0:2]
        center_o[...] = sums[0, 2:4] + sums[1, 2:4] + sums[2, 2:4] + sums[3, 2:4]
        residual_o[...] = jnp.broadcast_to(sums[0, 4:5], (2, 2048))
        for i in range(4):
            offs_o[pl.ds(1536 * i, 1536)] = sums[i, 5, 0:1536]
            hidden_o[pl.ds(2048 * i, 2048)] = sums[i, 6]


def fast_device(tokens, cotangent, documents, positions, project_weight, offsets, output_weight,
                up_weight, hidden_bias, down_weight, norm_gain, norm_bias, residual_bias):
    vmem, anywhere = pl.BlockSpec(memory_space=pltpu.VMEM), pl.BlockSpec(memory_space=pl.ANY)
    shape = jax.ShapeDtypeStruct
    low = lambda *size: pltpu.VMEM(size, bf16)
    full = lambda *size: pltpu.VMEM(size, f32)
    widths = (1536, 512, 2048, 2048)
    results = pl.pallas_call(
        layer_kernel,
        out_shape=[shape((256, 256), bf16), shape((256, 256), f32)]
        + [shape((12, 256, 512), bf16)] * 2 + [shape((4, 8, 2048), f32)],
        in_specs=[anywhere] * 12,
        out_specs=[vmem] * 2 + [anywhere] * 2 + [vmem],
        scratch_shapes=[
            low(2048, 1536), low(2048, 512), low(2048, 2048), low(2048, 2048),
            low(256, 256), low(256, 256), pltpu.VMEM((256,), jnp.int32), full(1, 2048), full(1, 2048),
            full(1, 2048), full(1536), full(2048),
            low(512, 2048), low(512, 2048), full(4, 8, 256), full(1024, 128), full(512, 128),
            full(512, 128), full(2, 8, 2048), full(128, 2048), full(512, 128), full(512, 128),
            low(128, 2048), low(256, 2048), GD(512, 2048), low(512, 2048), low(512, 2048),
            low(4, 128, 512), low(1024, 512), low(512, 512), low(512, 1536), full(1024, 128),
            full(1024, 128), full(1024, 128), full(1024, 128), low(4, 2, 128, 256),
            low(4, 2, 128, 256), low(4, 2, 128, 256), low(4, 2, 128, 256), low(2, 128, 256),
            low(2, 128, 256), full(128, 2048), low(512, 512), low(512, 512),
            low(512, 512), low(12, 256, 512),
            low(12, 256, 512), full(8, 2048), full(8, 2048), full(3, 8, 2048),
            pltpu.SemaphoreType.DMA((2, 150)), pltpu.SemaphoreType.DMA((40,))],
        compiler_params=pltpu.CompilerParams(
            collective_id=0, has_side_effects=True, vmem_limit_bytes=LIMIT),
    )(tokens, cotangent, positions, norm_gain, norm_bias, residual_bias,
      offsets, hidden_bias, project_weight, output_weight, up_weight, down_weight)
    steps = 2
    whole = lambda *size: pl.BlockSpec(size, lambda i: (0,) * len(size))
    band = lambda width: pl.BlockSpec((256 // steps, width), lambda i: (i, 0))
    layer_out, input_grad, *rest = pl.pallas_call(
        emit_kernel,
        grid=(steps,),
        out_shape=[shape((256, 256), bf16), shape((256, 256), f32)]
        + [shape((256, width), f32) for width in widths]
        + [shape((6144,), f32), shape((8192,), f32)] + [shape((2, 2048), f32)] * 3,
        in_specs=[whole(256, 256)] * 2
        + [pl.BlockSpec((12, 256 // steps, 512), lambda i: (0, i, 0))] * 2 + [whole(4, 8, 2048)],
        out_specs=[whole(256, 256)] * 2 + [band(width) for width in widths]
        + [whole(6144), whole(8192)] + [whole(2, 2048)] * 3,
        compiler_params=pltpu.CompilerParams(vmem_limit_bytes=LIMIT),
    )(*results)
    return (layer_out, input_grad, *rest)


LIMIT = 63 << 20
GD = lambda *size: pltpu.VMEM(size, bf16)


def solution(mesh):
    fits = (mesh.shape["seq"], mesh.shape["branch"], mesh.shape["tensor"]) == (4, 2, 4)
    return jax.shard_map(
        fast_device if fits else on_device,
        mesh=mesh,
        in_specs=(
            P("seq", ("branch", "tensor")),
            P("seq", ("branch", "tensor")),
            P("seq"),
            P("seq"),
            P(None, "tensor"),
            P("tensor"),
            P(None, "tensor"),
            P(None, "tensor"),
            P("tensor"),
            P(None, "tensor"),
            P("branch", None),
            P("branch", None),
            P("branch", None),
        ),
        out_specs=(
            P("seq", ("branch", "tensor")),
            P("seq", ("branch", "tensor")),
            P(("seq", "branch"), "tensor"),
            P(("seq", "branch"), "tensor"),
            P(("seq", "branch"), "tensor"),
            P(("seq", "branch"), "tensor"),
            P(),
            P(),
            P(),
            P(),
            P(),
        ),
        check_vma=False,
    )
```

```python
from functools import partial

import jax
import jax.numpy as jnp
from jax import lax
from jax.experimental import pallas as pl
from jax.experimental.pallas import tpu as pltpu
from jax.sharding import PartitionSpec as P

HEAD_DIM = 128
ROT = 32


norm_eps = 1e-05
rope_base = 10000.0
masked_score = -1e30


def passed_along(value, axis, steps):
    count = lax.axis_size(axis)
    pairs = [(source, (source + steps) % count) for source in range(count)]
    return lax.ppermute(value, axis, pairs)


def shifted(array, axis, by):
    count = lax.axis_size(axis)
    pairs = [(i, i + by) for i in range(count) if 0 <= i + by < count]
    return lax.ppermute(array, axis, pairs)


def layer_norm(values, gain_row, shift_row):
    average = jnp.mean(values, axis=-1, keepdims=True)
    centered = values - average
    variance = jnp.mean(centered * centered, axis=-1, keepdims=True)
    return centered * lax.rsqrt(variance + norm_eps) * gain_row + shift_row


def rope_tables(places):
    half_rot = ROT // 2
    frequency = rope_base ** (-(2.0 * jnp.arange(half_rot, dtype=jnp.float32)) / ROT)
    angles = places.astype(jnp.float32)[:, None] * frequency[None, :]
    return (jnp.cos(angles), jnp.sin(angles))


def rotate(values, cosine, sine_rows, direction):
    half_rot = ROT // 2
    first_half = values[..., :half_rot]
    second_half = values[..., half_rot:ROT]
    cos_table = cosine[:, None, :]
    sin_table = direction * sine_rows[:, None, :]
    return jnp.concatenate(
        [
            first_half * cos_table - second_half * sin_table,
            second_half * cos_table + first_half * sin_table,
            values[..., ROT:],
        ],
        axis=-1,
    )


def contract_rows(first_side, second_side):
    return lax.dot_general(
        first_side, second_side, (((0,), (0,)), ((), ())), preferred_element_type=jnp.float32
    )


def contract_cols(first_side, second_side):
    return lax.dot_general(
        first_side, second_side, (((1,), (1,)), ((), ())), preferred_element_type=jnp.float32
    )


def on_device(
    tokens,
    cotangent,
    documents,
    positions,
    project_weight,
    offsets,
    output_weight,
    up_weight,
    hidden_bias,
    down_weight,
    norm_gain,
    norm_bias,
    residual_bias,
):
    tok_rows = tokens.shape[0]
    model_width = up_weight.shape[0]
    attn_width = output_weight.shape[1]
    local_heads = attn_width // HEAD_DIM
    hidden_local = up_weight.shape[1]
    seq_count = lax.axis_size("seq")
    seq_index = lax.axis_index("seq")
    branch_index = lax.axis_index("branch")
    tensor_index = lax.axis_index("tensor")
    is_attention = branch_index == 0
    lead_tensor = tensor_index == 0
    score_scale = HEAD_DIM ** (-0.5)
    local_index = jnp.arange(tok_rows, dtype=jnp.int32)
    query_index = seq_index * tok_rows + local_index
    full_tokens, full_cotangent = (
        lax.all_gather(tokens, ("branch", "tensor"), axis=1, tiled=True),
        lax.all_gather(cotangent, ("branch", "tensor"), axis=1, tiled=True),
    )
    gain_row = norm_gain[0]
    shift_row = norm_bias[0]
    normed, norm_pullback = jax.vjp(
        layer_norm, full_tokens.astype(jnp.float32), gain_row, shift_row
    )
    normed_low = normed.astype(jnp.bfloat16)
    cosine, sine_rows = rope_tables(positions)
    zeros_heads = jnp.zeros((tok_rows, attn_width), jnp.bfloat16)
    zeros_hidden = jnp.zeros((tok_rows, hidden_local), jnp.float32)
    hidden_zero = jnp.zeros((tok_rows, hidden_local), jnp.bfloat16)
    zeros_stats = jnp.zeros((local_heads, tok_rows), jnp.float32)
    grad_zero = jnp.zeros((tok_rows, local_heads, HEAD_DIM), jnp.float32)

    def attention_front(unused):
        packed = jnp.dot(normed_low, project_weight, preferred_element_type=jnp.float32) + offsets
        packed = packed.reshape(tok_rows, local_heads, 3, HEAD_DIM)
        query_rot = rotate(packed[:, :, 0], cosine, sine_rows, 1.0).reshape(tok_rows, attn_width)
        key_rot = rotate(packed[:, :, 1], cosine, sine_rows, 1.0).reshape(tok_rows, attn_width)
        value_rows = packed[:, :, 2].reshape(tok_rows, attn_width)
        return (
            query_rot.astype(jnp.bfloat16),
            key_rot.astype(jnp.bfloat16),
            value_rows.astype(jnp.bfloat16),
            zeros_hidden,
            hidden_zero,
        )

    def feed_front(unused):
        up_rows = jnp.dot(normed_low, up_weight, preferred_element_type=jnp.float32) + hidden_bias
        active = jax.nn.gelu(up_rows, approximate=False).astype(jnp.bfloat16)
        return (zeros_heads, zeros_heads, zeros_heads, up_rows, active)

    query_low, key_low, value_low, up_rows, active = lax.cond(
        is_attention, attention_front, feed_front, 0
    )
    query_heads = query_low.reshape(tok_rows, local_heads, HEAD_DIM)

    def absorb(totals, key_rows, value_rows, key_ids, offset):
        key_count = key_rows.shape[0]
        key_index = offset + jnp.arange(key_count, dtype=jnp.int32)
        visible = (documents[:, None] == key_ids[None, :]) & (
            key_index[None, :] <= query_index[:, None]
        )

        def update(running):
            run_max, run_sum, run_acc = running
            scores = (
                jnp.einsum(
                    "qhd,khd->hqk",
                    query_heads,
                    key_rows.reshape(key_count, local_heads, HEAD_DIM),
                    preferred_element_type=jnp.float32,
                )
                * score_scale
            )
            masked = jnp.where(visible[None], scores, masked_score)
            new_max = jnp.maximum(run_max, jnp.max(masked, axis=-1))
            weights = jnp.where(visible[None], jnp.exp(masked - new_max[:, :, None]), 0.0)
            factor = jnp.exp(run_max - new_max)
            blended = jnp.einsum(
                "hqk,khd->qhd",
                weights.astype(jnp.bfloat16),
                value_rows.reshape(key_count, local_heads, HEAD_DIM),
                preferred_element_type=jnp.float32,
            )
            return (
                new_max,
                run_sum * factor + jnp.sum(weights, axis=-1),
                run_acc * factor.T[:, :, None] + blended,
            )

        def unchanged(running):
            return running

        return lax.cond(is_attention & jnp.any(visible), update, unchanged, totals)

    initial = (jnp.full((local_heads, tok_rows), masked_score, jnp.float32), zeros_stats, grad_zero)
    totals = initial
    key_rows = lax.all_gather(key_low, "seq", axis=0, tiled=True)
    value_rows = lax.all_gather(value_low, "seq", axis=0, tiled=True)
    key_ids = lax.all_gather(documents, "seq", axis=0, tiled=True)
    key_count = key_rows.shape[0]
    groups = key_count // tok_rows

    def absorb_group(running, sliced):
        return (absorb(running, sliced[0], sliced[1], sliced[2], sliced[3]), None)

    starts = tok_rows * jnp.arange(groups, dtype=jnp.int32)
    stacked = (
        key_rows.reshape(groups, tok_rows, attn_width),
        value_rows.reshape(groups, tok_rows, attn_width),
        key_ids.reshape(groups, tok_rows),
        starts,
    )
    totals, unused = lax.scan(absorb_group, totals, stacked)
    run_max, run_sum, run_acc = totals

    def attention_out(unused):
        attended = run_acc / run_sum.T[:, :, None]
        attended_low = attended.reshape(tok_rows, attn_width).astype(jnp.bfloat16)
        return (
            contract_cols(attended_low, output_weight),
            attended,
            attended_low,
            run_max + jnp.log(run_sum),
        )

    def feed_out(unused):
        return (contract_cols(active, down_weight), grad_zero, zeros_heads, zeros_stats)

    branch_out, attended, attended_low, lse_rows = lax.cond(
        is_attention, attention_out, feed_out, 0
    )
    branch_out = branch_out + jnp.where(lead_tensor, residual_bias[0], 0.0)
    summed = lax.psum_scatter(
        branch_out.astype(jnp.bfloat16), ("branch", "tensor"), scatter_dimension=1, tiled=True
    ).astype(jnp.float32)
    layer_out = (tokens.astype(jnp.float32) + summed).astype(jnp.bfloat16)

    def attention_prep(unused):
        grad_low = jnp.dot(
            full_cotangent, output_weight, preferred_element_type=jnp.float32
        ).astype(jnp.bfloat16)
        delta_rows = jnp.sum(
            grad_low.reshape(tok_rows, local_heads, HEAD_DIM).astype(jnp.float32) * attended,
            axis=-1,
        ).T
        return (grad_low, delta_rows, hidden_zero)

    def feed_prep(unused):
        active_grad = jnp.dot(full_cotangent, down_weight, preferred_element_type=jnp.float32)
        gelu_value, gelu_pullback = jax.vjp(partial(jax.nn.gelu, approximate=False), up_rows)
        return (zeros_heads, zeros_stats, gelu_pullback(active_grad)[0].astype(jnp.bfloat16))

    grad_low, delta_rows, hidden_low = lax.cond(is_attention, attention_prep, feed_prep, 0)

    def block_grads(
        query_rows,
        grad_rows,
        query_lse,
        query_delta,
        query_ids,
        query_place,
        key_rows,
        value_rows,
        key_ids,
        key_place,
    ):
        visible = (query_ids[:, None] == key_ids[None, :]) & (
            key_place[None, :] <= query_place[:, None]
        )

        def compute(unused):
            query_part_heads = query_rows.reshape(tok_rows, local_heads, HEAD_DIM)
            grad_heads = grad_rows.reshape(tok_rows, local_heads, HEAD_DIM)
            key_heads = key_rows.reshape(tok_rows, local_heads, HEAD_DIM)
            value_heads = value_rows.reshape(tok_rows, local_heads, HEAD_DIM)
            scores = (
                jnp.einsum(
                    "qhd,khd->hqk", query_part_heads, key_heads, preferred_element_type=jnp.float32
                )
                * score_scale
            )
            weights = jnp.exp(
                jnp.where(visible[None], scores - query_lse[:, :, None], masked_score)
            )
            value_part = jnp.einsum(
                "hqk,qhd->khd",
                weights.astype(jnp.bfloat16),
                grad_heads,
                preferred_element_type=jnp.float32,
            )
            weight_grad = jnp.einsum(
                "qhd,khd->hqk", grad_heads, value_heads, preferred_element_type=jnp.float32
            )
            score_grad = (weights * (weight_grad - query_delta[:, :, None])).astype(jnp.bfloat16)
            query_part = (
                jnp.einsum(
                    "hqk,khd->qhd", score_grad, key_heads, preferred_element_type=jnp.float32
                )
                * score_scale
            )
            key_part = (
                jnp.einsum(
                    "hqk,qhd->khd", score_grad, query_part_heads, preferred_element_type=jnp.float32
                )
                * score_scale
            )
            return (query_part, key_part, value_part)

        def nothing(unused):
            return (grad_zero, grad_zero, grad_zero)

        return lax.cond(is_attention & jnp.any(visible), compute, nothing, 0)

    def send_grads(key_acc, value_acc):
        return (
            passed_along(key_acc.astype(jnp.bfloat16), "seq", 1).astype(key_acc.dtype),
            passed_along(value_acc.astype(jnp.bfloat16), "seq", 1).astype(value_acc.dtype),
        )

    def key_step(cycle_state, unused):
        key_rows, value_rows, key_ids, key_acc, value_acc, hop_count, query_acc = cycle_state
        source = (seq_index - hop_count) % seq_count
        partial_terms = block_grads(
            query_low,
            grad_low,
            lse_rows,
            delta_rows,
            documents,
            query_index,
            key_rows,
            value_rows,
            key_ids,
            source * tok_rows + local_index,
        )
        key_rows, value_rows, key_ids = shifted((key_rows, value_rows, key_ids), "seq", 1)
        key_acc, value_acc = send_grads(key_acc + partial_terms[1], value_acc + partial_terms[2])
        return (
            (
                key_rows,
                value_rows,
                key_ids,
                key_acc,
                value_acc,
                hop_count + 1,
                query_acc + partial_terms[0],
            ),
            None,
        )

    start_state = (key_low, value_low, documents, grad_zero, grad_zero, jnp.int32(0), grad_zero)
    cycle_state, unused = lax.scan(key_step, start_state, None, length=seq_count - 1)
    key_rows, value_rows, key_ids, key_acc, value_acc, hop_count, query_acc = cycle_state
    source = (seq_index - hop_count) % seq_count
    partial_terms = block_grads(
        query_low,
        grad_low,
        lse_rows,
        delta_rows,
        documents,
        query_index,
        key_rows,
        value_rows,
        key_ids,
        source * tok_rows + local_index,
    )
    key_grad, value_grad = send_grads(key_acc + partial_terms[1], value_acc + partial_terms[2])
    query_grad = query_acc + partial_terms[0]

    def attention_tail(unused):
        query_back = rotate(query_grad, cosine, sine_rows, -1.0)
        key_back = rotate(key_grad, cosine, sine_rows, -1.0)
        packed_grad = (
            jnp.stack([query_back, key_back, value_grad], axis=2)
            .reshape(tok_rows, 3 * attn_width)
            .astype(jnp.bfloat16)
        )
        return (contract_cols(packed_grad, project_weight), packed_grad)

    def feed_tail(unused):
        return (
            contract_cols(hidden_low, up_weight),
            jnp.zeros((tok_rows, 3 * attn_width), jnp.bfloat16),
        )

    norm_grad, packed_grad = lax.cond(is_attention, attention_tail, feed_tail, 0)
    input_part, gain_part, shift_part = norm_pullback(norm_grad)
    input_grad = lax.psum_scatter(
        input_part.astype(jnp.bfloat16), ("branch", "tensor"), scatter_dimension=1, tiled=True
    ).astype(jnp.float32) + cotangent.astype(jnp.float32)

    def attention_rows(unused):
        return jnp.concatenate(
            [
                contract_rows(normed_low, packed_grad),
                contract_rows(full_cotangent, attended_low),
                jnp.zeros(
                    (
                        model_width
                        // (seq_count * lax.axis_size("branch"))
                        * lax.axis_size(("seq", "branch")),
                        2 * hidden_local,
                    ),
                    jnp.float32,
                ),
            ],
            axis=1,
        )

    def feed_rows(unused):
        return jnp.concatenate(
            [
                jnp.zeros(
                    (
                        model_width
                        // (seq_count * lax.axis_size("branch"))
                        * lax.axis_size(("seq", "branch")),
                        4 * attn_width,
                    ),
                    jnp.float32,
                ),
                contract_rows(normed_low, hidden_low),
                contract_rows(full_cotangent, active),
            ],
            axis=1,
        )

    shares = lax.psum_scatter(
        lax.cond(is_attention, attention_rows, feed_rows, 0).astype(jnp.bfloat16),
        ("seq", "branch"),
        scatter_dimension=0,
        tiled=True,
    ).astype(jnp.float32)
    project_grad = shares[:, : 3 * attn_width]
    output_grad = shares[:, 3 * attn_width : 4 * attn_width]
    up_grad = shares[:, 4 * attn_width : 4 * attn_width + hidden_local]
    down_grad = shares[:, 4 * attn_width + hidden_local :]
    offsets_part = lax.dynamic_update_slice(
        jnp.zeros((3 * model_width,), jnp.float32),
        jnp.sum(packed_grad, axis=0, dtype=jnp.float32),
        (tensor_index * (3 * attn_width),),
    )
    hidden_part = lax.dynamic_update_slice(
        jnp.zeros((hidden_local * lax.axis_size("tensor"),), jnp.float32),
        jnp.sum(hidden_low, axis=0, dtype=jnp.float32),
        (tensor_index * hidden_local,),
    )
    pair_zero = jnp.zeros((2, model_width), jnp.float32)
    gain_rows = lax.dynamic_update_slice(
        pair_zero, gain_part[None, :], (branch_index, jnp.int32(0))
    )
    shift_rows = lax.dynamic_update_slice(
        pair_zero, shift_part[None, :], (branch_index, jnp.int32(0))
    )
    column_sums = jnp.where(lead_tensor, jnp.sum(full_cotangent, axis=0, dtype=jnp.float32), 0.0)
    residual_rows = lax.dynamic_update_slice(
        pair_zero, column_sums[None, :], (branch_index, jnp.int32(0))
    )
    offsets_grad, hidden_grad, gain_grad, center_grad, residual_grad = lax.psum(
        (offsets_part, hidden_part, gain_rows, shift_rows, residual_rows),
        ("seq", "branch", "tensor"),
    )
    return (
        layer_out,
        input_grad,
        project_grad,
        output_grad,
        up_grad,
        down_grad,
        offsets_grad,
        hidden_grad,
        gain_grad,
        center_grad,
        residual_grad,
    )


MESH = pl.DeviceIdType.MESH
bf16, f32 = jnp.bfloat16, jnp.float32


def place():
    s, b, t = lax.axis_index("seq"), lax.axis_index("branch"), lax.axis_index("tensor")
    return s, b, t, s // 2, s % 2


def flip(value, bit):
    return value + bit - 2 * bit * value


def flip4(value, k):
    return 2 * flip(value // 2, k // 2) + flip(value % 2, k % 2)


def plane_peer(k):
    s, b, t, x, c = place()
    return (2 * flip(x, k // 2) + c, flip(b, k % 2), t)


def grid_peer(k):
    s, b, t, x, c = place()
    return (s, flip(b, k // 4), flip4(t, k % 4))


def sibling():
    s, b, t, x, c = place()
    return (flip4(s, 1), b, t)


def meet(devices):
    barrier = pltpu.get_barrier_semaphore()
    for device in devices:
        pl.semaphore_signal(barrier, inc=1, device_id=device, device_id_type=MESH)
    pl.semaphore_wait(barrier, len(devices))


def at(index, size):
    return pl.ds(pl.multiple_of(index * size, size), size)


def dot(first, second):
    return jnp.dot(first, second, preferred_element_type=f32)


def turned(values, cosine, sines):
    lane = lax.broadcasted_iota(jnp.int32, values.shape, 1)
    swapped = jnp.where(
        lane < ROT // 2,
        pltpu.roll(values, HEAD_DIM - ROT // 2, 1),
        pltpu.roll(values, ROT // 2, 1),
    )
    return values * cosine + sines * swapped


def layer_kernel(
    tok, cot, places_h, gain_h, shift_h, residual_h, offs_h, hbias_h, wp_h, wo_h, wu_h, wd_h,
    layer_o, grad_o, kept_o, came_o, sums_o,
    wp, wo, wu, wd, tok_v, cot_v, places, gain, shift, residual, offs, hbias, xg, cg, posr, starts, cosr, sinr, rows2, xh, mean_s, inv_s, n0, n1, gd, act, hid,
    hs, heads, att, pack, attf, lse, dk_acc, dv_acc, ob, ro, gb, rg, swap_b, back_b, accg,
    n0t, n1t, ct, other, kept, usum, pair, near, sems, local,
):
    s, b, t, x, c = place()
    m, j = 2 * x + b, 4 * b + t
    slot = 4 * x + 2 * c + b
    scale = HEAD_DIM ** -0.5
    mine = at(m, 128)
    used = {"sem": 0, "local": 0}
    sent, inner_sent = [], []
    inner = (t == 1) | (t == 2)

    def describe(src, dst, device, there=None):
        index = used["sem"]
        used["sem"] += 1
        return pltpu.make_async_remote_copy(
            src_ref=src, dst_ref=dst, send_sem=sems.at[0, index],
            recv_sem=sems.at[1, index if there is None else there],
            device_id=device, device_id_type=MESH)

    def send(src, dst, device):
        copy = describe(src, dst, device)
        copy.start()
        sent.append(copy)
        return copy

    def send_inner(src, dst, device, there=None):
        copy = describe(src, dst, device, there)
        pl.when(inner)(copy.start)
        inner_sent.append(copy)
        return copy

    def move(src, dst):
        index = used["local"]
        used["local"] += 1
        copy = pltpu.make_async_copy(src, dst, local.at[index])
        copy.start()
        return copy

    def arrive(copies):
        for copy in copies:
            copy.wait_recv()

    def direct(view):
        return [send(view(m), view(m), plane_peer(k)) for k in (2, 1)]

    def relay(copies, half):
        out = []
        for i, k in enumerate((2, 1)):
            copies[i].wait_recv()
            part = half(flip4(m, k), i)
            out.append(send(part, part, plane_peer(3 - k)))
        return out

    def loop(count, body):
        def step(i, carry):
            body(i)
            return carry
        lax.fori_loop(0, count, step, 0)

    def block(k):
        return at(4 * flip(b, k // 4) + flip4(t, k % 4), 256)

    def gather(src, dst):
        half, place = src.at[at(b, 128)], dst.at[mine, at(j, 256)]
        over = send(src.at[at(1 - b, 128)], dst.at[at(flip4(m, 1), 128), at(j, 256)], grid_peer(4))
        return {"over": over, "half": half, "place": place, "own": move(half, place), "dst": dst,
                "plane": {}}

    def gather_near(state):
        state["near"] = to_tensor(state["half"], state["place"])

    def to_tensor(src, dst):
        last = used["sem"]
        third = send_inner(src, dst, grid_peer(3))
        return {2: send(src, dst, grid_peer(2)), 1: send(src, dst, grid_peer(1)), 3: third, "last": last}

    def on_plane(state, k):
        part = state["dst"].at[mine, block(k)]
        state["plane"][k] = [send(part, part, plane_peer(i)) for i in (2, 1)]

    def gather_over(state):
        state["own"].wait()
        state["over"].wait_recv()
        part = state["dst"].at[mine, block(4)]
        state["far"] = to_tensor(part, part)

    def gather_step(state, k):
        for which, first in (("near", 0), ("far", 4)):
            state[which][k].wait_recv()
            if k == 2:
                part = state["dst"].at[mine, block(first + 2)]
                send_inner(part, part, grid_peer(1), state[which]["last"])

    def both_on_plane(state, k):
        on_plane(state, k)
        on_plane(state, k + 4)

    def plane_relay(state, k, here=False):
        dst, plane = state["dst"], state["plane"]
        plane[k][0].wait_recv()
        part = dst.at[at(flip4(m, 2), 128), block(k)]
        first = send(part, part, plane_peer(1))
        if not here:
            plane[k + 4][1].wait_recv()
        part = dst.at[at(flip4(m, 1), 128), block(k)]
        return [first, send(part, part, plane_peer(2)), plane[k + 4][0]]

    meet([grid_peer(k) for k in (1, 2, 3, 4)] + [plane_peer(2), plane_peer(3)]
         + [(flip4(s, k), b, t) for k in (1, 3)])
    x_state = gather(tok, xg)
    gather_near(x_state)
    g_state = gather(cot, cg)
    small = [move(src, dst) for src, dst in (
        (places_h, places), (gain_h, gain), (shift_h, shift), (residual_h, residual),
        (offs_h, offs), (hbias_h, hbias))]
    wp_load, wu_load = move(wp_h, wp), move(wu_h, wu)
    wo_load, wd_load = move(wo_h, wo), move(wd_h, wd)
    late = [move(tok, tok_v), move(cot, cot_v)]
    for copy in small:
        copy.wait()
    rows2[b] = jnp.zeros((8, 2048), f32)
    rows2[b, 0:1, :] = gain[...]
    rows2[b, 1:2, :] = shift[...]
    rows2[b, 2:3, :] = residual[...]
    posr[s] = jnp.broadcast_to(places[...].astype(f32)[None, :], (8, 256))
    row_copy = send(rows2.at[b], rows2.at[b], grid_peer(4))
    place_copies = [send(posr.at[s], posr.at[s], (flip4(s, k), b, t)) for k in (1, 2, 3)]
    gather_over(x_state)
    both_on_plane(x_state, 0)
    usum[...] = jnp.zeros_like(usum)
    dk_acc[...] = jnp.zeros_like(dk_acc)
    dv_acc[...] = jnp.zeros_like(dv_acc)
    arrive(place_copies)
    for i in range(4):
        row = jnp.broadcast_to(posr[i, 0:1, :], (128, 256))
        index = (256 * i + lax.broadcasted_iota(jnp.int32, (256, 128), 0)).astype(f32)
        starts[pl.ds(256 * i, 256), :] = index - row.T
    line = lax.broadcasted_iota(jnp.int32, (ROT, 256), 0)
    waves = jnp.zeros((ROT, 256), f32)
    for i in range(ROT // 2):
        waves = jnp.where(line % (ROT // 2) == i, rope_base ** (-2.0 * i / ROT), waves)
    for i in (0, 1):
        angle = posr[2 * i + c, 0:1, :] * waves
        part = pl.ds(256 * i, 256)
        sign = jnp.where(line < ROT // 2, -1.0, 1.0)
        rest = jnp.zeros((HEAD_DIM - ROT, 256), f32)
        cosr[part, :] = jnp.concatenate([jnp.cos(angle), rest + 1.0], axis=0).T
        sinr[part, :] = jnp.concatenate([jnp.sin(angle) * sign, rest], axis=0).T
    for k in (1, 2, 3):
        gather_step(x_state, k)
        both_on_plane(x_state, k)
        if k == 2:
            gather_near(g_state)
            gather_over(g_state)
    arrive([row_copy])

    def norm(which, whole):
        def rows(i):
            part = pl.ds(pl.multiple_of(which * 128 + 32 * i, 32), 32)
            v = xg[part, :].astype(f32)
            mean = jnp.mean(v, axis=-1, keepdims=True)
            centered = v - mean
            inverse = lax.rsqrt(jnp.mean(centered * centered, axis=-1, keepdims=True) + norm_eps)
            hat = centered * inverse
            mean_s[part, :] = jnp.broadcast_to(mean, (32, 128))
            inv_s[part, :] = jnp.broadcast_to(inverse, (32, 128))
            n1_part = pl.ds(pl.multiple_of((which % 2) * 128 + 32 * i, 32), 32)
            n1[n1_part, :] = (hat * rows2[1, 0:1, :] + rows2[1, 1:2, :]).astype(bf16)
            if whole:
                xh[at(i, 32), :] = hat
                n0[at(i, 32), :] = (hat * rows2[0, 0:1, :] + rows2[0, 1:2, :]).astype(bf16)

        loop(4, rows)

    norm(m, True)
    x_relays = []
    for k in (0, 1, 2):
        x_relays += plane_relay(x_state, k)
    wp_load.wait()
    turn = pl.ds(pl.multiple_of(256 * x + 128 * b, 128), 128)

    def project(h):
        p = dot(n0[...], wp[:, at(h, 384)]) + offs[at(h, 384)][None, :]
        hs[h, :, 0:128] = turned(p[:, 0:128], cosr[turn, :], sinr[turn, :]).astype(bf16)
        hs[h, :, 128:256] = turned(p[:, 128:256], cosr[turn, :], sinr[turn, :]).astype(bf16)
        hs[h, :, 256:384] = p[:, 256:384].astype(bf16)

    loop(4, project)

    def to_heads(cols):
        copies = [send(hs.at[flip4(m, k), :, cols], heads.at[at(slot, 128), cols], plane_peer(k))
                  for k in (3, 2, 1)]
        return copies, move(hs.at[m, :, cols], heads.at[at(slot, 128), cols])

    def to_sibling(copies, kept, cols):
        arrive(copies)
        kept.wait()
        parts = [heads.at[pl.ds(512 * i + 256 * c, 256), cols] for i in (0, 1)]
        return [send(part, part, sibling()) for part in parts]

    qkv_cols, up_cols = pl.ds(0, 384), pl.ds(384, 128)
    qkv_copies, qkv_own = to_heads(qkv_cols)
    x_relays += plane_relay(x_state, 3)
    gather_step(g_state, 1)
    arrive([x_state["plane"][k][1] for k in range(4)])
    norm(flip4(m, 1), False)
    gather_step(g_state, 2)
    wu_load.wait()

    def feed(pair_index, first, count):
        rows = at(pair_index, 256)

        def tile(n):
            cols = at(first + n, 512)
            u = dot(n1[...], wu[:, cols]) + hbias[cols][None, :]
            phi = 0.5 + 0.5 * lax.erf(u * 0.7071067811865476)
            act[rows, cols] = (u * phi).astype(bf16)
            gd[rows, cols] = (phi + u * (0.3989422804014327 * jnp.exp(-0.5 * u * u))).astype(gd.dtype)

        loop(count, tile)

    feed(x, 0, 2)
    qkv_pair = to_sibling(qkv_copies, qkv_own, qkv_cols)
    att_view = lambda i: att.at[:, at(i, 128)]
    att_half = lambda i, h: att.at[pl.ds(256 * h, 256), at(i, 128)]
    pack_view = lambda i: pack.at[:, at(i, 384)]
    pack_half = lambda i, h: pack.at[pl.ds(256 * h, 256), at(i, 384)]

    def score_rows(i):
        width = 256 * (i + 1)
        part = pl.ds(256 * i, 256)
        scores = contract_cols(heads[part, 0:128], heads[0:width, 128:256]) * scale
        query = (256 * i + lax.broadcasted_iota(jnp.int32, (256, 1), 0)).astype(f32)
        key = lax.broadcasted_iota(jnp.int32, (256, width), 1).astype(f32)
        visible = (key <= query) & (key >= starts[part, 0:1])
        return part, width, jnp.where(visible, scores, masked_score), visible

    gather_step(g_state, 3)
    wo_load.wait()

    head_low = dot(cg[mine, :], wo[...]).astype(bf16)
    for h in range(4):
        hs[h, :, 384:512] = head_low[:, 128 * h : 128 * (h + 1)]
    up_copies, up_own = to_heads(up_cols)
    arrive(qkv_pair)
    for i in range(4):
        part, width, masked, visible = score_rows(i)
        top = jnp.max(masked, axis=-1, keepdims=True)
        weights = jnp.where(visible, jnp.exp(masked - top), 0.0)
        total = jnp.sum(weights, axis=-1, keepdims=True)
        attf[part, :] = dot(weights.astype(bf16), heads[0:width, 256:384]) / total
        lse[part, :] = jnp.broadcast_to(top + jnp.log(total), (256, 128))

    for i in (0, 1):
        att[pl.ds(256 * i, 256), at(m, 128)] = attf[pl.ds(512 * i + 256 * c, 256), :].astype(bf16)
    att_copies = direct(att_view)
    both_on_plane(g_state, 0)
    both_on_plane(g_state, 1)
    up_pair = to_sibling(up_copies, up_own, up_cols)
    arrive(up_pair)

    for i in range(4):
        part, width, masked, visible = score_rows(i)
        probs = jnp.where(visible, jnp.exp(masked - lse[part, 0:1]), 0.0)
        up = heads[part, 384:512]
        delta = jnp.sum(up.astype(f32) * attf[part, :], axis=-1, keepdims=True)
        grads = (probs * (contract_cols(up, heads[0:width, 256:384]) - delta)).astype(bf16)
        dv_acc[0:width, :] += contract_rows(probs.astype(bf16), up)
        dk_acc[0:width, :] += contract_rows(grads, heads[part, 0:128])

        @pl.when(i % 2 == c)
        def _():
            here = pl.ds(256 * (i // 2), 256)
            back = dot(grads, heads[0:width, 128:256]) * scale
            pack[here, at(3 * m, 128)] = turned(back, cosr[here, :], -sinr[here, :]).astype(bf16)

    for i in (0, 1):
        part, here = pl.ds(512 * i + 256 * c, 256), pl.ds(256 * i, 256)
        key_back = turned(dk_acc[part, :] * scale, cosr[here, :], -sinr[here, :])
        pack[here, at(3 * m + 1, 128)] = key_back.astype(bf16)
        pack[here, at(3 * m + 2, 128)] = dv_acc[part, :].astype(bf16)
    att_relays = relay(att_copies, att_half)
    pack_copies = direct(pack_view)
    both_on_plane(g_state, 2)
    both_on_plane(g_state, 3)
    feed(x, 2, 2)
    arrive(x_relays)
    norm(flip4(m, 2), False)
    norm(flip4(m, 3), False)
    wd_load.wait()

    def feed_out(n):
        accg[:, at(n, 1024)] = contract_cols(act[mine, :], wd[at(n, 1024), :])

    loop(2, feed_out)
    arrive(att_relays)

    def finish_out(n):
        total = accg[:, at(n, 1024)] + contract_cols(att[mine, :], wo[at(n, 1024), :])
        for i in range(4):
            ob[i, n] = total[:, 256 * i : 256 * (i + 1)].astype(bf16)

    loop(2, finish_out)

    def scatter(src, dst):
        copies = [send(src.at[flip4(t, k)], dst.at[t], grid_peer(k)) for k in (3, 2, 1)]
        return copies, move(src.at[t], dst.at[t])

    def across(copies, kept, src, which):
        arrive(copies)
        kept.wait()
        sums = [sum(src[i, half].astype(f32) for i in range(4)) for half in (0, 1)]
        keep = jnp.where(b == 0, sums[0], sums[1])
        swap_b[which] = jnp.where(b == 0, sums[1], sums[0]).astype(bf16)
        return keep, send(swap_b.at[which], back_b.at[which], grid_peer(4))

    out_copies, out_own = scatter(ob, ro)

    def hidden(rows):
        def tile(n):
            cols = at(n, 512)
            hid[rows, cols] = (dot(cg[rows, :], wd[:, cols]) * gd[rows, cols].astype(f32)).astype(bf16)

        loop(4, tile)

    hidden(mine)

    def norm_grad(n, values, weight, which):
        cols = at(n, 1024)
        ng = contract_cols(values, weight[cols, :])
        usum[which : which + 1, cols] = jnp.sum(ng * xh[:, cols], axis=0, keepdims=True)
        usum[which + 2 : which + 3, cols] = jnp.sum(ng, axis=0, keepdims=True)
        return ng * rows2[which, 0:1, cols]

    def feed_grad(n):
        cols = at(n, 1024)
        accg[:, cols] = norm_grad(n, hid[mine, :], wu, 1)
        usum[6:7, cols] = jnp.sum(hid[mine, cols].astype(f32), axis=0, keepdims=True)
        usum[4:5, cols] = jnp.sum(cg[mine, cols].astype(f32), axis=0, keepdims=True)

    loop(2, feed_grad)
    pack_relays = relay(pack_copies, pack_half)
    feed(1 - x, 0, 4)
    arrive([g_state["plane"][k][1] for k in range(8)])
    g_relays = []
    for k in range(4):
        g_relays += plane_relay(g_state, k, True)
    def transpose_tokens(i):
        part = at(i, 128)
        for half in (0, 1):
            cols = pl.ds(256 * half, 256)
            features = at(4 * x + 2 * flip(c, half) + b, 256)
            hat = (xg[part, features].astype(f32) - mean_s[part, 0:1]) * inv_s[part, 0:1]
            for which, dst in ((0, n0t), (1, n1t)):
                low = hat * rows2[which, 0:1, features] + rows2[which, 1:2, features]
                dst[cols, part] = low.T.astype(bf16)

    loop(4, transpose_tokens)
    hidden(at(flip4(m, 1), 128))
    arrive(pack_relays)

    def attention_grad(n):
        accg[:, at(n, 1024)] += norm_grad(n, pack[mine, :], wp, 0)

    loop(2, attention_grad)
    usum[5:6, 0:1536] = jnp.sum(pack[mine, :].astype(f32), axis=0, keepdims=True)
    pair_copy = send(usum, pair, sibling())
    zero = jnp.zeros((128, 1), f32)

    def means(n, carry):
        g = accg[:, at(n, 256)]
        return (carry[0] + jnp.sum(g, axis=-1, keepdims=True),
                carry[1] + jnp.sum(g * xh[:, at(n, 256)], axis=-1, keepdims=True))

    mean, slope = lax.fori_loop(0, 8, means, (zero, zero))
    mean, slope = mean * (1.0 / 2048), slope * (1.0 / 2048)

    def finish_grad(n):
        gb[n % 4, n // 4] = (inv_s[mine, 0:1] * (accg[:, at(n, 256)] - mean - xh[:, at(n, 256)] * slope)).astype(bf16)

    loop(8, finish_grad)
    grad_copies, grad_own = scatter(gb, rg)
    writes, swaps = [], []

    def matrix(lhs, rhs, count, base):
        first, here = used["sem"], used["local"]
        used["sem"] += count
        used["local"] += count

        def swap(i):
            return pltpu.make_async_remote_copy(
                src_ref=other.at[base + i], dst_ref=came_o.at[base + i],
                send_sem=sems.at[0, first + i], recv_sem=sems.at[1, first + i],
                device_id=sibling(), device_id_type=MESH)

        def keep(i):
            return pltpu.make_async_copy(kept.at[base + i], kept_o.at[base + i], local.at[here + i])

        def produce(i):
            both = dot(lhs[...], rhs[:, at(i, 512)]).astype(bf16)
            other[base + i] = both[256:]
            swap(i).start()
            kept[base + i] = both[:256]
            keep(i).start()

        loop(count, produce)
        for i in range(count):
            writes.append(keep(i))
            swaps.append(swap(i))

    matrix(n0t, pack, 3, 9)
    arrive(g_relays)
    hidden(at(1 - x, 256))

    def transpose_grads(i):
        part = at(i, 128)
        for half in (0, 1):
            features = at(4 * x + 2 * flip(c, half) + b, 256)
            ct[pl.ds(256 * half, 256), part] = cg[part, features].astype(f32).T.astype(bf16)

    loop(4, transpose_grads)
    arrive([pair_copy])
    pair[...] += usum[...]
    near_copies = [send(pair, near.at[k - 1], plane_peer(k)) for k in (1, 2, 3)]
    matrix(ct, act, 4, 0)
    arrive(near_copies)
    sums_o[t] = pair[...] + near[0] + near[1] + near[2]
    sum_copies = [send(sums_o.at[t], sums_o.at[t], grid_peer(k)) for k in (1, 2, 3)]
    out_keep, out_swap = across(out_copies, out_own, ro, 0)
    matrix(n1t, hid, 4, 4)
    grad_keep, grad_swap = across(grad_copies, grad_own, rg, 1)
    matrix(ct, att, 1, 8)
    for copy in late:
        copy.wait()
    columns = at(j, 256)
    bias = rows2[0, 2:3, columns] + rows2[1, 2:3, columns]
    here, there = at(b, 128), at(1 - b, 128)
    layer_o[here, :] = (bias + tok_v[here, :].astype(f32) + out_keep).astype(bf16)
    arrive([out_swap])
    layer_o[there, :] = (bias + tok_v[there, :].astype(f32) + back_b[0].astype(f32)).astype(bf16)
    grad_o[here, :] = cot_v[here, :].astype(f32) + grad_keep
    arrive(sum_copies + [grad_swap])
    grad_o[there, :] = cot_v[there, :].astype(f32) + back_b[1].astype(f32)
    for copy in writes + swaps:
        copy.wait()
    for copy in sent:
        copy.wait_send()
    for copy in inner_sent:
        pl.when(inner)(copy.wait_send)
    assert used["sem"] <= 150 and used["local"] <= 40, used


def emit_kernel(layer, grad, kept, came, sums, layer_o, grad_o, project_o, output_o,
                up_o, down_o, offs_o, hidden_o, gain_o, center_o, residual_o):
    for out, base, count in ((down_o, 0, 4), (up_o, 4, 4), (output_o, 8, 1), (project_o, 9, 3)):
        for i in range(count):
            out[:, pl.ds(512 * i, 512)] = kept[base + i].astype(f32) + came[base + i].astype(f32)

    @pl.when(pl.program_id(0) == 0)
    def _():
        layer_o[...] = layer[...]
        grad_o[...] = grad[...]
        gain_o[...] = sums[0, 0:2] + sums[1, 0:2] + sums[2, 0:2] + sums[3, 0:2]
        center_o[...] = sums[0, 2:4] + sums[1, 2:4] + sums[2, 2:4] + sums[3, 2:4]
        residual_o[...] = jnp.broadcast_to(sums[0, 4:5], (2, 2048))
        for i in range(4):
            offs_o[pl.ds(1536 * i, 1536)] = sums[i, 5, 0:1536]
            hidden_o[pl.ds(2048 * i, 2048)] = sums[i, 6]


def fast_device(tokens, cotangent, documents, positions, project_weight, offsets, output_weight,
                up_weight, hidden_bias, down_weight, norm_gain, norm_bias, residual_bias):
    vmem, anywhere = pl.BlockSpec(memory_space=pltpu.VMEM), pl.BlockSpec(memory_space=pl.ANY)
    shape = jax.ShapeDtypeStruct
    low = lambda *size: pltpu.VMEM(size, bf16)
    full = lambda *size: pltpu.VMEM(size, f32)
    widths = (1536, 512, 2048, 2048)
    results = pl.pallas_call(
        layer_kernel,
        out_shape=[shape((256, 256), bf16), shape((256, 256), f32)]
        + [shape((12, 256, 512), bf16)] * 2 + [shape((4, 8, 2048), f32)],
        in_specs=[anywhere] * 12,
        out_specs=[vmem] * 2 + [anywhere] * 2 + [vmem],
        scratch_shapes=[
            low(2048, 1536), low(2048, 512), low(2048, 2048), low(2048, 2048),
            low(256, 256), low(256, 256), pltpu.VMEM((256,), jnp.int32), full(1, 2048), full(1, 2048),
            full(1, 2048), full(1536), full(2048),
            low(512, 2048), low(512, 2048), full(4, 8, 256), full(1024, 128), full(512, 128),
            full(512, 128), full(2, 8, 2048), full(128, 2048), full(512, 128), full(512, 128),
            low(128, 2048), low(256, 2048), GD(512, 2048), low(512, 2048), low(512, 2048),
            low(4, 128, 512), low(1024, 512), low(512, 512), low(512, 1536), full(1024, 128),
            full(1024, 128), full(1024, 128), full(1024, 128), low(4, 2, 128, 256),
            low(4, 2, 128, 256), low(4, 2, 128, 256), low(4, 2, 128, 256), low(2, 128, 256),
            low(2, 128, 256), full(128, 2048), low(512, 512), low(512, 512),
            low(512, 512), low(12, 256, 512),
            low(12, 256, 512), full(8, 2048), full(8, 2048), full(3, 8, 2048),
            pltpu.SemaphoreType.DMA((2, 150)), pltpu.SemaphoreType.DMA((40,))],
        compiler_params=pltpu.CompilerParams(
            collective_id=0, has_side_effects=True, vmem_limit_bytes=LIMIT),
    )(tokens, cotangent, positions, norm_gain, norm_bias, residual_bias,
      offsets, hidden_bias, project_weight, output_weight, up_weight, down_weight)
    steps = 2
    whole = lambda *size: pl.BlockSpec(size, lambda i: (0,) * len(size))
    band = lambda width: pl.BlockSpec((256 // steps, width), lambda i: (i, 0))
    layer_out, input_grad, *rest = pl.pallas_call(
        emit_kernel,
        grid=(steps,),
        out_shape=[shape((256, 256), bf16), shape((256, 256), f32)]
        + [shape((256, width), f32) for width in widths]
        + [shape((6144,), f32), shape((8192,), f32)] + [shape((2, 2048), f32)] * 3,
        in_specs=[whole(256, 256)] * 2
        + [pl.BlockSpec((12, 256 // steps, 512), lambda i: (0, i, 0))] * 2 + [whole(4, 8, 2048)],
        out_specs=[whole(256, 256)] * 2 + [band(width) for width in widths]
        + [whole(6144), whole(8192)] + [whole(2, 2048)] * 3,
        compiler_params=pltpu.CompilerParams(vmem_limit_bytes=LIMIT),
    )(*results)
    return (layer_out, input_grad, *rest)


LIMIT = 63 << 20
GD = lambda *size: pltpu.VMEM(size, bf16)


def solution(mesh):
    fits = (mesh.shape["seq"], mesh.shape["branch"], mesh.shape["tensor"]) == (4, 2, 4)
    return jax.shard_map(
        fast_device if fits else on_device,
        mesh=mesh,
        in_specs=(
            P("seq", ("branch", "tensor")),
            P("seq", ("branch", "tensor")),
            P("seq"),
            P("seq"),
            P(None, "tensor"),
            P("tensor"),
            P(None, "tensor"),
            P(None, "tensor"),
            P("tensor"),
            P(None, "tensor"),
            P("branch", None),
            P("branch", None),
            P("branch", None),
        ),
        out_specs=(
            P("seq", ("branch", "tensor")),
            P("seq", ("branch", "tensor")),
            P(("seq", "branch"), "tensor"),
            P(("seq", "branch"), "tensor"),
            P(("seq", "branch"), "tensor"),
            P(("seq", "branch"), "tensor"),
            P(),
            P(),
            P(),
            P(),
            P(),
        ),
        check_vma=False,
    )
```

```python
from functools import partial

import jax
import jax.numpy as jnp
from jax import lax
from jax.experimental import pallas as pl
from jax.experimental.pallas import tpu as pltpu
from jax.sharding import PartitionSpec as P

HEAD_DIM = 128
ROT = 32


norm_eps = 1e-05
rope_base = 10000.0
masked_score = -1e30


def passed_along(value, axis, steps):
    count = lax.axis_size(axis)
    pairs = [(source, (source + steps) % count) for source in range(count)]
    return lax.ppermute(value, axis, pairs)


def shifted(array, axis, by):
    count = lax.axis_size(axis)
    pairs = [(i, i + by) for i in range(count) if 0 <= i + by < count]
    return lax.ppermute(array, axis, pairs)


def layer_norm(values, gain_row, shift_row):
    average = jnp.mean(values, axis=-1, keepdims=True)
    centered = values - average
    variance = jnp.mean(centered * centered, axis=-1, keepdims=True)
    return centered * lax.rsqrt(variance + norm_eps) * gain_row + shift_row


def rope_tables(places):
    half_rot = ROT // 2
    frequency = rope_base ** (-(2.0 * jnp.arange(half_rot, dtype=jnp.float32)) / ROT)
    angles = places.astype(jnp.float32)[:, None] * frequency[None, :]
    return (jnp.cos(angles), jnp.sin(angles))


def rotate(values, cosine, sine_rows, direction):
    half_rot = ROT // 2
    first_half = values[..., :half_rot]
    second_half = values[..., half_rot:ROT]
    cos_table = cosine[:, None, :]
    sin_table = direction * sine_rows[:, None, :]
    return jnp.concatenate(
        [
            first_half * cos_table - second_half * sin_table,
            second_half * cos_table + first_half * sin_table,
            values[..., ROT:],
        ],
        axis=-1,
    )


def contract_rows(first_side, second_side):
    return lax.dot_general(
        first_side, second_side, (((0,), (0,)), ((), ())), preferred_element_type=jnp.float32
    )


def contract_cols(first_side, second_side):
    return lax.dot_general(
        first_side, second_side, (((1,), (1,)), ((), ())), preferred_element_type=jnp.float32
    )


def on_device(
    tokens,
    cotangent,
    documents,
    positions,
    project_weight,
    offsets,
    output_weight,
    up_weight,
    hidden_bias,
    down_weight,
    norm_gain,
    norm_bias,
    residual_bias,
):
    tok_rows = tokens.shape[0]
    model_width = up_weight.shape[0]
    attn_width = output_weight.shape[1]
    local_heads = attn_width // HEAD_DIM
    hidden_local = up_weight.shape[1]
    seq_count = lax.axis_size("seq")
    seq_index = lax.axis_index("seq")
    branch_index = lax.axis_index("branch")
    tensor_index = lax.axis_index("tensor")
    is_attention = branch_index == 0
    lead_tensor = tensor_index == 0
    score_scale = HEAD_DIM ** (-0.5)
    local_index = jnp.arange(tok_rows, dtype=jnp.int32)
    query_index = seq_index * tok_rows + local_index
    full_tokens, full_cotangent = (
        lax.all_gather(tokens, ("branch", "tensor"), axis=1, tiled=True),
        lax.all_gather(cotangent, ("branch", "tensor"), axis=1, tiled=True),
    )
    gain_row = norm_gain[0]
    shift_row = norm_bias[0]
    normed, norm_pullback = jax.vjp(
        layer_norm, full_tokens.astype(jnp.float32), gain_row, shift_row
    )
    normed_low = normed.astype(jnp.bfloat16)
    cosine, sine_rows = rope_tables(positions)
    zeros_heads = jnp.zeros((tok_rows, attn_width), jnp.bfloat16)
    zeros_hidden = jnp.zeros((tok_rows, hidden_local), jnp.float32)
    hidden_zero = jnp.zeros((tok_rows, hidden_local), jnp.bfloat16)
    zeros_stats = jnp.zeros((local_heads, tok_rows), jnp.float32)
    grad_zero = jnp.zeros((tok_rows, local_heads, HEAD_DIM), jnp.float32)

    def attention_front(unused):
        packed = jnp.dot(normed_low, project_weight, preferred_element_type=jnp.float32) + offsets
        packed = packed.reshape(tok_rows, local_heads, 3, HEAD_DIM)
        query_rot = rotate(packed[:, :, 0], cosine, sine_rows, 1.0).reshape(tok_rows, attn_width)
        key_rot = rotate(packed[:, :, 1], cosine, sine_rows, 1.0).reshape(tok_rows, attn_width)
        value_rows = packed[:, :, 2].reshape(tok_rows, attn_width)
        return (
            query_rot.astype(jnp.bfloat16),
            key_rot.astype(jnp.bfloat16),
            value_rows.astype(jnp.bfloat16),
            zeros_hidden,
            hidden_zero,
        )

    def feed_front(unused):
        up_rows = jnp.dot(normed_low, up_weight, preferred_element_type=jnp.float32) + hidden_bias
        active = jax.nn.gelu(up_rows, approximate=False).astype(jnp.bfloat16)
        return (zeros_heads, zeros_heads, zeros_heads, up_rows, active)

    query_low, key_low, value_low, up_rows, active = lax.cond(
        is_attention, attention_front, feed_front, 0
    )
    query_heads = query_low.reshape(tok_rows, local_heads, HEAD_DIM)

    def absorb(totals, key_rows, value_rows, key_ids, offset):
        key_count = key_rows.shape[0]
        key_index = offset + jnp.arange(key_count, dtype=jnp.int32)
        visible = (documents[:, None] == key_ids[None, :]) & (
            key_index[None, :] <= query_index[:, None]
        )

        def update(running):
            run_max, run_sum, run_acc = running
            scores = (
                jnp.einsum(
                    "qhd,khd->hqk",
                    query_heads,
                    key_rows.reshape(key_count, local_heads, HEAD_DIM),
                    preferred_element_type=jnp.float32,
                )
                * score_scale
            )
            masked = jnp.where(visible[None], scores, masked_score)
            new_max = jnp.maximum(run_max, jnp.max(masked, axis=-1))
            weights = jnp.where(visible[None], jnp.exp(masked - new_max[:, :, None]), 0.0)
            factor = jnp.exp(run_max - new_max)
            blended = jnp.einsum(
                "hqk,khd->qhd",
                weights.astype(jnp.bfloat16),
                value_rows.reshape(key_count, local_heads, HEAD_DIM),
                preferred_element_type=jnp.float32,
            )
            return (
                new_max,
                run_sum * factor + jnp.sum(weights, axis=-1),
                run_acc * factor.T[:, :, None] + blended,
            )

        def unchanged(running):
            return running

        return lax.cond(is_attention & jnp.any(visible), update, unchanged, totals)

    initial = (jnp.full((local_heads, tok_rows), masked_score, jnp.float32), zeros_stats, grad_zero)
    totals = initial
    key_rows = lax.all_gather(key_low, "seq", axis=0, tiled=True)
    value_rows = lax.all_gather(value_low, "seq", axis=0, tiled=True)
    key_ids = lax.all_gather(documents, "seq", axis=0, tiled=True)
    key_count = key_rows.shape[0]
    groups = key_count // tok_rows

    def absorb_group(running, sliced):
        return (absorb(running, sliced[0], sliced[1], sliced[2], sliced[3]), None)

    starts = tok_rows * jnp.arange(groups, dtype=jnp.int32)
    stacked = (
        key_rows.reshape(groups, tok_rows, attn_width),
        value_rows.reshape(groups, tok_rows, attn_width),
        key_ids.reshape(groups, tok_rows),
        starts,
    )
    totals, unused = lax.scan(absorb_group, totals, stacked)
    run_max, run_sum, run_acc = totals

    def attention_out(unused):
        attended = run_acc / run_sum.T[:, :, None]
        attended_low = attended.reshape(tok_rows, attn_width).astype(jnp.bfloat16)
        return (
            contract_cols(attended_low, output_weight),
            attended,
            attended_low,
            run_max + jnp.log(run_sum),
        )

    def feed_out(unused):
        return (contract_cols(active, down_weight), grad_zero, zeros_heads, zeros_stats)

    branch_out, attended, attended_low, lse_rows = lax.cond(
        is_attention, attention_out, feed_out, 0
    )
    branch_out = branch_out + jnp.where(lead_tensor, residual_bias[0], 0.0)
    summed = lax.psum_scatter(
        branch_out.astype(jnp.bfloat16), ("branch", "tensor"), scatter_dimension=1, tiled=True
    ).astype(jnp.float32)
    layer_out = (tokens.astype(jnp.float32) + summed).astype(jnp.bfloat16)

    def attention_prep(unused):
        grad_low = jnp.dot(
            full_cotangent, output_weight, preferred_element_type=jnp.float32
        ).astype(jnp.bfloat16)
        delta_rows = jnp.sum(
            grad_low.reshape(tok_rows, local_heads, HEAD_DIM).astype(jnp.float32) * attended,
            axis=-1,
        ).T
        return (grad_low, delta_rows, hidden_zero)

    def feed_prep(unused):
        active_grad = jnp.dot(full_cotangent, down_weight, preferred_element_type=jnp.float32)
        gelu_value, gelu_pullback = jax.vjp(partial(jax.nn.gelu, approximate=False), up_rows)
        return (zeros_heads, zeros_stats, gelu_pullback(active_grad)[0].astype(jnp.bfloat16))

    grad_low, delta_rows, hidden_low = lax.cond(is_attention, attention_prep, feed_prep, 0)

    def block_grads(
        query_rows,
        grad_rows,
        query_lse,
        query_delta,
        query_ids,
        query_place,
        key_rows,
        value_rows,
        key_ids,
        key_place,
    ):
        visible = (query_ids[:, None] == key_ids[None, :]) & (
            key_place[None, :] <= query_place[:, None]
        )

        def compute(unused):
            query_part_heads = query_rows.reshape(tok_rows, local_heads, HEAD_DIM)
            grad_heads = grad_rows.reshape(tok_rows, local_heads, HEAD_DIM)
            key_heads = key_rows.reshape(tok_rows, local_heads, HEAD_DIM)
            value_heads = value_rows.reshape(tok_rows, local_heads, HEAD_DIM)
            scores = (
                jnp.einsum(
                    "qhd,khd->hqk", query_part_heads, key_heads, preferred_element_type=jnp.float32
                )
                * score_scale
            )
            weights = jnp.exp(
                jnp.where(visible[None], scores - query_lse[:, :, None], masked_score)
            )
            value_part = jnp.einsum(
                "hqk,qhd->khd",
                weights.astype(jnp.bfloat16),
                grad_heads,
                preferred_element_type=jnp.float32,
            )
            weight_grad = jnp.einsum(
                "qhd,khd->hqk", grad_heads, value_heads, preferred_element_type=jnp.float32
            )
            score_grad = (weights * (weight_grad - query_delta[:, :, None])).astype(jnp.bfloat16)
            query_part = (
                jnp.einsum(
                    "hqk,khd->qhd", score_grad, key_heads, preferred_element_type=jnp.float32
                )
                * score_scale
            )
            key_part = (
                jnp.einsum(
                    "hqk,qhd->khd", score_grad, query_part_heads, preferred_element_type=jnp.float32
                )
                * score_scale
            )
            return (query_part, key_part, value_part)

        def nothing(unused):
            return (grad_zero, grad_zero, grad_zero)

        return lax.cond(is_attention & jnp.any(visible), compute, nothing, 0)

    def send_grads(key_acc, value_acc):
        return (
            passed_along(key_acc.astype(jnp.bfloat16), "seq", 1).astype(key_acc.dtype),
            passed_along(value_acc.astype(jnp.bfloat16), "seq", 1).astype(value_acc.dtype),
        )

    def key_step(cycle_state, unused):
        key_rows, value_rows, key_ids, key_acc, value_acc, hop_count, query_acc = cycle_state
        source = (seq_index - hop_count) % seq_count
        partial_terms = block_grads(
            query_low,
            grad_low,
            lse_rows,
            delta_rows,
            documents,
            query_index,
            key_rows,
            value_rows,
            key_ids,
            source * tok_rows + local_index,
        )
        key_rows, value_rows, key_ids = shifted((key_rows, value_rows, key_ids), "seq", 1)
        key_acc, value_acc = send_grads(key_acc + partial_terms[1], value_acc + partial_terms[2])
        return (
            (
                key_rows,
                value_rows,
                key_ids,
                key_acc,
                value_acc,
                hop_count + 1,
                query_acc + partial_terms[0],
            ),
            None,
        )

    start_state = (key_low, value_low, documents, grad_zero, grad_zero, jnp.int32(0), grad_zero)
    cycle_state, unused = lax.scan(key_step, start_state, None, length=seq_count - 1)
    key_rows, value_rows, key_ids, key_acc, value_acc, hop_count, query_acc = cycle_state
    source = (seq_index - hop_count) % seq_count
    partial_terms = block_grads(
        query_low,
        grad_low,
        lse_rows,
        delta_rows,
        documents,
        query_index,
        key_rows,
        value_rows,
        key_ids,
        source * tok_rows + local_index,
    )
    key_grad, value_grad = send_grads(key_acc + partial_terms[1], value_acc + partial_terms[2])
    query_grad = query_acc + partial_terms[0]

    def attention_tail(unused):
        query_back = rotate(query_grad, cosine, sine_rows, -1.0)
        key_back = rotate(key_grad, cosine, sine_rows, -1.0)
        packed_grad = (
            jnp.stack([query_back, key_back, value_grad], axis=2)
            .reshape(tok_rows, 3 * attn_width)
            .astype(jnp.bfloat16)
        )
        return (contract_cols(packed_grad, project_weight), packed_grad)

    def feed_tail(unused):
        return (
            contract_cols(hidden_low, up_weight),
            jnp.zeros((tok_rows, 3 * attn_width), jnp.bfloat16),
        )

    norm_grad, packed_grad = lax.cond(is_attention, attention_tail, feed_tail, 0)
    input_part, gain_part, shift_part = norm_pullback(norm_grad)
    input_grad = lax.psum_scatter(
        input_part.astype(jnp.bfloat16), ("branch", "tensor"), scatter_dimension=1, tiled=True
    ).astype(jnp.float32) + cotangent.astype(jnp.float32)

    def attention_rows(unused):
        return jnp.concatenate(
            [
                contract_rows(normed_low, packed_grad),
                contract_rows(full_cotangent, attended_low),
                jnp.zeros(
                    (
                        model_width
                        // (seq_count * lax.axis_size("branch"))
                        * lax.axis_size(("seq", "branch")),
                        2 * hidden_local,
                    ),
                    jnp.float32,
                ),
            ],
            axis=1,
        )

    def feed_rows(unused):
        return jnp.concatenate(
            [
                jnp.zeros(
                    (
                        model_width
                        // (seq_count * lax.axis_size("branch"))
                        * lax.axis_size(("seq", "branch")),
                        4 * attn_width,
                    ),
                    jnp.float32,
                ),
                contract_rows(normed_low, hidden_low),
                contract_rows(full_cotangent, active),
            ],
            axis=1,
        )

    shares = lax.psum_scatter(
        lax.cond(is_attention, attention_rows, feed_rows, 0).astype(jnp.bfloat16),
        ("seq", "branch"),
        scatter_dimension=0,
        tiled=True,
    ).astype(jnp.float32)
    project_grad = shares[:, : 3 * attn_width]
    output_grad = shares[:, 3 * attn_width : 4 * attn_width]
    up_grad = shares[:, 4 * attn_width : 4 * attn_width + hidden_local]
    down_grad = shares[:, 4 * attn_width + hidden_local :]
    offsets_part = lax.dynamic_update_slice(
        jnp.zeros((3 * model_width,), jnp.float32),
        jnp.sum(packed_grad, axis=0, dtype=jnp.float32),
        (tensor_index * (3 * attn_width),),
    )
    hidden_part = lax.dynamic_update_slice(
        jnp.zeros((hidden_local * lax.axis_size("tensor"),), jnp.float32),
        jnp.sum(hidden_low, axis=0, dtype=jnp.float32),
        (tensor_index * hidden_local,),
    )
    pair_zero = jnp.zeros((2, model_width), jnp.float32)
    gain_rows = lax.dynamic_update_slice(
        pair_zero, gain_part[None, :], (branch_index, jnp.int32(0))
    )
    shift_rows = lax.dynamic_update_slice(
        pair_zero, shift_part[None, :], (branch_index, jnp.int32(0))
    )
    column_sums = jnp.where(lead_tensor, jnp.sum(full_cotangent, axis=0, dtype=jnp.float32), 0.0)
    residual_rows = lax.dynamic_update_slice(
        pair_zero, column_sums[None, :], (branch_index, jnp.int32(0))
    )
    offsets_grad, hidden_grad, gain_grad, center_grad, residual_grad = lax.psum(
        (offsets_part, hidden_part, gain_rows, shift_rows, residual_rows),
        ("seq", "branch", "tensor"),
    )
    return (
        layer_out,
        input_grad,
        project_grad,
        output_grad,
        up_grad,
        down_grad,
        offsets_grad,
        hidden_grad,
        gain_grad,
        center_grad,
        residual_grad,
    )


MESH = pl.DeviceIdType.MESH
bf16, f32 = jnp.bfloat16, jnp.float32


def place():
    s, b, t = lax.axis_index("seq"), lax.axis_index("branch"), lax.axis_index("tensor")
    return s, b, t, s // 2, s % 2


def flip(value, bit):
    return value + bit - 2 * bit * value


def flip4(value, k):
    return 2 * flip(value // 2, k // 2) + flip(value % 2, k % 2)


def plane_peer(k):
    s, b, t, x, c = place()
    return (2 * flip(x, k // 2) + c, flip(b, k % 2), t)


def grid_peer(k):
    s, b, t, x, c = place()
    return (s, flip(b, k // 4), flip4(t, k % 4))


def sibling():
    s, b, t, x, c = place()
    return (flip4(s, 1), b, t)


def meet(devices):
    barrier = pltpu.get_barrier_semaphore()
    for device in devices:
        pl.semaphore_signal(barrier, inc=1, device_id=device, device_id_type=MESH)
    pl.semaphore_wait(barrier, len(devices))


def at(index, size):
    return pl.ds(pl.multiple_of(index * size, size), size)


def dot(first, second):
    return jnp.dot(first, second, preferred_element_type=f32)


def turned(values, cosine, sines):
    lane = lax.broadcasted_iota(jnp.int32, values.shape, 1)
    swapped = jnp.where(
        lane < ROT // 2,
        pltpu.roll(values, HEAD_DIM - ROT // 2, 1),
        pltpu.roll(values, ROT // 2, 1),
    )
    return values * cosine + sines * swapped


def layer_kernel(
    tok, cot, places_h, gain_h, shift_h, residual_h, offs_h, hbias_h, wp_h, wo_h, wu_h, wd_h,
    layer_o, grad_o, kept_o, came_o, sums_o,
    wp, wo, wu, wd, tok_v, cot_v, places, gain, shift, residual, offs, hbias, xg, cg, posr, starts, cosr, sinr, rows2, xh, mean_s, inv_s, n0, n1, gd, act, hid,
    hs, heads, att, pack, attf, lse, dk_acc, dv_acc, ob, ro, gb, rg, swap_b, back_b, accg,
    n0t, n1t, ct, other, kept, usum, pair, near, sems, local,
):
    s, b, t, x, c = place()
    m, j = 2 * x + b, 4 * b + t
    slot = 4 * x + 2 * c + b
    scale = HEAD_DIM ** -0.5
    mine = at(m, 128)
    used = {"sem": 0, "local": 0}
    sent, inner_sent = [], []
    inner = (t == 1) | (t == 2)

    def describe(src, dst, device, there=None):
        index = used["sem"]
        used["sem"] += 1
        return pltpu.make_async_remote_copy(
            src_ref=src, dst_ref=dst, send_sem=sems.at[0, index],
            recv_sem=sems.at[1, index if there is None else there],
            device_id=device, device_id_type=MESH)

    def send(src, dst, device):
        copy = describe(src, dst, device)
        copy.start()
        sent.append(copy)
        return copy

    def send_inner(src, dst, device, there=None):
        copy = describe(src, dst, device, there)
        pl.when(inner)(copy.start)
        inner_sent.append(copy)
        return copy

    def move(src, dst):
        index = used["local"]
        used["local"] += 1
        copy = pltpu.make_async_copy(src, dst, local.at[index])
        copy.start()
        return copy

    def arrive(copies):
        for copy in copies:
            copy.wait_recv()

    def direct(view):
        return [send(view(m), view(m), plane_peer(k)) for k in (2, 1)]

    def relay(copies, half):
        out = []
        for i, k in enumerate((2, 1)):
            copies[i].wait_recv()
            part = half(flip4(m, k), i)
            out.append(send(part, part, plane_peer(3 - k)))
        return out

    def loop(count, body):
        def step(i, carry):
            body(i)
            return carry
        lax.fori_loop(0, count, step, 0)

    def block(k):
        return at(4 * flip(b, k // 4) + flip4(t, k % 4), 256)

    def gather(src, dst):
        half, place = src.at[at(b, 128)], dst.at[mine, at(j, 256)]
        over = send(src.at[at(1 - b, 128)], dst.at[at(flip4(m, 1), 128), at(j, 256)], grid_peer(4))
        return {"over": over, "half": half, "place": place, "own": move(half, place), "dst": dst,
                "plane": {}}

    def gather_near(state):
        state["near"] = to_tensor(state["half"], state["place"])

    def to_tensor(src, dst):
        last = used["sem"]
        third = send_inner(src, dst, grid_peer(3))
        near = send(src, dst, grid_peer(1))
        return {2: send(src, dst, grid_peer(2)), 1: near, 3: third, "last": last}

    def on_plane(state, k):
        part = state["dst"].at[mine, block(k)]
        state["plane"][k] = [send(part, part, plane_peer(i)) for i in (2, 1)]

    def gather_over(state):
        state["own"].wait()
        state["over"].wait_recv()
        part = state["dst"].at[mine, block(4)]
        state["far"] = to_tensor(part, part)

    def gather_step(state, k):
        for which, first in (("near", 0), ("far", 4)):
            state[which][k].wait_recv()
            if k == 2:
                part = state["dst"].at[mine, block(first + 2)]
                send_inner(part, part, grid_peer(1), state[which]["last"])

    def both_on_plane(state, k):
        on_plane(state, k)
        on_plane(state, k + 4)

    def plane_relay(state, k, here=False):
        dst, plane = state["dst"], state["plane"]
        plane[k][0].wait_recv()
        part = dst.at[at(flip4(m, 2), 128), block(k)]
        first = send(part, part, plane_peer(1))
        if not here:
            plane[k + 4][1].wait_recv()
        part = dst.at[at(flip4(m, 1), 128), block(k)]
        return [first, send(part, part, plane_peer(2)), plane[k + 4][0]]

    meet([grid_peer(k) for k in (1, 2, 3, 4)] + [plane_peer(2), plane_peer(3)]
         + [(flip4(s, k), b, t) for k in (1, 3)])
    x_state = gather(tok, xg)
    gather_near(x_state)
    g_state = gather(cot, cg)
    small = [move(src, dst) for src, dst in (
        (places_h, places), (gain_h, gain), (shift_h, shift), (residual_h, residual),
        (offs_h, offs), (hbias_h, hbias))]
    wp_load, wu_load = move(wp_h, wp), move(wu_h, wu)
    wo_load, wd_load = move(wo_h, wo), move(wd_h, wd)
    late = [move(tok, tok_v), move(cot, cot_v)]
    for copy in small:
        copy.wait()
    rows2[b] = jnp.zeros((8, 2048), f32)
    rows2[b, 0:1, :] = gain[...]
    rows2[b, 1:2, :] = shift[...]
    rows2[b, 2:3, :] = residual[...]
    posr[s] = jnp.broadcast_to(places[...].astype(f32)[None, :], (8, 256))
    row_copy = send(rows2.at[b], rows2.at[b], grid_peer(4))
    place_copies = [send(posr.at[s], posr.at[s], (flip4(s, k), b, t)) for k in (1, 2, 3)]
    gather_over(x_state)
    both_on_plane(x_state, 0)
    usum[...] = jnp.zeros_like(usum)
    dk_acc[...] = jnp.zeros_like(dk_acc)
    dv_acc[...] = jnp.zeros_like(dv_acc)
    arrive(place_copies)
    for i in range(4):
        row = jnp.broadcast_to(posr[i, 0:1, :], (128, 256))
        index = (256 * i + lax.broadcasted_iota(jnp.int32, (256, 128), 0)).astype(f32)
        starts[pl.ds(256 * i, 256), :] = index - row.T
    line = lax.broadcasted_iota(jnp.int32, (ROT, 256), 0)
    waves = jnp.zeros((ROT, 256), f32)
    for i in range(ROT // 2):
        waves = jnp.where(line % (ROT // 2) == i, rope_base ** (-2.0 * i / ROT), waves)
    for i in (0, 1):
        angle = posr[2 * i + c, 0:1, :] * waves
        part = pl.ds(256 * i, 256)
        sign = jnp.where(line < ROT // 2, -1.0, 1.0)
        rest = jnp.zeros((HEAD_DIM - ROT, 256), f32)
        cosr[part, :] = jnp.concatenate([jnp.cos(angle), rest + 1.0], axis=0).T
        sinr[part, :] = jnp.concatenate([jnp.sin(angle) * sign, rest], axis=0).T
    for k in (1, 2, 3):
        gather_step(x_state, k)
        both_on_plane(x_state, k)
        if k == 2:
            gather_near(g_state)
            gather_over(g_state)
    arrive([row_copy])

    def norm(which, whole):
        def rows(i):
            part = pl.ds(pl.multiple_of(which * 128 + 32 * i, 32), 32)
            v = xg[part, :].astype(f32)
            mean = jnp.mean(v, axis=-1, keepdims=True)
            centered = v - mean
            inverse = lax.rsqrt(jnp.mean(centered * centered, axis=-1, keepdims=True) + norm_eps)
            hat = centered * inverse
            mean_s[part, :] = jnp.broadcast_to(mean, (32, 128))
            inv_s[part, :] = jnp.broadcast_to(inverse, (32, 128))
            n1_part = pl.ds(pl.multiple_of((which % 2) * 128 + 32 * i, 32), 32)
            n1[n1_part, :] = (hat * rows2[1, 0:1, :] + rows2[1, 1:2, :]).astype(bf16)
            if whole:
                xh[at(i, 32), :] = hat
                n0[at(i, 32), :] = (hat * rows2[0, 0:1, :] + rows2[0, 1:2, :]).astype(bf16)

        loop(4, rows)

    norm(m, True)
    x_relays = []
    for k in (0, 1, 2):
        x_relays += plane_relay(x_state, k)
    wp_load.wait()
    turn = pl.ds(pl.multiple_of(256 * x + 128 * b, 128), 128)

    def project(n):
        both = dot(n0[...], wp[:, at(n, 768)]) + offs[at(n, 768)][None, :]
        for i in (0, 1):
            h, p = 2 * n + i, both[:, 384 * i : 384 * (i + 1)]
            hs[h, :, 0:128] = turned(p[:, 0:128], cosr[turn, :], sinr[turn, :]).astype(bf16)
            hs[h, :, 128:256] = turned(p[:, 128:256], cosr[turn, :], sinr[turn, :]).astype(bf16)
            hs[h, :, 256:384] = p[:, 256:384].astype(bf16)

    loop(2, project)

    def to_heads(cols):
        copies = [send(hs.at[flip4(m, k), :, cols], heads.at[at(slot, 128), cols], plane_peer(k))
                  for k in (3, 2, 1)]
        return copies, move(hs.at[m, :, cols], heads.at[at(slot, 128), cols])

    def to_sibling(copies, kept, cols):
        arrive(copies)
        kept.wait()
        parts = [heads.at[pl.ds(512 * i + 256 * c, 256), cols] for i in (0, 1)]
        return [send(part, part, sibling()) for part in parts]

    qkv_cols, up_cols = pl.ds(0, 384), pl.ds(384, 128)
    qkv_copies, qkv_own = to_heads(qkv_cols)
    x_relays += plane_relay(x_state, 3)
    gather_step(g_state, 1)
    arrive([x_state["plane"][k][1] for k in range(4)])
    norm(flip4(m, 1), False)
    gather_step(g_state, 2)
    wu_load.wait()

    def feed(pair_index, first, count):
        rows = at(pair_index, 256)

        def tile(n):
            cols = at(first + n, 512)
            u = dot(n1[...], wu[:, cols]) + hbias[cols][None, :]
            phi = 0.5 + 0.5 * lax.erf(u * 0.7071067811865476)
            act[rows, cols] = (u * phi).astype(bf16)
            gd[rows, cols] = (phi + u * (0.3989422804014327 * jnp.exp(-0.5 * u * u))).astype(gd.dtype)

        loop(count, tile)

    feed(x, 0, 2)
    qkv_pair = to_sibling(qkv_copies, qkv_own, qkv_cols)
    att_view = lambda i: att.at[:, at(i, 128)]
    att_half = lambda i, h: att.at[pl.ds(256 * h, 256), at(i, 128)]
    pack_view = lambda i: pack.at[:, at(i, 384)]
    pack_half = lambda i, h: pack.at[pl.ds(256 * h, 256), at(i, 384)]

    def score_rows(i):
        width = 256 * (i + 1)
        part = pl.ds(256 * i, 256)
        scores = contract_cols(heads[part, 0:128], heads[0:width, 128:256]) * scale
        query = (256 * i + lax.broadcasted_iota(jnp.int32, (256, 1), 0)).astype(f32)
        key = lax.broadcasted_iota(jnp.int32, (256, width), 1).astype(f32)
        visible = (key <= query) & (key >= starts[part, 0:1])
        return part, width, jnp.where(visible, scores, masked_score), visible

    gather_step(g_state, 3)
    wo_load.wait()

    head_low = dot(cg[mine, :], wo[...]).astype(bf16)
    for h in range(4):
        hs[h, :, 384:512] = head_low[:, 128 * h : 128 * (h + 1)]
    up_copies, up_own = to_heads(up_cols)
    arrive(qkv_pair)
    for i in range(4):
        part, width, masked, visible = score_rows(i)
        top = jnp.max(masked, axis=-1, keepdims=True)
        weights = jnp.where(visible, jnp.exp(masked - top), 0.0)
        total = jnp.sum(weights, axis=-1, keepdims=True)
        attf[part, :] = dot(weights.astype(bf16), heads[0:width, 256:384]) / total
        lse[part, :] = jnp.broadcast_to(top + jnp.log(total), (256, 128))

    for i in (0, 1):
        att[pl.ds(256 * i, 256), at(m, 128)] = attf[pl.ds(512 * i + 256 * c, 256), :].astype(bf16)
    att_copies = direct(att_view)
    both_on_plane(g_state, 0)
    both_on_plane(g_state, 1)
    up_pair = to_sibling(up_copies, up_own, up_cols)
    arrive(up_pair)

    for i in range(4):
        part, width, masked, visible = score_rows(i)
        probs = jnp.where(visible, jnp.exp(masked - lse[part, 0:1]), 0.0)
        up = heads[part, 384:512]
        delta = jnp.sum(up.astype(f32) * attf[part, :], axis=-1, keepdims=True)
        grads = (probs * (contract_cols(up, heads[0:width, 256:384]) - delta)).astype(bf16)
        dv_acc[0:width, :] += contract_rows(probs.astype(bf16), up)
        dk_acc[0:width, :] += contract_rows(grads, heads[part, 0:128])

        @pl.when(i % 2 == c)
        def _():
            here = pl.ds(256 * (i // 2), 256)
            back = dot(grads, heads[0:width, 128:256]) * scale
            pack[here, at(3 * m, 128)] = turned(back, cosr[here, :], -sinr[here, :]).astype(bf16)

    for i in (0, 1):
        part, here = pl.ds(512 * i + 256 * c, 256), pl.ds(256 * i, 256)
        key_back = turned(dk_acc[part, :] * scale, cosr[here, :], -sinr[here, :])
        pack[here, at(3 * m + 1, 128)] = key_back.astype(bf16)
        pack[here, at(3 * m + 2, 128)] = dv_acc[part, :].astype(bf16)
    att_relays = relay(att_copies, att_half)
    pack_copies = direct(pack_view)
    both_on_plane(g_state, 2)
    both_on_plane(g_state, 3)
    feed(x, 2, 2)
    arrive(x_relays)
    norm(flip4(m, 2), False)
    norm(flip4(m, 3), False)
    wd_load.wait()

    def feed_out(n):
        accg[:, at(n, 1024)] = contract_cols(act[mine, :], wd[at(n, 1024), :])

    loop(2, feed_out)
    arrive(att_relays)

    def finish_out(n):
        total = accg[:, at(n, 1024)] + contract_cols(att[mine, :], wo[at(n, 1024), :])
        for i in range(4):
            ob[i, n] = total[:, 256 * i : 256 * (i + 1)].astype(bf16)

    loop(2, finish_out)

    def scatter(src, dst):
        copies = [send(src.at[flip4(t, k)], dst.at[t], grid_peer(k)) for k in (3, 2, 1)]
        return copies, move(src.at[t], dst.at[t])

    def across(copies, kept, src, which):
        arrive(copies)
        kept.wait()
        sums = [sum(src[i, half].astype(f32) for i in range(4)) for half in (0, 1)]
        keep = jnp.where(b == 0, sums[0], sums[1])
        swap_b[which] = jnp.where(b == 0, sums[1], sums[0]).astype(bf16)
        return keep, send(swap_b.at[which], back_b.at[which], grid_peer(4))

    out_copies, out_own = scatter(ob, ro)

    def hidden(rows, width=512):
        def tile(n):
            cols = at(n, width)
            hid[rows, cols] = (dot(cg[rows, :], wd[:, cols]) * gd[rows, cols].astype(f32)).astype(bf16)

        loop(2048 // width, tile)

    hidden(mine, 1024)

    def norm_grad(n, values, weight, which):
        cols = at(n, 1024)
        ng = contract_cols(values, weight[cols, :])
        usum[which : which + 1, cols] = jnp.sum(ng * xh[:, cols], axis=0, keepdims=True)
        usum[which + 2 : which + 3, cols] = jnp.sum(ng, axis=0, keepdims=True)
        return ng * rows2[which, 0:1, cols]

    def feed_grad(n):
        cols = at(n, 1024)
        accg[:, cols] = norm_grad(n, hid[mine, :], wu, 1)
        usum[6:7, cols] = jnp.sum(hid[mine, cols].astype(f32), axis=0, keepdims=True)
        usum[4:5, cols] = jnp.sum(cg[mine, cols].astype(f32), axis=0, keepdims=True)

    loop(2, feed_grad)
    pack_relays = relay(pack_copies, pack_half)
    feed(1 - x, 0, 4)
    def transpose_tokens(i):
        part = at(i, 128)
        for half in (0, 1):
            cols = pl.ds(256 * half, 256)
            features = at(4 * x + 2 * flip(c, half) + b, 256)
            hat = (xg[part, features].astype(f32) - mean_s[part, 0:1]) * inv_s[part, 0:1]
            for which, dst in ((0, n0t), (1, n1t)):
                low = hat * rows2[which, 0:1, features] + rows2[which, 1:2, features]
                dst[cols, part] = low.T.astype(bf16)

    loop(4, transpose_tokens)
    arrive([g_state["plane"][k][1] for k in range(8)])
    g_relays = []
    for k in range(4):
        g_relays += plane_relay(g_state, k, True)
    hidden(at(flip4(m, 1), 128), 1024)
    arrive(pack_relays)

    def attention_grad(n):
        accg[:, at(n, 1024)] += norm_grad(n, pack[mine, :], wp, 0)

    loop(2, attention_grad)
    usum[5:6, 0:1536] = jnp.sum(pack[mine, :].astype(f32), axis=0, keepdims=True)
    pair_copy = send(usum, pair, sibling())
    zero = jnp.zeros((128, 1), f32)

    def means(n, carry):
        g = accg[:, at(n, 256)]
        return (carry[0] + jnp.sum(g, axis=-1, keepdims=True),
                carry[1] + jnp.sum(g * xh[:, at(n, 256)], axis=-1, keepdims=True))

    mean, slope = lax.fori_loop(0, 8, means, (zero, zero))
    mean, slope = mean * (1.0 / 2048), slope * (1.0 / 2048)

    def finish_grad(n):
        gb[n % 4, n // 4] = (inv_s[mine, 0:1] * (accg[:, at(n, 256)] - mean - xh[:, at(n, 256)] * slope)).astype(bf16)

    loop(8, finish_grad)
    grad_copies, grad_own = scatter(gb, rg)
    writes, swaps = [], []

    def matrix(lhs, rhs, count, base):
        first, here = used["sem"], used["local"]
        used["sem"] += count
        used["local"] += count

        def swap(i):
            return pltpu.make_async_remote_copy(
                src_ref=other.at[base + i], dst_ref=came_o.at[base + i],
                send_sem=sems.at[0, first + i], recv_sem=sems.at[1, first + i],
                device_id=sibling(), device_id_type=MESH)

        def keep(i):
            return pltpu.make_async_copy(kept.at[base + i], kept_o.at[base + i], local.at[here + i])

        def produce(i):
            both = dot(lhs[...], rhs[:, at(i, 512)]).astype(bf16)
            other[base + i] = both[256:]
            swap(i).start()
            kept[base + i] = both[:256]
            keep(i).start()

        loop(count, produce)
        for i in range(count):
            writes.append(keep(i))
            swaps.append(swap(i))

    matrix(n0t, pack, 3, 9)
    arrive(g_relays)
    hidden(at(1 - x, 256))

    def transpose_grads(i):
        part = at(i, 128)
        for half in (0, 1):
            features = at(4 * x + 2 * flip(c, half) + b, 256)
            ct[pl.ds(256 * half, 256), part] = cg[part, features].astype(f32).T.astype(bf16)

    loop(4, transpose_grads)
    arrive([pair_copy])
    pair[...] += usum[...]
    near_copies = [send(pair, near.at[k - 1], plane_peer(k)) for k in (1, 2, 3)]
    matrix(ct, act, 4, 0)
    arrive(near_copies)
    sums_o[t] = pair[...] + near[0] + near[1] + near[2]
    sum_copies = [send(sums_o.at[t], sums_o.at[t], grid_peer(k)) for k in (1, 2, 3)]
    out_keep, out_swap = across(out_copies, out_own, ro, 0)
    matrix(n1t, hid, 4, 4)
    grad_keep, grad_swap = across(grad_copies, grad_own, rg, 1)
    matrix(ct, att, 1, 8)
    for copy in late:
        copy.wait()
    columns = at(j, 256)
    bias = rows2[0, 2:3, columns] + rows2[1, 2:3, columns]
    here, there = at(b, 128), at(1 - b, 128)
    layer_o[here, :] = (bias + tok_v[here, :].astype(f32) + out_keep).astype(bf16)
    arrive([out_swap])
    layer_o[there, :] = (bias + tok_v[there, :].astype(f32) + back_b[0].astype(f32)).astype(bf16)
    grad_o[here, :] = cot_v[here, :].astype(f32) + grad_keep
    arrive(sum_copies + [grad_swap])
    grad_o[there, :] = cot_v[there, :].astype(f32) + back_b[1].astype(f32)
    for copy in writes + swaps:
        copy.wait()
    for copy in sent:
        copy.wait_send()
    for copy in inner_sent:
        pl.when(inner)(copy.wait_send)
    assert used["sem"] <= 150 and used["local"] <= 40, used


def emit_kernel(layer, grad, kept, came, sums, layer_o, grad_o, project_o, output_o,
                up_o, down_o, offs_o, hidden_o, gain_o, center_o, residual_o):
    for out, base, count in ((down_o, 0, 4), (up_o, 4, 4), (output_o, 8, 1), (project_o, 9, 3)):
        for i in range(count):
            out[:, pl.ds(512 * i, 512)] = kept[base + i].astype(f32) + came[base + i].astype(f32)

    @pl.when(pl.program_id(0) == 0)
    def _():
        layer_o[...] = layer[...]
        grad_o[...] = grad[...]
        gain_o[...] = sums[0, 0:2] + sums[1, 0:2] + sums[2, 0:2] + sums[3, 0:2]
        center_o[...] = sums[0, 2:4] + sums[1, 2:4] + sums[2, 2:4] + sums[3, 2:4]
        residual_o[...] = jnp.broadcast_to(sums[0, 4:5], (2, 2048))
        for i in range(4):
            offs_o[pl.ds(1536 * i, 1536)] = sums[i, 5, 0:1536]
            hidden_o[pl.ds(2048 * i, 2048)] = sums[i, 6]


def fast_device(tokens, cotangent, documents, positions, project_weight, offsets, output_weight,
                up_weight, hidden_bias, down_weight, norm_gain, norm_bias, residual_bias):
    vmem, anywhere = pl.BlockSpec(memory_space=pltpu.VMEM), pl.BlockSpec(memory_space=pl.ANY)
    shape = jax.ShapeDtypeStruct
    low = lambda *size: pltpu.VMEM(size, bf16)
    full = lambda *size: pltpu.VMEM(size, f32)
    widths = (1536, 512, 2048, 2048)
    results = pl.pallas_call(
        layer_kernel,
        out_shape=[shape((256, 256), bf16), shape((256, 256), f32)]
        + [shape((12, 256, 512), bf16)] * 2 + [shape((4, 8, 2048), f32)],
        in_specs=[anywhere] * 12,
        out_specs=[vmem] * 2 + [anywhere] * 2 + [vmem],
        scratch_shapes=[
            low(2048, 1536), low(2048, 512), low(2048, 2048), low(2048, 2048),
            low(256, 256), low(256, 256), pltpu.VMEM((256,), jnp.int32), full(1, 2048), full(1, 2048),
            full(1, 2048), full(1536), full(2048),
            low(512, 2048), low(512, 2048), full(4, 8, 256), full(1024, 128), full(512, 128),
            full(512, 128), full(2, 8, 2048), full(128, 2048), full(512, 128), full(512, 128),
            low(128, 2048), low(256, 2048), GD(512, 2048), low(512, 2048), low(512, 2048),
            low(4, 128, 512), low(1024, 512), low(512, 512), low(512, 1536), full(1024, 128),
            full(1024, 128), full(1024, 128), full(1024, 128), low(4, 2, 128, 256),
            low(4, 2, 128, 256), low(4, 2, 128, 256), low(4, 2, 128, 256), low(2, 128, 256),
            low(2, 128, 256), full(128, 2048), low(512, 512), low(512, 512),
            low(512, 512), low(12, 256, 512),
            low(12, 256, 512), full(8, 2048), full(8, 2048), full(3, 8, 2048),
            pltpu.SemaphoreType.DMA((2, 150)), pltpu.SemaphoreType.DMA((40,))],
        compiler_params=pltpu.CompilerParams(
            collective_id=0, has_side_effects=True, vmem_limit_bytes=LIMIT),
    )(tokens, cotangent, positions, norm_gain, norm_bias, residual_bias,
      offsets, hidden_bias, project_weight, output_weight, up_weight, down_weight)
    steps = 2
    whole = lambda *size: pl.BlockSpec(size, lambda i: (0,) * len(size))
    band = lambda width: pl.BlockSpec((256 // steps, width), lambda i: (i, 0))
    layer_out, input_grad, *rest = pl.pallas_call(
        emit_kernel,
        grid=(steps,),
        out_shape=[shape((256, 256), bf16), shape((256, 256), f32)]
        + [shape((256, width), f32) for width in widths]
        + [shape((6144,), f32), shape((8192,), f32)] + [shape((2, 2048), f32)] * 3,
        in_specs=[whole(256, 256)] * 2
        + [pl.BlockSpec((12, 256 // steps, 512), lambda i: (0, i, 0))] * 2 + [whole(4, 8, 2048)],
        out_specs=[whole(256, 256)] * 2 + [band(width) for width in widths]
        + [whole(6144), whole(8192)] + [whole(2, 2048)] * 3,
        compiler_params=pltpu.CompilerParams(vmem_limit_bytes=LIMIT),
    )(*results)
    return (layer_out, input_grad, *rest)


LIMIT = 63 << 20
GD = lambda *size: pltpu.VMEM(size, bf16)


def solution(mesh):
    fits = (mesh.shape["seq"], mesh.shape["branch"], mesh.shape["tensor"]) == (4, 2, 4)
    return jax.shard_map(
        fast_device if fits else on_device,
        mesh=mesh,
        in_specs=(
            P("seq", ("branch", "tensor")),
            P("seq", ("branch", "tensor")),
            P("seq"),
            P("seq"),
            P(None, "tensor"),
            P("tensor"),
            P(None, "tensor"),
            P(None, "tensor"),
            P("tensor"),
            P(None, "tensor"),
            P("branch", None),
            P("branch", None),
            P("branch", None),
        ),
        out_specs=(
            P("seq", ("branch", "tensor")),
            P("seq", ("branch", "tensor")),
            P(("seq", "branch"), "tensor"),
            P(("seq", "branch"), "tensor"),
            P(("seq", "branch"), "tensor"),
            P(("seq", "branch"), "tensor"),
            P(),
            P(),
            P(),
            P(),
            P(),
        ),
        check_vma=False,
    )
```

```python
from functools import partial

import jax
import jax.numpy as jnp
from jax import lax
from jax.experimental import pallas as pl
from jax.experimental.pallas import tpu as pltpu
from jax.sharding import PartitionSpec as P

HEAD_DIM = 128
ROT = 32


norm_eps = 1e-05
rope_base = 10000.0
masked_score = -1e30


def passed_along(value, axis, steps):
    count = lax.axis_size(axis)
    pairs = [(source, (source + steps) % count) for source in range(count)]
    return lax.ppermute(value, axis, pairs)


def shifted(array, axis, by):
    count = lax.axis_size(axis)
    pairs = [(i, i + by) for i in range(count) if 0 <= i + by < count]
    return lax.ppermute(array, axis, pairs)


def layer_norm(values, gain_row, shift_row):
    average = jnp.mean(values, axis=-1, keepdims=True)
    centered = values - average
    variance = jnp.mean(centered * centered, axis=-1, keepdims=True)
    return centered * lax.rsqrt(variance + norm_eps) * gain_row + shift_row


def rope_tables(places):
    half_rot = ROT // 2
    frequency = rope_base ** (-(2.0 * jnp.arange(half_rot, dtype=jnp.float32)) / ROT)
    angles = places.astype(jnp.float32)[:, None] * frequency[None, :]
    return (jnp.cos(angles), jnp.sin(angles))


def rotate(values, cosine, sine_rows, direction):
    half_rot = ROT // 2
    first_half = values[..., :half_rot]
    second_half = values[..., half_rot:ROT]
    cos_table = cosine[:, None, :]
    sin_table = direction * sine_rows[:, None, :]
    return jnp.concatenate(
        [
            first_half * cos_table - second_half * sin_table,
            second_half * cos_table + first_half * sin_table,
            values[..., ROT:],
        ],
        axis=-1,
    )


def contract_rows(first_side, second_side):
    return lax.dot_general(
        first_side, second_side, (((0,), (0,)), ((), ())), preferred_element_type=jnp.float32
    )


def contract_cols(first_side, second_side):
    return lax.dot_general(
        first_side, second_side, (((1,), (1,)), ((), ())), preferred_element_type=jnp.float32
    )


def on_device(
    tokens,
    cotangent,
    documents,
    positions,
    project_weight,
    offsets,
    output_weight,
    up_weight,
    hidden_bias,
    down_weight,
    norm_gain,
    norm_bias,
    residual_bias,
):
    tok_rows = tokens.shape[0]
    model_width = up_weight.shape[0]
    attn_width = output_weight.shape[1]
    local_heads = attn_width // HEAD_DIM
    hidden_local = up_weight.shape[1]
    seq_count = lax.axis_size("seq")
    seq_index = lax.axis_index("seq")
    branch_index = lax.axis_index("branch")
    tensor_index = lax.axis_index("tensor")
    is_attention = branch_index == 0
    lead_tensor = tensor_index == 0
    score_scale = HEAD_DIM ** (-0.5)
    local_index = jnp.arange(tok_rows, dtype=jnp.int32)
    query_index = seq_index * tok_rows + local_index
    full_tokens, full_cotangent = (
        lax.all_gather(tokens, ("branch", "tensor"), axis=1, tiled=True),
        lax.all_gather(cotangent, ("branch", "tensor"), axis=1, tiled=True),
    )
    gain_row = norm_gain[0]
    shift_row = norm_bias[0]
    normed, norm_pullback = jax.vjp(
        layer_norm, full_tokens.astype(jnp.float32), gain_row, shift_row
    )
    normed_low = normed.astype(jnp.bfloat16)
    cosine, sine_rows = rope_tables(positions)
    zeros_heads = jnp.zeros((tok_rows, attn_width), jnp.bfloat16)
    zeros_hidden = jnp.zeros((tok_rows, hidden_local), jnp.float32)
    hidden_zero = jnp.zeros((tok_rows, hidden_local), jnp.bfloat16)
    zeros_stats = jnp.zeros((local_heads, tok_rows), jnp.float32)
    grad_zero = jnp.zeros((tok_rows, local_heads, HEAD_DIM), jnp.float32)

    def attention_front(unused):
        packed = jnp.dot(normed_low, project_weight, preferred_element_type=jnp.float32) + offsets
        packed = packed.reshape(tok_rows, local_heads, 3, HEAD_DIM)
        query_rot = rotate(packed[:, :, 0], cosine, sine_rows, 1.0).reshape(tok_rows, attn_width)
        key_rot = rotate(packed[:, :, 1], cosine, sine_rows, 1.0).reshape(tok_rows, attn_width)
        value_rows = packed[:, :, 2].reshape(tok_rows, attn_width)
        return (
            query_rot.astype(jnp.bfloat16),
            key_rot.astype(jnp.bfloat16),
            value_rows.astype(jnp.bfloat16),
            zeros_hidden,
            hidden_zero,
        )

    def feed_front(unused):
        up_rows = jnp.dot(normed_low, up_weight, preferred_element_type=jnp.float32) + hidden_bias
        active = jax.nn.gelu(up_rows, approximate=False).astype(jnp.bfloat16)
        return (zeros_heads, zeros_heads, zeros_heads, up_rows, active)

    query_low, key_low, value_low, up_rows, active = lax.cond(
        is_attention, attention_front, feed_front, 0
    )
    query_heads = query_low.reshape(tok_rows, local_heads, HEAD_DIM)

    def absorb(totals, key_rows, value_rows, key_ids, offset):
        key_count = key_rows.shape[0]
        key_index = offset + jnp.arange(key_count, dtype=jnp.int32)
        visible = (documents[:, None] == key_ids[None, :]) & (
            key_index[None, :] <= query_index[:, None]
        )

        def update(running):
            run_max, run_sum, run_acc = running
            scores = (
                jnp.einsum(
                    "qhd,khd->hqk",
                    query_heads,
                    key_rows.reshape(key_count, local_heads, HEAD_DIM),
                    preferred_element_type=jnp.float32,
                )
                * score_scale
            )
            masked = jnp.where(visible[None], scores, masked_score)
            new_max = jnp.maximum(run_max, jnp.max(masked, axis=-1))
            weights = jnp.where(visible[None], jnp.exp(masked - new_max[:, :, None]), 0.0)
            factor = jnp.exp(run_max - new_max)
            blended = jnp.einsum(
                "hqk,khd->qhd",
                weights.astype(jnp.bfloat16),
                value_rows.reshape(key_count, local_heads, HEAD_DIM),
                preferred_element_type=jnp.float32,
            )
            return (
                new_max,
                run_sum * factor + jnp.sum(weights, axis=-1),
                run_acc * factor.T[:, :, None] + blended,
            )

        def unchanged(running):
            return running

        return lax.cond(is_attention & jnp.any(visible), update, unchanged, totals)

    initial = (jnp.full((local_heads, tok_rows), masked_score, jnp.float32), zeros_stats, grad_zero)
    totals = initial
    key_rows = lax.all_gather(key_low, "seq", axis=0, tiled=True)
    value_rows = lax.all_gather(value_low, "seq", axis=0, tiled=True)
    key_ids = lax.all_gather(documents, "seq", axis=0, tiled=True)
    key_count = key_rows.shape[0]
    groups = key_count // tok_rows

    def absorb_group(running, sliced):
        return (absorb(running, sliced[0], sliced[1], sliced[2], sliced[3]), None)

    starts = tok_rows * jnp.arange(groups, dtype=jnp.int32)
    stacked = (
        key_rows.reshape(groups, tok_rows, attn_width),
        value_rows.reshape(groups, tok_rows, attn_width),
        key_ids.reshape(groups, tok_rows),
        starts,
    )
    totals, unused = lax.scan(absorb_group, totals, stacked)
    run_max, run_sum, run_acc = totals

    def attention_out(unused):
        attended = run_acc / run_sum.T[:, :, None]
        attended_low = attended.reshape(tok_rows, attn_width).astype(jnp.bfloat16)
        return (
            contract_cols(attended_low, output_weight),
            attended,
            attended_low,
            run_max + jnp.log(run_sum),
        )

    def feed_out(unused):
        return (contract_cols(active, down_weight), grad_zero, zeros_heads, zeros_stats)

    branch_out, attended, attended_low, lse_rows = lax.cond(
        is_attention, attention_out, feed_out, 0
    )
    branch_out = branch_out + jnp.where(lead_tensor, residual_bias[0], 0.0)
    summed = lax.psum_scatter(
        branch_out.astype(jnp.bfloat16), ("branch", "tensor"), scatter_dimension=1, tiled=True
    ).astype(jnp.float32)
    layer_out = (tokens.astype(jnp.float32) + summed).astype(jnp.bfloat16)

    def attention_prep(unused):
        grad_low = jnp.dot(
            full_cotangent, output_weight, preferred_element_type=jnp.float32
        ).astype(jnp.bfloat16)
        delta_rows = jnp.sum(
            grad_low.reshape(tok_rows, local_heads, HEAD_DIM).astype(jnp.float32) * attended,
            axis=-1,
        ).T
        return (grad_low, delta_rows, hidden_zero)

    def feed_prep(unused):
        active_grad = jnp.dot(full_cotangent, down_weight, preferred_element_type=jnp.float32)
        gelu_value, gelu_pullback = jax.vjp(partial(jax.nn.gelu, approximate=False), up_rows)
        return (zeros_heads, zeros_stats, gelu_pullback(active_grad)[0].astype(jnp.bfloat16))

    grad_low, delta_rows, hidden_low = lax.cond(is_attention, attention_prep, feed_prep, 0)

    def block_grads(
        query_rows,
        grad_rows,
        query_lse,
        query_delta,
        query_ids,
        query_place,
        key_rows,
        value_rows,
        key_ids,
        key_place,
    ):
        visible = (query_ids[:, None] == key_ids[None, :]) & (
            key_place[None, :] <= query_place[:, None]
        )

        def compute(unused):
            query_part_heads = query_rows.reshape(tok_rows, local_heads, HEAD_DIM)
            grad_heads = grad_rows.reshape(tok_rows, local_heads, HEAD_DIM)
            key_heads = key_rows.reshape(tok_rows, local_heads, HEAD_DIM)
            value_heads = value_rows.reshape(tok_rows, local_heads, HEAD_DIM)
            scores = (
                jnp.einsum(
                    "qhd,khd->hqk", query_part_heads, key_heads, preferred_element_type=jnp.float32
                )
                * score_scale
            )
            weights = jnp.exp(
                jnp.where(visible[None], scores - query_lse[:, :, None], masked_score)
            )
            value_part = jnp.einsum(
                "hqk,qhd->khd",
                weights.astype(jnp.bfloat16),
                grad_heads,
                preferred_element_type=jnp.float32,
            )
            weight_grad = jnp.einsum(
                "qhd,khd->hqk", grad_heads, value_heads, preferred_element_type=jnp.float32
            )
            score_grad = (weights * (weight_grad - query_delta[:, :, None])).astype(jnp.bfloat16)
            query_part = (
                jnp.einsum(
                    "hqk,khd->qhd", score_grad, key_heads, preferred_element_type=jnp.float32
                )
                * score_scale
            )
            key_part = (
                jnp.einsum(
                    "hqk,qhd->khd", score_grad, query_part_heads, preferred_element_type=jnp.float32
                )
                * score_scale
            )
            return (query_part, key_part, value_part)

        def nothing(unused):
            return (grad_zero, grad_zero, grad_zero)

        return lax.cond(is_attention & jnp.any(visible), compute, nothing, 0)

    def send_grads(key_acc, value_acc):
        return (
            passed_along(key_acc.astype(jnp.bfloat16), "seq", 1).astype(key_acc.dtype),
            passed_along(value_acc.astype(jnp.bfloat16), "seq", 1).astype(value_acc.dtype),
        )

    def key_step(cycle_state, unused):
        key_rows, value_rows, key_ids, key_acc, value_acc, hop_count, query_acc = cycle_state
        source = (seq_index - hop_count) % seq_count
        partial_terms = block_grads(
            query_low,
            grad_low,
            lse_rows,
            delta_rows,
            documents,
            query_index,
            key_rows,
            value_rows,
            key_ids,
            source * tok_rows + local_index,
        )
        key_rows, value_rows, key_ids = shifted((key_rows, value_rows, key_ids), "seq", 1)
        key_acc, value_acc = send_grads(key_acc + partial_terms[1], value_acc + partial_terms[2])
        return (
            (
                key_rows,
                value_rows,
                key_ids,
                key_acc,
                value_acc,
                hop_count + 1,
                query_acc + partial_terms[0],
            ),
            None,
        )

    start_state = (key_low, value_low, documents, grad_zero, grad_zero, jnp.int32(0), grad_zero)
    cycle_state, unused = lax.scan(key_step, start_state, None, length=seq_count - 1)
    key_rows, value_rows, key_ids, key_acc, value_acc, hop_count, query_acc = cycle_state
    source = (seq_index - hop_count) % seq_count
    partial_terms = block_grads(
        query_low,
        grad_low,
        lse_rows,
        delta_rows,
        documents,
        query_index,
        key_rows,
        value_rows,
        key_ids,
        source * tok_rows + local_index,
    )
    key_grad, value_grad = send_grads(key_acc + partial_terms[1], value_acc + partial_terms[2])
    query_grad = query_acc + partial_terms[0]

    def attention_tail(unused):
        query_back = rotate(query_grad, cosine, sine_rows, -1.0)
        key_back = rotate(key_grad, cosine, sine_rows, -1.0)
        packed_grad = (
            jnp.stack([query_back, key_back, value_grad], axis=2)
            .reshape(tok_rows, 3 * attn_width)
            .astype(jnp.bfloat16)
        )
        return (contract_cols(packed_grad, project_weight), packed_grad)

    def feed_tail(unused):
        return (
            contract_cols(hidden_low, up_weight),
            jnp.zeros((tok_rows, 3 * attn_width), jnp.bfloat16),
        )

    norm_grad, packed_grad = lax.cond(is_attention, attention_tail, feed_tail, 0)
    input_part, gain_part, shift_part = norm_pullback(norm_grad)
    input_grad = lax.psum_scatter(
        input_part.astype(jnp.bfloat16), ("branch", "tensor"), scatter_dimension=1, tiled=True
    ).astype(jnp.float32) + cotangent.astype(jnp.float32)

    def attention_rows(unused):
        return jnp.concatenate(
            [
                contract_rows(normed_low, packed_grad),
                contract_rows(full_cotangent, attended_low),
                jnp.zeros(
                    (
                        model_width
                        // (seq_count * lax.axis_size("branch"))
                        * lax.axis_size(("seq", "branch")),
                        2 * hidden_local,
                    ),
                    jnp.float32,
                ),
            ],
            axis=1,
        )

    def feed_rows(unused):
        return jnp.concatenate(
            [
                jnp.zeros(
                    (
                        model_width
                        // (seq_count * lax.axis_size("branch"))
                        * lax.axis_size(("seq", "branch")),
                        4 * attn_width,
                    ),
                    jnp.float32,
                ),
                contract_rows(normed_low, hidden_low),
                contract_rows(full_cotangent, active),
            ],
            axis=1,
        )

    shares = lax.psum_scatter(
        lax.cond(is_attention, attention_rows, feed_rows, 0).astype(jnp.bfloat16),
        ("seq", "branch"),
        scatter_dimension=0,
        tiled=True,
    ).astype(jnp.float32)
    project_grad = shares[:, : 3 * attn_width]
    output_grad = shares[:, 3 * attn_width : 4 * attn_width]
    up_grad = shares[:, 4 * attn_width : 4 * attn_width + hidden_local]
    down_grad = shares[:, 4 * attn_width + hidden_local :]
    offsets_part = lax.dynamic_update_slice(
        jnp.zeros((3 * model_width,), jnp.float32),
        jnp.sum(packed_grad, axis=0, dtype=jnp.float32),
        (tensor_index * (3 * attn_width),),
    )
    hidden_part = lax.dynamic_update_slice(
        jnp.zeros((hidden_local * lax.axis_size("tensor"),), jnp.float32),
        jnp.sum(hidden_low, axis=0, dtype=jnp.float32),
        (tensor_index * hidden_local,),
    )
    pair_zero = jnp.zeros((2, model_width), jnp.float32)
    gain_rows = lax.dynamic_update_slice(
        pair_zero, gain_part[None, :], (branch_index, jnp.int32(0))
    )
    shift_rows = lax.dynamic_update_slice(
        pair_zero, shift_part[None, :], (branch_index, jnp.int32(0))
    )
    column_sums = jnp.where(lead_tensor, jnp.sum(full_cotangent, axis=0, dtype=jnp.float32), 0.0)
    residual_rows = lax.dynamic_update_slice(
        pair_zero, column_sums[None, :], (branch_index, jnp.int32(0))
    )
    offsets_grad, hidden_grad, gain_grad, center_grad, residual_grad = lax.psum(
        (offsets_part, hidden_part, gain_rows, shift_rows, residual_rows),
        ("seq", "branch", "tensor"),
    )
    return (
        layer_out,
        input_grad,
        project_grad,
        output_grad,
        up_grad,
        down_grad,
        offsets_grad,
        hidden_grad,
        gain_grad,
        center_grad,
        residual_grad,
    )


MESH = pl.DeviceIdType.MESH
bf16, f32 = jnp.bfloat16, jnp.float32


def place():
    s, b, t = lax.axis_index("seq"), lax.axis_index("branch"), lax.axis_index("tensor")
    return s, b, t, s // 2, s % 2


def flip(value, bit):
    return value + bit - 2 * bit * value


def flip4(value, k):
    return 2 * flip(value // 2, k // 2) + flip(value % 2, k % 2)


def plane_peer(k):
    s, b, t, x, c = place()
    return (2 * flip(x, k // 2) + c, flip(b, k % 2), t)


def grid_peer(k):
    s, b, t, x, c = place()
    return (s, flip(b, k // 4), flip4(t, k % 4))


def sibling():
    s, b, t, x, c = place()
    return (flip4(s, 1), b, t)


def meet(devices):
    barrier = pltpu.get_barrier_semaphore()
    for device in devices:
        pl.semaphore_signal(barrier, inc=1, device_id=device, device_id_type=MESH)
    pl.semaphore_wait(barrier, len(devices))


def at(index, size):
    return pl.ds(pl.multiple_of(index * size, size), size)


def dot(first, second):
    return jnp.dot(first, second, preferred_element_type=f32)


def turned(values, cosine, sines):
    lane = lax.broadcasted_iota(jnp.int32, values.shape, 1)
    swapped = jnp.where(
        lane < ROT // 2,
        pltpu.roll(values, HEAD_DIM - ROT // 2, 1),
        pltpu.roll(values, ROT // 2, 1),
    )
    return values * cosine + sines * swapped


def layer_kernel(
    tok, cot, places_h, gain_h, shift_h, residual_h, offs_h, hbias_h, wp_h, wo_h, wu_h, wd_h,
    layer_o, grad_o, kept_o, came_o, sums_o,
    wp, wo, wu, wd, tok_v, cot_v, places, gain, shift, residual, offs, hbias, xg, cg, posr, starts, cosr, sinr, rows2, xh, mean_s, inv_s, n0, n1, gd, act, hid,
    hs, heads, att, pack, attf, lse, dk_acc, dv_acc, ob, ro, gb, rg, swap_b, back_b, accg,
    n0t, n1t, ct, other, kept, usum, pair, near, sems, local,
):
    s, b, t, x, c = place()
    m, j = 2 * x + b, 4 * b + t
    slot = 4 * x + 2 * c + b
    scale = HEAD_DIM ** -0.5
    mine = at(m, 128)
    used = {"sem": 0, "local": 0}
    sent, inner_sent = [], []
    inner = (t == 1) | (t == 2)

    def describe(src, dst, device, there=None):
        index = used["sem"]
        used["sem"] += 1
        return pltpu.make_async_remote_copy(
            src_ref=src, dst_ref=dst, send_sem=sems.at[0, index],
            recv_sem=sems.at[1, index if there is None else there],
            device_id=device, device_id_type=MESH)

    def send(src, dst, device):
        copy = describe(src, dst, device)
        copy.start()
        sent.append(copy)
        return copy

    def send_inner(src, dst, device, there=None):
        copy = describe(src, dst, device, there)
        pl.when(inner)(copy.start)
        inner_sent.append(copy)
        return copy

    def move(src, dst):
        index = used["local"]
        used["local"] += 1
        copy = pltpu.make_async_copy(src, dst, local.at[index])
        copy.start()
        return copy

    def arrive(copies):
        for copy in copies:
            copy.wait_recv()

    def direct(view):
        return [send(view(m), view(m), plane_peer(k)) for k in (2, 1)]

    def relay(copies, half):
        out = []
        for i, k in enumerate((2, 1)):
            copies[i].wait_recv()
            part = half(flip4(m, k), i)
            out.append(send(part, part, plane_peer(3 - k)))
        return out

    def loop(count, body):
        def step(i, carry):
            body(i)
            return carry
        lax.fori_loop(0, count, step, 0)

    def block(k):
        return at(4 * flip(b, k // 4) + flip4(t, k % 4), 256)

    def gather(src, dst):
        half, place = src.at[at(b, 128)], dst.at[mine, at(j, 256)]
        over = send(src.at[at(1 - b, 128)], dst.at[at(flip4(m, 1), 128), at(j, 256)], grid_peer(4))
        return {"over": over, "half": half, "place": place, "own": move(half, place), "dst": dst,
                "plane": {}}

    def gather_near(state):
        state["near"] = to_tensor(state["half"], state["place"])

    def to_tensor(src, dst):
        last = used["sem"]
        third = send_inner(src, dst, grid_peer(3))
        near = send(src, dst, grid_peer(1))
        return {2: send(src, dst, grid_peer(2)), 1: near, 3: third, "last": last}

    def on_plane(state, k):
        part = state["dst"].at[mine, block(k)]
        state["plane"][k] = [send(part, part, plane_peer(i)) for i in (2, 1)]

    def gather_over(state):
        state["own"].wait()
        state["over"].wait_recv()
        part = state["dst"].at[mine, block(4)]
        state["far"] = to_tensor(part, part)

    def gather_step(state, k):
        for which, first in (("near", 0), ("far", 4)):
            state[which][k].wait_recv()
            if k == 2:
                part = state["dst"].at[mine, block(first + 2)]
                send_inner(part, part, grid_peer(1), state[which]["last"])

    def both_on_plane(state, k):
        on_plane(state, k)
        on_plane(state, k + 4)

    def plane_relay(state, k, here=False):
        dst, plane = state["dst"], state["plane"]
        plane[k][0].wait_recv()
        part = dst.at[at(flip4(m, 2), 128), block(k)]
        first = send(part, part, plane_peer(1))
        if not here:
            plane[k + 4][1].wait_recv()
        part = dst.at[at(flip4(m, 1), 128), block(k)]
        return [first, send(part, part, plane_peer(2)), plane[k + 4][0]]

    meet([grid_peer(k) for k in (1, 2, 3, 4)] + [plane_peer(2), plane_peer(3)]
         + [(flip4(s, k), b, t) for k in (1, 3)])
    x_state = gather(tok, xg)
    gather_near(x_state)
    g_state = gather(cot, cg)
    small = [move(src, dst) for src, dst in (
        (places_h, places), (gain_h, gain), (shift_h, shift), (residual_h, residual),
        (offs_h, offs), (hbias_h, hbias))]
    wp_load, wu_load = move(wp_h, wp), move(wu_h, wu)
    wo_load, wd_load = move(wo_h, wo), move(wd_h, wd)
    late = [move(tok, tok_v), move(cot, cot_v)]
    for copy in small:
        copy.wait()
    rows2[b] = jnp.zeros((8, 2048), f32)
    rows2[b, 0:1, :] = gain[...]
    rows2[b, 1:2, :] = shift[...]
    rows2[b, 2:3, :] = residual[...]
    posr[s] = jnp.broadcast_to(places[...].astype(f32)[None, :], (8, 256))
    row_copy = send(rows2.at[b], rows2.at[b], grid_peer(4))
    place_copies = [send(posr.at[s], posr.at[s], (flip4(s, k), b, t)) for k in (1, 2, 3)]
    gather_over(x_state)
    both_on_plane(x_state, 0)
    usum[...] = jnp.zeros_like(usum)
    dk_acc[...] = jnp.zeros_like(dk_acc)
    dv_acc[...] = jnp.zeros_like(dv_acc)
    arrive(place_copies)
    for i in range(4):
        row = jnp.broadcast_to(posr[i, 0:1, :], (128, 256))
        index = (256 * i + lax.broadcasted_iota(jnp.int32, (256, 128), 0)).astype(f32)
        starts[pl.ds(256 * i, 256), :] = index - row.T
    line = lax.broadcasted_iota(jnp.int32, (ROT, 256), 0)
    waves = jnp.zeros((ROT, 256), f32)
    for i in range(ROT // 2):
        waves = jnp.where(line % (ROT // 2) == i, rope_base ** (-2.0 * i / ROT), waves)
    for i in (0, 1):
        angle = posr[2 * i + c, 0:1, :] * waves
        part = pl.ds(256 * i, 256)
        sign = jnp.where(line < ROT // 2, -1.0, 1.0)
        rest = jnp.zeros((HEAD_DIM - ROT, 256), f32)
        cosr[part, :] = jnp.concatenate([jnp.cos(angle), rest + 1.0], axis=0).T
        sinr[part, :] = jnp.concatenate([jnp.sin(angle) * sign, rest], axis=0).T
    for k in (1, 2, 3):
        gather_step(x_state, k)
        both_on_plane(x_state, k)
        if k == 2:
            gather_near(g_state)
            gather_over(g_state)
    arrive([row_copy])

    def norm(which, whole):
        def rows(i):
            part = pl.ds(pl.multiple_of(which * 128 + 32 * i, 32), 32)
            v = xg[part, :].astype(f32)
            mean = jnp.mean(v, axis=-1, keepdims=True)
            centered = v - mean
            inverse = lax.rsqrt(jnp.mean(centered * centered, axis=-1, keepdims=True) + norm_eps)
            hat = centered * inverse
            mean_s[part, :] = jnp.broadcast_to(mean, (32, 128))
            inv_s[part, :] = jnp.broadcast_to(inverse, (32, 128))
            n1_part = pl.ds(pl.multiple_of((which % 2) * 128 + 32 * i, 32), 32)
            n1[n1_part, :] = (hat * rows2[1, 0:1, :] + rows2[1, 1:2, :]).astype(bf16)
            if whole:
                xh[at(i, 32), :] = hat
                n0[at(i, 32), :] = (hat * rows2[0, 0:1, :] + rows2[0, 1:2, :]).astype(bf16)

        loop(4, rows)

    norm(m, True)
    x_relays = []
    for k in (0, 1, 2):
        x_relays += plane_relay(x_state, k)
    wp_load.wait()
    turn = pl.ds(pl.multiple_of(256 * x + 128 * b, 128), 128)

    def project(h):
        p = dot(n0[...], wp[:, at(h, 384)]) + offs[at(h, 384)][None, :]
        hs[h, :, 0:128] = turned(p[:, 0:128], cosr[turn, :], sinr[turn, :]).astype(bf16)
        hs[h, :, 128:256] = turned(p[:, 128:256], cosr[turn, :], sinr[turn, :]).astype(bf16)
        hs[h, :, 256:384] = p[:, 256:384].astype(bf16)

    loop(4, project)

    def to_heads(cols):
        copies = [send(hs.at[flip4(m, k), :, cols], heads.at[at(slot, 128), cols], plane_peer(k))
                  for k in (3, 2, 1)]
        return copies, move(hs.at[m, :, cols], heads.at[at(slot, 128), cols])

    def to_sibling(copies, kept, cols):
        arrive(copies)
        kept.wait()
        parts = [heads.at[pl.ds(512 * i + 256 * c, 256), cols] for i in (0, 1)]
        return [send(part, part, sibling()) for part in parts]

    qkv_cols, up_cols = pl.ds(0, 384), pl.ds(384, 128)
    qkv_copies, qkv_own = to_heads(qkv_cols)
    x_relays += plane_relay(x_state, 3)
    gather_step(g_state, 1)
    arrive([x_state["plane"][k][1] for k in range(4)])
    norm(flip4(m, 1), False)
    gather_step(g_state, 2)
    wu_load.wait()

    def feed(pair_index, first, count):
        rows = at(pair_index, 256)

        def tile(n):
            cols = at(first + n, 512)
            u = dot(n1[...], wu[:, cols]) + hbias[cols][None, :]
            phi = 0.5 + 0.5 * lax.erf(u * 0.7071067811865476)
            act[rows, cols] = (u * phi).astype(bf16)
            gd[rows, cols] = (phi + u * (0.3989422804014327 * jnp.exp(-0.5 * u * u))).astype(gd.dtype)

        loop(count, tile)

    feed(x, 0, 2)
    qkv_pair = to_sibling(qkv_copies, qkv_own, qkv_cols)
    att_view = lambda i: att.at[:, at(i, 128)]
    att_half = lambda i, h: att.at[pl.ds(256 * h, 256), at(i, 128)]
    pack_view = lambda i: pack.at[:, at(i, 384)]
    pack_half = lambda i, h: pack.at[pl.ds(256 * h, 256), at(i, 384)]

    def score_rows(i):
        width = 256 * (i + 1)
        part = pl.ds(256 * i, 256)
        scores = contract_cols(heads[part, 0:128], heads[0:width, 128:256]) * scale
        query = (256 * i + lax.broadcasted_iota(jnp.int32, (256, 1), 0)).astype(f32)
        key = lax.broadcasted_iota(jnp.int32, (256, width), 1).astype(f32)
        visible = (key <= query) & (key >= starts[part, 0:1])
        return part, width, jnp.where(visible, scores, masked_score), visible

    gather_step(g_state, 3)
    wo_load.wait()

    head_low = dot(cg[mine, :], wo[...]).astype(bf16)
    for h in range(4):
        hs[h, :, 384:512] = head_low[:, 128 * h : 128 * (h + 1)]
    up_copies, up_own = to_heads(up_cols)
    arrive(qkv_pair)
    for i in range(4):
        part, width, masked, visible = score_rows(i)
        top = jnp.max(masked, axis=-1, keepdims=True)
        weights = jnp.where(visible, jnp.exp(masked - top), 0.0)
        total = jnp.sum(weights, axis=-1, keepdims=True)
        attf[part, :] = dot(weights.astype(bf16), heads[0:width, 256:384]) / total
        lse[part, :] = jnp.broadcast_to(top + jnp.log(total), (256, 128))

    for i in (0, 1):
        att[pl.ds(256 * i, 256), at(m, 128)] = attf[pl.ds(512 * i + 256 * c, 256), :].astype(bf16)
    att_copies = direct(att_view)
    both_on_plane(g_state, 0)
    both_on_plane(g_state, 1)
    up_pair = to_sibling(up_copies, up_own, up_cols)
    arrive(up_pair)

    for i in range(4):
        part, width, masked, visible = score_rows(i)
        probs = jnp.where(visible, jnp.exp(masked - lse[part, 0:1]), 0.0)
        up = heads[part, 384:512]
        delta = jnp.sum(up.astype(f32) * attf[part, :], axis=-1, keepdims=True)
        grads = (probs * (contract_cols(up, heads[0:width, 256:384]) - delta)).astype(bf16)
        dv_acc[0:width, :] += contract_rows(probs.astype(bf16), up)
        dk_acc[0:width, :] += contract_rows(grads, heads[part, 0:128])

        @pl.when(i % 2 == c)
        def _():
            here = pl.ds(256 * (i // 2), 256)
            back = dot(grads, heads[0:width, 128:256]) * scale
            pack[here, at(3 * m, 128)] = turned(back, cosr[here, :], -sinr[here, :]).astype(bf16)

    for i in (0, 1):
        part, here = pl.ds(512 * i + 256 * c, 256), pl.ds(256 * i, 256)
        key_back = turned(dk_acc[part, :] * scale, cosr[here, :], -sinr[here, :])
        pack[here, at(3 * m + 1, 128)] = key_back.astype(bf16)
        pack[here, at(3 * m + 2, 128)] = dv_acc[part, :].astype(bf16)
    att_relays = relay(att_copies, att_half)
    pack_copies = direct(pack_view)
    both_on_plane(g_state, 2)
    both_on_plane(g_state, 3)
    feed(x, 2, 2)
    arrive(x_relays)
    norm(flip4(m, 2), False)
    norm(flip4(m, 3), False)
    wd_load.wait()

    def feed_out(n):
        accg[:, at(n, 1024)] = contract_cols(act[mine, :], wd[at(n, 1024), :])

    loop(2, feed_out)
    arrive(att_relays)

    def finish_out(n):
        total = accg[:, at(n, 1024)] + contract_cols(att[mine, :], wo[at(n, 1024), :])
        for i in range(4):
            ob[i, n] = total[:, 256 * i : 256 * (i + 1)].astype(bf16)

    loop(2, finish_out)

    def scatter(src, dst):
        copies = [send(src.at[flip4(t, k)], dst.at[t], grid_peer(k)) for k in (3, 2, 1)]
        return copies, move(src.at[t], dst.at[t])

    def across(copies, kept, src, which):
        arrive(copies)
        kept.wait()
        sums = [sum(src[i, half].astype(f32) for i in range(4)) for half in (0, 1)]
        keep = jnp.where(b == 0, sums[0], sums[1])
        swap_b[which] = jnp.where(b == 0, sums[1], sums[0]).astype(bf16)
        return keep, send(swap_b.at[which], back_b.at[which], grid_peer(4))

    out_copies, out_own = scatter(ob, ro)

    def hidden(rows):
        def tile(n):
            cols = at(n, 512)
            hid[rows, cols] = (dot(cg[rows, :], wd[:, cols]) * gd[rows, cols].astype(f32)).astype(bf16)

        loop(4, tile)

    hidden(mine)

    def norm_grad(n, values, weight, which):
        cols = at(n, 1024)
        ng = contract_cols(values, weight[cols, :])
        usum[which : which + 1, cols] = jnp.sum(ng * xh[:, cols], axis=0, keepdims=True)
        usum[which + 2 : which + 3, cols] = jnp.sum(ng, axis=0, keepdims=True)
        return ng * rows2[which, 0:1, cols]

    def feed_grad(n):
        cols = at(n, 1024)
        accg[:, cols] = norm_grad(n, hid[mine, :], wu, 1)
        usum[6:7, cols] = jnp.sum(hid[mine, cols].astype(f32), axis=0, keepdims=True)
        usum[4:5, cols] = jnp.sum(cg[mine, cols].astype(f32), axis=0, keepdims=True)

    loop(2, feed_grad)
    pack_relays = relay(pack_copies, pack_half)
    feed(1 - x, 0, 4)
    arrive([g_state["plane"][k][1] for k in range(8)])
    g_relays = []
    for k in range(4):
        g_relays += plane_relay(g_state, k, True)
    def transpose_tokens(i):
        part = at(i, 128)
        for half in (0, 1):
            cols = pl.ds(256 * half, 256)
            features = at(4 * x + 2 * flip(c, half) + b, 256)
            hat = (xg[part, features].astype(f32) - mean_s[part, 0:1]) * inv_s[part, 0:1]
            for which, dst in ((0, n0t), (1, n1t)):
                low = hat * rows2[which, 0:1, features] + rows2[which, 1:2, features]
                dst[cols, part] = low.T.astype(bf16)

    loop(4, transpose_tokens)
    hidden(at(flip4(m, 1), 128))
    arrive(pack_relays)

    def attention_grad(n):
        accg[:, at(n, 1024)] += norm_grad(n, pack[mine, :], wp, 0)

    loop(2, attention_grad)
    usum[5:6, 0:1536] = jnp.sum(pack[mine, :].astype(f32), axis=0, keepdims=True)
    pair_copy = send(usum, pair, sibling())
    zero = jnp.zeros((128, 1), f32)

    def means(n, carry):
        g = accg[:, at(n, 256)]
        return (carry[0] + jnp.sum(g, axis=-1, keepdims=True),
                carry[1] + jnp.sum(g * xh[:, at(n, 256)], axis=-1, keepdims=True))

    mean, slope = lax.fori_loop(0, 8, means, (zero, zero))
    mean, slope = mean * (1.0 / 2048), slope * (1.0 / 2048)

    def finish_grad(n):
        gb[n % 4, n // 4] = (inv_s[mine, 0:1] * (accg[:, at(n, 256)] - mean - xh[:, at(n, 256)] * slope)).astype(bf16)

    loop(8, finish_grad)
    grad_copies, grad_own = scatter(gb, rg)
    writes, swaps = [], []

    def matrix(lhs, rhs, count, base):
        first, here = used["sem"], used["local"]
        used["sem"] += count
        used["local"] += count

        def swap(i):
            return pltpu.make_async_remote_copy(
                src_ref=other.at[base + i], dst_ref=came_o.at[base + i],
                send_sem=sems.at[0, first + i], recv_sem=sems.at[1, first + i],
                device_id=sibling(), device_id_type=MESH)

        def keep(i):
            return pltpu.make_async_copy(kept.at[base + i], kept_o.at[base + i], local.at[here + i])

        def produce(i):
            both = dot(lhs[...], rhs[:, at(i, 512)]).astype(bf16)
            other[base + i] = both[256:]
            swap(i).start()
            kept[base + i] = both[:256]
            keep(i).start()

        loop(count, produce)
        for i in range(count):
            writes.append(keep(i))
            swaps.append(swap(i))

    matrix(n0t, pack, 3, 9)
    arrive(g_relays)
    hidden(at(1 - x, 256))

    def transpose_grads(i):
        part = at(i, 128)
        for half in (0, 1):
            features = at(4 * x + 2 * flip(c, half) + b, 256)
            ct[pl.ds(256 * half, 256), part] = cg[part, features].astype(f32).T.astype(bf16)

    loop(4, transpose_grads)
    arrive([pair_copy])
    pair[...] += usum[...]
    near_copies = [send(pair, near.at[k - 1], plane_peer(k)) for k in (1, 2, 3)]
    matrix(ct, act, 4, 0)
    arrive(near_copies)
    sums_o[t] = pair[...] + near[0] + near[1] + near[2]
    sum_copies = [send(sums_o.at[t], sums_o.at[t], grid_peer(k)) for k in (1, 2, 3)]
    out_keep, out_swap = across(out_copies, out_own, ro, 0)
    matrix(n1t, hid, 4, 4)
    grad_keep, grad_swap = across(grad_copies, grad_own, rg, 1)
    matrix(ct, att, 1, 8)
    for copy in late:
        copy.wait()
    columns = at(j, 256)
    bias = rows2[0, 2:3, columns] + rows2[1, 2:3, columns]
    here, there = at(b, 128), at(1 - b, 128)
    layer_o[here, :] = (bias + tok_v[here, :].astype(f32) + out_keep).astype(bf16)
    arrive([out_swap])
    layer_o[there, :] = (bias + tok_v[there, :].astype(f32) + back_b[0].astype(f32)).astype(bf16)
    grad_o[here, :] = cot_v[here, :].astype(f32) + grad_keep
    arrive(sum_copies + [grad_swap])
    grad_o[there, :] = cot_v[there, :].astype(f32) + back_b[1].astype(f32)
    for copy in writes + swaps:
        copy.wait()
    for copy in sent:
        copy.wait_send()
    for copy in inner_sent:
        pl.when(inner)(copy.wait_send)
    assert used["sem"] <= 150 and used["local"] <= 40, used


def emit_kernel(layer, grad, kept, came, sums, layer_o, grad_o, project_o, output_o,
                up_o, down_o, offs_o, hidden_o, gain_o, center_o, residual_o):
    for out, base, count in ((down_o, 0, 4), (up_o, 4, 4), (output_o, 8, 1), (project_o, 9, 3)):
        for i in range(count):
            out[:, pl.ds(512 * i, 512)] = kept[base + i].astype(f32) + came[base + i].astype(f32)

    @pl.when(pl.program_id(0) == 0)
    def _():
        layer_o[...] = layer[...]
        grad_o[...] = grad[...]
        gain_o[...] = sums[0, 0:2] + sums[1, 0:2] + sums[2, 0:2] + sums[3, 0:2]
        center_o[...] = sums[0, 2:4] + sums[1, 2:4] + sums[2, 2:4] + sums[3, 2:4]
        residual_o[...] = jnp.broadcast_to(sums[0, 4:5], (2, 2048))
        for i in range(4):
            offs_o[pl.ds(1536 * i, 1536)] = sums[i, 5, 0:1536]
            hidden_o[pl.ds(2048 * i, 2048)] = sums[i, 6]


def fast_device(tokens, cotangent, documents, positions, project_weight, offsets, output_weight,
                up_weight, hidden_bias, down_weight, norm_gain, norm_bias, residual_bias):
    vmem, anywhere = pl.BlockSpec(memory_space=pltpu.VMEM), pl.BlockSpec(memory_space=pl.ANY)
    shape = jax.ShapeDtypeStruct
    low = lambda *size: pltpu.VMEM(size, bf16)
    full = lambda *size: pltpu.VMEM(size, f32)
    widths = (1536, 512, 2048, 2048)
    results = pl.pallas_call(
        layer_kernel,
        out_shape=[shape((256, 256), bf16), shape((256, 256), f32)]
        + [shape((12, 256, 512), bf16)] * 2 + [shape((4, 8, 2048), f32)],
        in_specs=[anywhere] * 12,
        out_specs=[vmem] * 2 + [anywhere] * 2 + [vmem],
        scratch_shapes=[
            low(2048, 1536), low(2048, 512), low(2048, 2048), low(2048, 2048),
            low(256, 256), low(256, 256), pltpu.VMEM((256,), jnp.int32), full(1, 2048), full(1, 2048),
            full(1, 2048), full(1536), full(2048),
            low(512, 2048), low(512, 2048), full(4, 8, 256), full(1024, 128), full(512, 128),
            full(512, 128), full(2, 8, 2048), full(128, 2048), full(512, 128), full(512, 128),
            low(128, 2048), low(256, 2048), GD(512, 2048), low(512, 2048), low(512, 2048),
            low(4, 128, 512), low(1024, 512), low(512, 512), low(512, 1536), full(1024, 128),
            full(1024, 128), full(1024, 128), full(1024, 128), low(4, 2, 128, 256),
            low(4, 2, 128, 256), low(4, 2, 128, 256), low(4, 2, 128, 256), low(2, 128, 256),
            low(2, 128, 256), full(128, 2048), low(512, 512), low(512, 512),
            low(512, 512), low(12, 256, 512),
            low(12, 256, 512), full(8, 2048), full(8, 2048), full(3, 8, 2048),
            pltpu.SemaphoreType.DMA((2, 150)), pltpu.SemaphoreType.DMA((40,))],
        compiler_params=pltpu.CompilerParams(
            collective_id=0, has_side_effects=True, vmem_limit_bytes=LIMIT),
    )(tokens, cotangent, positions, norm_gain, norm_bias, residual_bias,
      offsets, hidden_bias, project_weight, output_weight, up_weight, down_weight)
    steps = 2
    whole = lambda *size: pl.BlockSpec(size, lambda i: (0,) * len(size))
    band = lambda width: pl.BlockSpec((256 // steps, width), lambda i: (i, 0))
    layer_out, input_grad, *rest = pl.pallas_call(
        emit_kernel,
        grid=(steps,),
        out_shape=[shape((256, 256), bf16), shape((256, 256), f32)]
        + [shape((256, width), f32) for width in widths]
        + [shape((6144,), f32), shape((8192,), f32)] + [shape((2, 2048), f32)] * 3,
        in_specs=[whole(256, 256)] * 2
        + [pl.BlockSpec((12, 256 // steps, 512), lambda i: (0, i, 0))] * 2 + [whole(4, 8, 2048)],
        out_specs=[whole(256, 256)] * 2 + [band(width) for width in widths]
        + [whole(6144), whole(8192)] + [whole(2, 2048)] * 3,
        compiler_params=pltpu.CompilerParams(vmem_limit_bytes=LIMIT),
    )(*results)
    return (layer_out, input_grad, *rest)


LIMIT = 63 << 20
GD = lambda *size: pltpu.VMEM(size, bf16)


def solution(mesh):
    fits = (mesh.shape["seq"], mesh.shape["branch"], mesh.shape["tensor"]) == (4, 2, 4)
    return jax.shard_map(
        fast_device if fits else on_device,
        mesh=mesh,
        in_specs=(
            P("seq", ("branch", "tensor")),
            P("seq", ("branch", "tensor")),
            P("seq"),
            P("seq"),
            P(None, "tensor"),
            P("tensor"),
            P(None, "tensor"),
            P(None, "tensor"),
            P("tensor"),
            P(None, "tensor"),
            P("branch", None),
            P("branch", None),
            P("branch", None),
        ),
        out_specs=(
            P("seq", ("branch", "tensor")),
            P("seq", ("branch", "tensor")),
            P(("seq", "branch"), "tensor"),
            P(("seq", "branch"), "tensor"),
            P(("seq", "branch"), "tensor"),
            P(("seq", "branch"), "tensor"),
            P(),
            P(),
            P(),
            P(),
            P(),
        ),
        check_vma=False,
    )
```
